32 devices in a mesh: dp: 16 (over z, y, x), blk: 2 (over core).
Axes of the slice: x: 2, y: 2, z: 4, core: 2. Of those that a mesh axis runs over, the one named last changes fastest.
Arguments:
- tokens: bfloat16 [16, 512, 1024], P('dp', 'blk'), may hold values from -6 to 6
- doc_lengths: int32 [16, 8], P('dp'), may hold values from 0 to 512, as said below
- cotangent: bfloat16 [16, 512, 1024], P('dp', 'blk'), may hold values from -6 to 6
- w_qkv: bfloat16 [1024, 3072], P('dp'), may hold values from -0.1875 to 0.1875
- qv_bias: bfloat16 [2048], P('dp'), may hold values from -1.25 to 1.25
- w_out: bfloat16 [1024, 1024], P('dp'), may hold values from -0.5 to 0.5
- out_bias: bfloat16 [1024], P('dp'), may hold values from -1.25 to 1.25
- w_up: bfloat16 [1024, 4096], P('dp'), may hold values from -0.1875 to 0.1875
- up_bias: bfloat16 [4096], P('dp'), may hold values from -1.25 to 1.25
- w_down: bfloat16 [4096, 1024], P('dp'), may hold values from -0.09375 to 0.09375
- down_bias: bfloat16 [1024], P('dp'), may hold values from -1.25 to 1.25
- norm_gain: bfloat16 [4, 1024], P(None, 'dp'), may hold values from 0.5 to 1.5
- norm_bias: bfloat16 [4, 1024], P(None, 'dp'), may hold values from -1.25 to 1.25
Outputs:
- layer_out: bfloat16 [16, 512, 1024], P('dp', 'blk')
- grad_tokens: float32 [16, 512, 1024], P('dp', 'blk')
- grad_w_qkv: float32 [1024, 3072], P('dp')
- grad_qv_bias: float32 [2048], P('dp')
- grad_w_out: float32 [1024, 1024], P('dp')
- grad_out_bias: float32 [1024], P('dp')
- grad_w_up: float32 [1024, 4096], P('dp')
- grad_up_bias: float32 [4096], P('dp')
- grad_w_down: float32 [4096, 1024], P('dp')
- grad_down_bias: float32 [1024], P('dp')
- grad_norm_gain: float32 [4, 1024], P(None, 'dp')
- grad_norm_bias: float32 [4, 1024], P(None, 'dp')
The draws below stay inside these ranges and needn't reach their ends.
Inputs may be any that keep to these rules, and one draw needn't show every extreme that they name: `doc_lengths`: in each row the lengths sum to at most 512; slots past the sum are padding, and unused document slots hold 0. Every row holds one document that starts within its first 256 slots and ends within its last 256.
All inputs are finite; a program needn't handle non-finite values.
Results may differ from the reference program's by a relative error of at most 0.015.
Values may be sent and summed in bfloat16 or wider, within the bound.
A program may use at most 192 MiB of HBM per device.

```python
import math
import jax
import jax.numpy as jnp
from jax import lax

D = 1024
HEADS = 16
HEAD_DIM = 64
FF = 4096
SEQ = 512
DOCS = 8
ALPHA = 32
ROWS = 16
SPAN = 256


def draw_doc_lengths(key, part):
    key = jax.random.fold_in(key, 11)
    row_keys = jax.random.split(jax.random.fold_in(key, 1), ROWS)
    full_row = jax.random.randint(jax.random.fold_in(key, 2), (), 0, ROWS)

    def one_row(row_key, row_index):
        split_keys = jax.random.split(row_key, 6)
        slot_index = jnp.arange(DOCS, dtype=jnp.int32)
        count_front = jax.random.randint(split_keys[0], (), 0, 3)
        front_len = jax.random.randint(split_keys[1], (DOCS,), 1, SPAN // 4 + 1)
        front_len = jnp.where(slot_index < count_front, front_len, 0)
        prefix = jnp.sum(front_len)
        lowest = SEQ - SPAN + 1 - prefix
        long_range = SEQ - prefix - lowest + 1
        long_len = lowest + jax.random.randint(split_keys[2], (), 0, long_range)
        remainder = SEQ - prefix - long_len
        count_back = jax.random.randint(split_keys[3], (), 1, 4)
        weights = jax.random.randint(split_keys[4], (DOCS,), 1, 9) ** 3
        back_slot = (slot_index > count_front) & (slot_index <= count_front + count_back)
        weights = jnp.where(back_slot, weights, 0)
        pad_weight = jax.random.randint(split_keys[5], (), 1, 9) ** 3
        back_len = remainder * weights // (jnp.sum(weights) + pad_weight)
        lengths = jnp.where(slot_index == count_front, long_len, front_len + back_len)
        forced = jnp.where(slot_index == 0, SEQ, 0)
        return jnp.where(row_index == full_row, forced, lengths).astype(jnp.int32)
    return jax.vmap(one_row)(row_keys, jnp.arange(ROWS, dtype=jnp.int32))


def block_levels(stream_key, dims, cuts, low, largest):
    loudness, own = 1.0, jax.random.fold_in(stream_key, 6)
    for dim, shards_of in cuts:
        heights = jnp.exp(jax.random.uniform(jax.random.fold_in(own, dim), (shards_of,), jnp.float32, low / len(cuts), largest / len(cuts)))
        loudness = loudness * jnp.repeat(heights, dims[dim] // shards_of).reshape([-1 if axis == dim else 1 for axis in range(len(dims))])
    return loudness


def normal_values(own_key, shape, scale, limit, shards=(), kind=jnp.bfloat16):
    loudness = block_levels(own_key, shape, shards, -0.22, 0.18) if shards else 1.0
    array = jax.random.normal(own_key, shape, jnp.float32) * scale * loudness
    return jnp.minimum(jnp.maximum(array, -limit), limit).astype(kind)


def setup_inputs(seed: int = 0) -> dict:
    streams_of = jax.random.split(jax.random.key(seed), 14)
    tokens = normal_values(streams_of[0], (ROWS, SEQ, D), 1.0, 6.0, ((0, 16), (1, 2)))
    doc_lengths = draw_doc_lengths(jax.random.fold_in(streams_of[13], 71), 0)
    cotangent = normal_values(streams_of[2], (ROWS, SEQ, D), 1.0, 6.0, ((0, 16), (1, 2)))
    w_qkv = normal_values(streams_of[3], (D, 3 * D), D ** -0.5, 0.1875, ((0, 16),))
    qv_bias = normal_values(streams_of[4], (2 * D,), 0.2, 1.25, ((0, 16),))
    w_out = normal_values(streams_of[5], (D, D), (D // 8) ** -0.5, 0.5, ((0, 16),))
    out_bias = normal_values(streams_of[6], (D,), 0.2, 1.25, ((0, 16),))
    w_up = normal_values(streams_of[7], (D, FF), D ** -0.5, 0.1875, ((0, 16),))
    up_bias = normal_values(streams_of[8], (FF,), 0.2, 1.25, ((0, 16),))
    w_down = normal_values(streams_of[9], (FF, D), FF ** -0.5, 0.09375, ((0, 16),))
    down_bias = normal_values(streams_of[10], (D,), 0.2, 1.25, ((0, 16),))
    norm_gain = jnp.clip(1.0 + 0.1 * jax.random.normal(streams_of[11], (4, D), jnp.float32), 0.5, 1.5).astype(jnp.bfloat16)
    norm_bias = normal_values(streams_of[12], (4, D), 0.2, 1.25, ((1, 16),))
    return dict(tokens=tokens, doc_lengths=doc_lengths, cotangent=cotangent, w_qkv=w_qkv, qv_bias=qv_bias, w_out=w_out, out_bias=out_bias, w_up=w_up, up_bias=up_bias, w_down=w_down, down_bias=down_bias, norm_gain=norm_gain, norm_bias=norm_bias)


EPSILON = 1e-05
FILLER = -1000000000.0

@jax.custom_vjp
def low(v):
    return lax.optimization_barrier(v.astype(jnp.bfloat16)).astype(jnp.float32)

@jax.custom_vjp
def low_back(v):
    return v

def low_keep(v):
    return (low(v), None)

def low_pass(kept, grad):
    return (grad,)

def back_keep(v):
    return (v, None)

def back_low(kept, grad):
    return (low(grad),)
low.defvjp(low_keep, low_pass)
low_back.defvjp(back_keep, back_low)

def normalize(values, gain_row, shift_row):
    center = values - lax.optimization_barrier(jnp.mean(values, axis=-1, keepdims=True))
    inverse = lax.rsqrt(lax.optimization_barrier(jnp.mean(center * center, axis=-1, keepdims=True)) + EPSILON)
    return center * inverse * gain_row + shift_row

def valid_of(lengths):
    position = jnp.arange(SEQ, dtype=jnp.int32)
    filled = jnp.sum(lengths).astype(jnp.int32)
    return (position < filled).astype(jnp.float32)

def layer_row(params, inputs, lengths):
    qkv_weight, qv_shift, out_weight, out_shift, up_weight, up_shift, down_weight, down_shift, gain_rows, shift_rows = params
    highest = lax.Precision.HIGHEST
    query_scale = 1.0 / (ALPHA * math.sqrt(HEAD_DIM))
    doc_ends = jnp.cumsum(lengths).astype(jnp.int32)
    position = jnp.arange(SEQ, dtype=jnp.int32)
    segment = lax.optimization_barrier(jnp.sum((position[:, None] >= doc_ends[None, :]).astype(jnp.int32), axis=1))
    allowed = (segment[:, None] == segment[None, :]) & (position[None, :] <= position[:, None])
    attn_in = low(normalize(inputs, gain_rows[0], shift_rows[0]))
    projected = jnp.dot(attn_in, qkv_weight, precision=highest)
    queries = low_back(low((projected[:, :D] + qv_shift[:D]) * query_scale))
    key_rows = low_back(low(projected[:, D:2 * D]))
    value_rows = low_back(low(projected[:, 2 * D:] + qv_shift[D:]))
    query_heads = queries.reshape(SEQ, HEADS, HEAD_DIM)
    key_heads = key_rows.reshape(SEQ, HEADS, HEAD_DIM)
    value_heads = value_rows.reshape(SEQ, HEADS, HEAD_DIM)
    raw_scores = jnp.einsum('qhd,khd->hqk', query_heads, key_heads, precision=highest)
    masked = jnp.where(allowed[None], raw_scores, FILLER)
    row_top = lax.optimization_barrier(jnp.max(masked, axis=2, keepdims=True))
    weights = jnp.exp(ALPHA * (masked - row_top))
    probabilities = weights / lax.optimization_barrier(jnp.sum(weights, axis=2, keepdims=True))
    attended = jnp.einsum('hqk,khd->qhd', probabilities, value_heads, precision=highest).reshape(SEQ, D)
    attended = low_back(low(attended))
    branch = low_back(jnp.dot(attended, out_weight, precision=highest) + out_shift)
    middle = inputs + normalize(branch, gain_rows[1], shift_rows[1])
    ffn_in = low(normalize(middle, gain_rows[2], shift_rows[2]))
    pre_act = low_back(jnp.dot(ffn_in, up_weight, precision=highest) + up_shift)
    activated = low(jax.nn.gelu(pre_act, approximate=True))
    ffn_out = low_back(jnp.dot(activated, down_weight, precision=highest) + down_shift)
    return middle + normalize(ffn_out, gain_rows[3], shift_rows[3])

def reference(tokens, doc_lengths, cotangent, w_qkv, qv_bias, w_out, out_bias, w_up, up_bias, w_down, down_bias, norm_gain, norm_bias):
    params = (w_qkv.astype(jnp.float32), qv_bias.astype(jnp.float32), w_out.astype(jnp.float32), out_bias.astype(jnp.float32), w_up.astype(jnp.float32), up_bias.astype(jnp.float32), w_down.astype(jnp.float32), down_bias.astype(jnp.float32), norm_gain.astype(jnp.float32), norm_bias.astype(jnp.float32))
    inputs = tokens.astype(jnp.float32)

    def forward(layer_inputs, layer_params):

        def one_row(row_pair):
            return layer_row(layer_params, row_pair[0], row_pair[1])
        return lax.map(jax.checkpoint(one_row), (layer_inputs, doc_lengths))
    result, pullback = jax.vjp(forward, inputs, params)
    valid_rows = jax.vmap(valid_of)(doc_lengths)
    grad_inputs, grad_params = pullback(cotangent.astype(jnp.float32) * valid_rows[:, :, None])
    return (result.astype(jnp.bfloat16), grad_inputs, grad_params[0], grad_params[1], grad_params[2], grad_params[3], grad_params[4], grad_params[5], grad_params[6], grad_params[7], grad_params[8], grad_params[9])
```

```python
import functools
import math

import jax
import jax.numpy as jnp
from jax import lax
from jax.experimental import pallas as pl
from jax.experimental.pallas import tpu as pltpu
from jax.sharding import PartitionSpec as P

HEADS = 16
ALPHA = 32


EPSILON = 1e-05
FILLER = -1000000000.0


def normalize(values):
    center = values - jnp.mean(values, axis=-1, keepdims=True)
    inverse = lax.rsqrt(jnp.mean(center * center, axis=-1, keepdims=True) + EPSILON)
    return (center * inverse, inverse)


def norm_back(normed, inverse, gain_row, upstream):
    scaled = upstream * gain_row
    return inverse * (
        scaled
        - jnp.mean(scaled, axis=-1, keepdims=True)
        - normed * jnp.mean(scaled * normed, axis=-1, keepdims=True)
    )


def segment_of(position, doc_ends):
    return jnp.sum((position[:, None] >= doc_ends[None, :]).astype(jnp.int32), axis=1)


def gelu_tanh(values):
    return jax.nn.gelu(values, approximate=True)


def shards(
    tokens,
    doc_lengths,
    cotangent,
    w_qkv,
    qv_bias,
    w_out,
    out_bias,
    w_up,
    up_bias,
    w_down,
    down_bias,
    norm_gain,
    norm_bias,
):
    inputs = tokens[0].astype(jnp.float32)
    length = inputs.shape[0]
    model_width = inputs.shape[1]
    block_count = lax.axis_size("blk")
    seq_len = length * block_count
    offset = lax.axis_index("blk") * length
    doc_ends = jnp.cumsum(doc_lengths[0])
    filled = doc_ends[-1]
    query_pos = offset + jnp.arange(length, dtype=jnp.int32)
    query_seg = segment_of(query_pos, doc_ends)
    valid_rows = (query_pos < filled).astype(jnp.float32)
    key_seg = segment_of(jnp.arange(seq_len, dtype=jnp.int32), doc_ends)
    last_query = offset + length - 1

    def block_meets(first_row, piece_rows):
        first_at = jnp.asarray(first_row, jnp.int32)
        first_seg = lax.dynamic_index_in_dim(key_seg, first_at, keepdims=False)
        last_seg = lax.dynamic_index_in_dim(key_seg, first_at + piece_rows - 1, keepdims=False)
        return (first_at <= last_query) & (first_seg <= query_seg[-1]) & (last_seg >= query_seg[0])

    gathered = (
        lax.all_gather(w_qkv, "dp", axis=0, tiled=True),
        lax.all_gather(qv_bias, "dp", axis=0, tiled=True),
        lax.all_gather(w_out, "dp", axis=0, tiled=True),
        lax.all_gather(out_bias, "dp", axis=0, tiled=True),
        lax.all_gather(w_up, "dp", axis=0, tiled=True),
        lax.all_gather(up_bias, "dp", axis=0, tiled=True),
        lax.all_gather(w_down, "dp", axis=0, tiled=True),
        lax.all_gather(down_bias, "dp", axis=0, tiled=True),
        lax.all_gather(norm_gain, "dp", axis=1, tiled=True),
        lax.all_gather(norm_bias, "dp", axis=1, tiled=True),
    )
    (
        qkv_weight,
        qv_shift,
        out_weight,
        out_shift,
        up_weight,
        up_shift,
        down_weight,
        down_shift,
        gain_all,
        shift_all,
    ) = gathered
    gain_rows = gain_all.astype(jnp.float32)
    shift_rows = shift_all.astype(jnp.float32)
    query_scale = 1.0 / (ALPHA * math.sqrt(model_width // HEADS))
    first_hat, first_inv = normalize(inputs)
    attn_in = (first_hat * gain_rows[0] + shift_rows[0]).astype(jnp.bfloat16)
    projected = jnp.dot(attn_in, qkv_weight, preferred_element_type=jnp.float32)
    qv_float = qv_shift.astype(jnp.float32)
    queries = ((projected[:, :model_width] + qv_float[:model_width]) * query_scale).astype(
        jnp.bfloat16
    )
    keys_own = projected[:, model_width : 2 * model_width].astype(jnp.bfloat16)
    values_own = (projected[:, 2 * model_width :] + qv_float[model_width:]).astype(jnp.bfloat16)
    query_heads = queries.reshape(length, HEADS, -1)

    def scores_of(key_piece, first_row):
        piece_rows = key_piece.shape[0]
        piece_pos = first_row + jnp.arange(piece_rows, dtype=jnp.int32)
        piece_seg = lax.dynamic_slice_in_dim(key_seg, jnp.asarray(first_row, jnp.int32), piece_rows)
        allowed_pairs = (query_seg[:, None] == piece_seg[None, :]) & (
            piece_pos[None, :] <= query_pos[:, None]
        )
        raw_scores = jnp.einsum(
            "qhd,khd->hqk",
            query_heads,
            key_piece.reshape(piece_rows, HEADS, -1),
            preferred_element_type=jnp.float32,
        )
        return (jnp.where(allowed_pairs[None], raw_scores, FILLER), allowed_pairs[None])

    head_dim = model_width // HEADS
    start_state = (
        jnp.full((HEADS, length), FILLER, jnp.float32),
        jnp.zeros((HEADS, length), jnp.float32),
        jnp.zeros((HEADS, length, head_dim), jnp.float32),
    )
    accumulate_first_row = jnp.int32(0)
    accumulate_key_piece = lax.all_gather(keys_own, "blk", axis=0, tiled=True)
    accumulate_value_piece = lax.all_gather(values_own, "blk", axis=0, tiled=True)
    piece_rows = accumulate_value_piece.shape[0]

    def update(state):
        row_top, row_total, summed = state
        masked, allowed_pairs = scores_of(accumulate_key_piece, accumulate_first_row)
        new_top = jnp.maximum(row_top, jnp.max(masked, axis=2))
        factor = jnp.exp(ALPHA * (row_top - new_top))
        weights = jnp.where(allowed_pairs, jnp.exp(ALPHA * (masked - new_top[:, :, None])), 0.0)
        summed = summed * factor[:, :, None] + jnp.einsum(
            "hqk,khd->hqd",
            weights,
            accumulate_value_piece.reshape(piece_rows, HEADS, -1),
            preferred_element_type=jnp.float32,
        )
        return (new_top, row_total * factor + jnp.sum(weights, axis=2), summed)

    def unchanged(state):
        return state

    softmax_state = lax.cond(
        block_meets(accumulate_first_row, piece_rows), update, unchanged, start_state
    )
    row_top, row_total, summed = softmax_state
    attended_heads = summed / row_total[:, :, None]
    attended = jnp.transpose(attended_heads, (1, 0, 2)).reshape(length, model_width)
    attn_low = attended.astype(jnp.bfloat16)
    branch = jnp.dot(attn_low, out_weight, preferred_element_type=jnp.float32) + out_shift.astype(
        jnp.float32
    )
    second_hat, second_inv = normalize(branch)
    middle = inputs + second_hat * gain_rows[1] + shift_rows[1]
    third_hat, third_inv = normalize(middle)
    ffn_in = (third_hat * gain_rows[2] + shift_rows[2]).astype(jnp.bfloat16)
    pre_act = jnp.dot(ffn_in, up_weight, preferred_element_type=jnp.float32) + up_shift.astype(
        jnp.float32
    )
    activated, gelu_pullback = jax.vjp(gelu_tanh, pre_act)
    act_low = activated.astype(jnp.bfloat16)
    ffn_out = jnp.dot(act_low, down_weight, preferred_element_type=jnp.float32) + down_shift.astype(
        jnp.float32
    )
    fourth_hat, fourth_inv = normalize(ffn_out)
    result = middle + fourth_hat * gain_rows[3] + shift_rows[3]
    qkv_again, out_again, up_again, down_again, gain_again = (
        lax.all_gather(w_qkv, "dp", axis=0, tiled=True),
        lax.all_gather(w_out, "dp", axis=0, tiled=True),
        lax.all_gather(w_up, "dp", axis=0, tiled=True),
        lax.all_gather(w_down, "dp", axis=0, tiled=True),
        lax.all_gather(norm_gain, "dp", axis=1, tiled=True),
    )
    back_gains = gain_again.astype(jnp.float32)
    upstream = cotangent[0].astype(jnp.float32) * valid_rows[:, None]
    grad_ffn = norm_back(fourth_hat, fourth_inv, back_gains[3], upstream).astype(jnp.bfloat16)
    grad_down = jnp.einsum("tf,td->fd", act_low, grad_ffn, preferred_element_type=jnp.float32)
    grad_act = jnp.einsum("td,fd->tf", grad_ffn, down_again, preferred_element_type=jnp.float32)
    grad_pre = gelu_pullback(grad_act)[0].astype(jnp.bfloat16)
    grad_up = jnp.einsum("td,tf->df", ffn_in, grad_pre, preferred_element_type=jnp.float32)
    grad_ffn_in = jnp.einsum("tf,df->td", grad_pre, up_again, preferred_element_type=jnp.float32)
    grad_middle = upstream + norm_back(third_hat, third_inv, back_gains[2], grad_ffn_in)
    grad_branch = norm_back(second_hat, second_inv, back_gains[1], grad_middle).astype(jnp.bfloat16)
    grad_out = jnp.einsum("td,te->de", attn_low, grad_branch, preferred_element_type=jnp.float32)
    grad_attn = jnp.einsum(
        "te,de->td", grad_branch, out_again, preferred_element_type=jnp.float32
    ).astype(jnp.bfloat16)
    grad_heads = grad_attn.reshape(length, HEADS, -1)
    row_delta = jnp.einsum(
        "qhd,hqd->hq", grad_heads, attended_heads, preferred_element_type=jnp.float32
    )
    keys_all, values_all = (
        lax.all_gather(keys_own, "blk", axis=0, tiled=True),
        lax.all_gather(values_own, "blk", axis=0, tiled=True),
    )
    grad_query = jnp.zeros((length, HEADS, head_dim), jnp.float32)
    key_terms = []
    for block_index in range(block_count):
        first_row = block_index * length
        key_piece = keys_all[first_row : first_row + length]
        value_piece = values_all[first_row : first_row + length]

        def block_grads(operands):
            key_block, value_block = operands
            value_heads = value_block.reshape(length, HEADS, -1)
            masked, allowed_pairs = scores_of(key_block, first_row)
            probabilities = (
                jnp.where(allowed_pairs, jnp.exp(ALPHA * (masked - row_top[:, :, None])), 0.0)
                / row_total[:, :, None]
            )
            grad_probs = jnp.einsum(
                "qhd,khd->hqk", grad_heads, value_heads, preferred_element_type=jnp.float32
            )
            grad_scores = ALPHA * probabilities * (grad_probs - row_delta[:, :, None])
            query_term = jnp.einsum(
                "hqk,khd->qhd",
                grad_scores,
                key_block.reshape(length, HEADS, -1),
                preferred_element_type=jnp.float32,
            )
            grad_key = jnp.einsum(
                "hqk,qhd->khd", grad_scores, query_heads, preferred_element_type=jnp.float32
            )
            grad_value = jnp.einsum(
                "hqk,qhd->khd", probabilities, grad_heads, preferred_element_type=jnp.float32
            )
            return (
                query_term,
                jnp.concatenate(
                    [
                        grad_key.reshape(length, model_width),
                        grad_value.reshape(length, model_width),
                    ],
                    1,
                ),
            )

        def block_zeros(operands):
            return (
                jnp.zeros((length, HEADS, head_dim), jnp.float32),
                jnp.zeros((length, 2 * model_width), jnp.float32),
            )

        query_term, key_term = lax.cond(
            block_meets(first_row, length), block_grads, block_zeros, (key_piece, value_piece)
        )
        grad_query = grad_query + query_term
        key_terms.append(key_term)
    key_grads = lax.psum_scatter(
        jnp.concatenate(key_terms, 0).astype(jnp.bfloat16), "blk", scatter_dimension=0, tiled=True
    ).astype(jnp.float32)
    grad_keys = key_grads[:, :model_width].astype(jnp.bfloat16)
    grad_values = key_grads[:, model_width:].astype(jnp.bfloat16)
    grad_queries = grad_query.reshape(length, model_width).astype(jnp.bfloat16) * jnp.asarray(
        query_scale, jnp.bfloat16
    )
    grad_projected = jnp.concatenate([grad_queries, grad_keys, grad_values], 1)
    grad_qkv = jnp.einsum("td,te->de", attn_in, grad_projected, preferred_element_type=jnp.float32)
    grad_qv = jnp.concatenate(
        [
            jnp.sum(grad_queries.astype(jnp.float32), axis=0),
            jnp.sum(grad_values.astype(jnp.float32), axis=0),
        ]
    )
    grad_attn_in = jnp.einsum(
        "te,de->td", grad_projected, qkv_again, preferred_element_type=jnp.float32
    )
    grad_inputs = grad_middle + norm_back(first_hat, first_inv, back_gains[0], grad_attn_in)
    grad_gains = jnp.stack(
        [
            jnp.sum(grad_attn_in * first_hat, axis=0),
            jnp.sum(grad_middle * second_hat, axis=0),
            jnp.sum(grad_ffn_in * third_hat, axis=0),
            jnp.sum(upstream * fourth_hat, axis=0),
        ]
    )
    grad_shifts = jnp.stack(
        [
            jnp.sum(grad_attn_in, axis=0),
            jnp.sum(grad_middle, axis=0),
            jnp.sum(grad_ffn_in, axis=0),
            jnp.sum(upstream, axis=0),
        ]
    )
    grad_out_shift = jnp.sum(grad_branch.astype(jnp.float32), axis=0)
    grad_up_shift = jnp.sum(grad_pre.astype(jnp.float32), axis=0)
    grad_down_shift = jnp.sum(grad_ffn.astype(jnp.float32), axis=0)
    shares = (
        lax.psum_scatter(grad_qkv, "dp", scatter_dimension=0, tiled=True),
        lax.psum_scatter(grad_qv, "dp", scatter_dimension=0, tiled=True),
        lax.psum_scatter(grad_out, "dp", scatter_dimension=0, tiled=True),
        lax.psum_scatter(grad_out_shift, "dp", scatter_dimension=0, tiled=True),
        lax.psum_scatter(grad_up, "dp", scatter_dimension=0, tiled=True),
        lax.psum_scatter(grad_up_shift, "dp", scatter_dimension=0, tiled=True),
        lax.psum_scatter(grad_down, "dp", scatter_dimension=0, tiled=True),
        lax.psum_scatter(grad_down_shift, "dp", scatter_dimension=0, tiled=True),
        lax.psum_scatter(grad_gains, "dp", scatter_dimension=1, tiled=True),
        lax.psum_scatter(grad_shifts, "dp", scatter_dimension=1, tiled=True),
    )
    totals = (
        lax.psum(shares[0].astype(jnp.bfloat16), "blk").astype(jnp.float32),
        lax.psum(shares[1].astype(jnp.bfloat16), "blk").astype(jnp.float32),
        lax.psum(shares[2].astype(jnp.bfloat16), "blk").astype(jnp.float32),
        lax.psum(shares[3].astype(jnp.bfloat16), "blk").astype(jnp.float32),
        lax.psum(shares[4].astype(jnp.bfloat16), "blk").astype(jnp.float32),
        lax.psum(shares[5].astype(jnp.bfloat16), "blk").astype(jnp.float32),
        lax.psum(shares[6].astype(jnp.bfloat16), "blk").astype(jnp.float32),
        lax.psum(shares[7].astype(jnp.bfloat16), "blk").astype(jnp.float32),
        lax.psum(shares[8].astype(jnp.bfloat16), "blk").astype(jnp.float32),
        lax.psum(shares[9].astype(jnp.bfloat16), "blk").astype(jnp.float32),
    )
    return (result.astype(jnp.bfloat16)[None], grad_inputs[None]) + tuple(totals)


NZ = 4
NPOS = 512
LEN = 256
WIDTH = 1024
OWN = 512
HID = 2048
BF = jnp.bfloat16
F32 = jnp.float32
MESH = pl.DeviceIdType.MESH
MIB = 1 << 20
ROW_OUT, ROW_DOWN, ROW_GAIN, ROW_SHIFT = 3, 4, 5, 9
CORE = NZ


def dot_nn(a, b):
    return lax.dot_general(a, b, (((1,), (0,)), ((), ())), preferred_element_type=F32)


def dot_nt(a, b):
    return lax.dot_general(a, b, (((1,), (1,)), ((), ())), preferred_element_type=F32)


def dot_tn(a, b):
    return lax.dot_general(a, b, (((0,), (0,)), ((), ())), preferred_element_type=F32)


def loop(count, body):
    lax.fori_loop(0, count, lambda index, carry: (body(index), carry)[1], 0)


def mul(index, size):
    return pl.multiple_of(index * size, size)


class Net:
    def __init__(self, sems):
        self.chip = lax.axis_index("dp")
        self.core = lax.axis_index("blk")
        self.z = self.chip // 4
        self.y = (self.chip // 2) % 2
        self.x = self.chip % 2
        self.sems = sems
        self.used = 0
        self.unsent = []

    def sem(self):
        self.used += 1
        return self.sems.at[self.used - 1]

    def chip_at(self, z, y, x):
        return z * 4 + y * 2 + x

    def peers(self, dim):
        if dim == "x":
            return [(1, self.z, self.y, 1 - self.x, self.core)]
        if dim == "y":
            return [(1, self.z, 1 - self.y, self.x, self.core)]
        if dim == "c":
            return [(1, self.z, self.y, self.x, 1 - self.core)]
        return [(k, (self.z + k) % NZ, self.y, self.x, self.core) for k in range(1, NZ)]

    def send(self, src, dst, recv, peer):
        _, z, y, x, core = peer
        copy = pltpu.make_async_remote_copy(
            src_ref=src,
            dst_ref=dst,
            send_sem=self.sem(),
            recv_sem=recv,
            device_id=(self.chip_at(z, y, x), core),
            device_id_type=MESH,
        )
        copy.start()
        self.unsent.append(copy)
        return copy

    def drain(self):
        for copy in self.unsent:
            copy.wait_send()
        self.unsent = []

    def sibling(self, src, dst):
        return self.send(src, dst, self.sem(), self.peers("c")[0])

    def barrier(self):
        barrier = pltpu.get_barrier_semaphore()
        count = 0
        for dim in "xyzc":
            for _, z, y, x, core in self.peers(dim):
                pl.semaphore_signal(
                    barrier, inc=1, device_id=(self.chip_at(z, y, x), core), device_id_type=MESH
                )
                count += 1
        pl.semaphore_wait(barrier, count)


def gather_stages(net, ref, rows, lanes, order):
    def at(z, y, x):
        return ref.at[z, y, x, rows, lanes]

    def place(**given):
        where = {"z": net.z, "y": net.y, "x": net.x}
        where.update(given)
        return at(where["z"], where["y"], where["x"])

    every = {"z": slice(None), "y": slice(None), "x": slice(None)}
    first, second, third = order
    got_first, got_second, got_near, got_far = net.sem(), net.sem(), net.sem(), net.sem()

    def start():
        for peer in net.peers(first):
            net.send(place(), place(), got_first, peer)

    def await_bytes(view, sem):
        pltpu.make_async_copy(view, view, sem).wait()

    def after_first():
        if first == "z":
            await_bytes(ref.at[pl.ds(0, NZ - 1), net.y, net.x, rows, lanes], got_first)
        else:
            await_bytes(place(), got_first)
        held = {first: every[first]}
        for peer in net.peers(second):
            net.send(place(**held), place(**held), got_second, peer)
        for peer in net.peers(third):
            net.send(place(**held), place(**held), got_near, peer)

    def after_second():
        held = {first: every[first]}
        other = {"x": {"x": 1 - net.x}, "y": {"y": 1 - net.y}}[second]
        await_bytes(place(**held, **other), got_second)
        for peer in net.peers(third):
            net.send(place(**held, **other), place(**held, **other), got_far, peer)

    def finish():
        held = {first: every[first]}
        other = {"x": {"x": 1 - net.x}, "y": {"y": 1 - net.y}}[third]
        await_bytes(place(**held, **other), got_near)
        await_bytes(place(**held, **other), got_far)

    return start, after_first, after_second, finish


def scatter_stages(net, ref, rows, lanes, order, bufs, done):
    wide, half, line = bufs
    first, second = order[0], order[1]
    got_wide, got_half, got_line = net.sem(), net.sem(), net.sem()
    dtype = wide.dtype
    step = min(32, wide.shape[2])
    steps = wide.shape[2] // step

    def await_bytes(view, sem):
        pltpu.make_async_copy(view, view, sem).wait()

    def row_slice(part):
        return pl.ds(rows.start + part * step, step)

    def start():
        peer = net.peers(first)[0]
        if first == "x":
            src = ref.at[:, :, 1 - net.x, rows, lanes]
        else:
            src = ref.at[:, 1 - net.y, :, rows, lanes]
        net.send(src, wide, got_wide, peer)

    def after_first():
        await_bytes(wide, got_wide)

        def add(a, b):
            y, x = (b, net.x) if first == "x" else (net.y, b)
            for part in range(steps):
                kept = ref[a, y, x, row_slice(part), lanes].astype(F32)
                come = wide[a, b, pl.ds(part * step, step), :].astype(F32)
                ref[a, y, x, row_slice(part), lanes] = (kept + come).astype(dtype)

        gone = 1 - net.y if first == "x" else 1 - net.x
        loop(NZ, lambda a: add(a, gone))
        if first == "x":
            src = ref.at[:, 1 - net.y, net.x, rows, lanes]
        else:
            src = ref.at[:, net.y, 1 - net.x, rows, lanes]
        net.send(src, half, got_half, net.peers(second)[0])
        loop(NZ, lambda a: add(a, 1 - gone))

    def after_second():
        await_bytes(half, got_half)

        def add(a):
            for part in range(steps):
                kept = ref[a, net.y, net.x, row_slice(part), lanes].astype(F32)
                come = half[a, pl.ds(part * step, step), :].astype(F32)
                ref[a, net.y, net.x, row_slice(part), lanes] = (kept + come).astype(dtype)

        loop(NZ, add)
        for peer in net.peers("z"):
            net.send(
                ref.at[peer[1], net.y, net.x, rows, lanes], line.at[peer[0] - 1], got_line, peer
            )

    def finish():
        await_bytes(line, got_line)
        for part in range(steps):
            here = pl.ds(part * step, step)
            total = ref[net.z, net.y, net.x, row_slice(part), lanes].astype(F32)
            for k in range(NZ - 1):
                total = total + line[k, here, :].astype(F32)
            done(part * step, step, total)

    return start, after_first, after_second, finish


def layer_kernel(
    tok,
    doc,
    cot,
    wq_in,
    wo_in,
    wu_in,
    wd_in,
    vec_in,
    res_out,
    gtok_out,
    gq_out,
    go_out,
    gu_out,
    gd_out,
    gvec_out,
    wq,
    wo,
    wu,
    wd,
    vbuf,
    vecs,
    vq,
    vu,
    xin,
    qb,
    kb,
    vb,
    pb,
    att,
    attb,
    attx,
    hat1,
    hat2,
    inv1,
    inv2,
    mid,
    fin,
    act,
    dge,
    rcv,
    own,
    snd,
    gff,
    gbr,
    dob,
    dsb,
    gu,
    gd,
    swap,
    acc,
    acc_qv,
    acc_up,
    gvecs,
    gv,
    vother,
    r_q,
    r_o,
    r_u,
    r_d,
    r_v,
    st_q,
    st_o,
    st_u,
    st_d,
    sems,
    local_sems,
):
    (rq_a, rq_b), (ro_a, ro_b), (ru_a, ru_b), (rd_a, rd_b) = r_q, r_o, r_u, r_d
    net = Net(sems)
    core = net.core
    me = (net.z, net.y, net.x)

    locals_ = []

    def fetch(src, dst):
        copy = pltpu.make_async_copy(src, dst, local_sems.at[len(locals_)])
        copy.start()
        locals_.append(copy)

    def lanes_of(start, size):
        return pl.ds(pl.multiple_of(start, 128), size)

    for part in range(3):
        fetch(
            wq_in.at[:, lanes_of(part * WIDTH + core * OWN, OWN)],
            wq.at[net.z, net.y, net.x, :, pl.ds(part * OWN, OWN)],
        )
    fetch(wo_in.at[:, lanes_of(core * OWN, OWN)], wo.at[core, net.z, net.y, net.x])
    for i in range(NZ * 4):
        fetch(
            wu_in.at[:, lanes_of(i * 256 + core * 128, 128)],
            wu.at[net.z, net.y, net.x, :, pl.ds(i * 128, 128)],
        )
    fetch(wd_in.at[pl.ds(mul(core, 128), 128), :], wd.at[net.z, net.y, net.x])
    vbuf[net.z, net.y, net.x] = vec_in[...]
    wo_own = wo.at[core]

    full = slice(None)
    pieces = [gather_stages(net, vbuf, full, full, "zyx")]
    for ref, size in ((wq, 64), (wo_own, 64), (wu, 64), (wd, 128)):
        half = size // 2
        pieces.append(gather_stages(net, ref, pl.ds(0, half), full, "zyx"))
        pieces.append(gather_stages(net, ref, pl.ds(half, half), full, "zxy"))
    net.barrier()
    pieces[0][0]()
    ready = (0, 0, 0, 3, 3, 4, 4, 20, 20)
    landed = 0
    for piece, first in zip(pieces[1:], ready[1:], strict=True):
        need = {0: 3, 3: 4, 4: 20, 20: 21}[first]
        while landed < need:
            locals_[landed].wait()
            landed += 1
        piece[0]()

    events = [(0, 1), (0, 2), (0, 3)]
    for slot in range(1, len(pieces) + 4):
        for stage in (3, 2, 1):
            first = slot - 2 * (stage - 1)
            if first >= 1 and first < len(pieces) and first % 2 == 1:
                events.append((first, stage))
                events.append((first + 1, stage))
    state = {"at": 0}

    def pump(count):
        for _ in range(count):
            if state["at"] < len(events):
                piece, stage = events[state["at"]]
                pieces[piece][stage]()
                state["at"] += 1

    def pump_until(piece):
        last = max(events.index((p, 3)) for p in piece)
        while state["at"] <= last:
            pump(1)

    pump(3)

    for z in range(NZ):
        for y in range(2):
            both = vbuf[z, y, 0].astype(F32) + vbuf[z, y, 1].astype(F32)
            vecs[:, pl.ds((z * 2 + y) * 128, 128)] = both
    for y in range(2):
        for x in range(2):
            at = pl.ds((y * 2 + x) * 128, 128)
            vq[0:8, at] = vbuf[core, y, x].astype(F32)[0:8]
            vq[8:16, at] = vbuf[core + 2, y, x].astype(F32)[0:8]
            for z in range(NZ):
                block = vbuf[z, y, x].astype(F32)
                vu[0:1, pl.ds((z * 4 + y * 2 + x) * 128, 128)] = jnp.where(
                    core == 0, block[1:2], block[2:3]
                )

    def gain(n):
        return vecs[ROW_GAIN + n : ROW_GAIN + n + 1, :]

    def shift(n):
        return vecs[ROW_SHIFT + n : ROW_SHIFT + n + 1, :]

    def accumulate(row, value):
        parts = value.reshape(value.shape[0] // 8, 8, value.shape[1])
        acc[row] += jnp.sum(parts, axis=0)

    acc[...] = jnp.zeros_like(acc)
    acc_up[...] = jnp.zeros_like(acc_up)

    chunk = 32
    chunks = LEN // chunk

    def ln0(i):
        here = pl.ds(mul(i, chunk), chunk)
        hat, _ = normalize(tok[here, :].astype(F32))
        xin[core, here, :] = (hat * gain(0) + shift(0)).astype(BF)

    loop(chunks, ln0)
    got_x = net.sibling(xin.at[core], xin.at[core])
    pump(2)
    got_x.wait_recv()

    ends = []
    end = jnp.int32(0)
    for j in range(8):
        end = end + doc[0, j]
        ends.append(end)

    def segment(position):
        total = jnp.zeros(position.shape, jnp.int32)
        for value in ends:
            total = total + (position >= value).astype(jnp.int32)
        return total

    pump_until((1, 2))
    scale = 1.0 / (ALPHA * 8.0)

    def project(t):
        n = t // 2
        m = t % 2
        tile = pl.ds(mul(n, 256), 256)
        rows = pl.ds(mul(m, 256), 256)

        def part(index, dst, bias, factor):
            weight = wq[:, :, :, :, pl.ds(pl.multiple_of(index * OWN + n * 256, 256), 256)]
            value = dot_nn(xin[m], weight.reshape(WIDTH, 256))
            if bias is not None:
                value = value + vq[bias : bias + 1, tile]
            if factor is not None:
                value = value * factor
            dst[rows, tile] = value.astype(BF)

        part(0, qb, 0, scale)
        part(1, kb, None, None)
        part(2, vb, 8, None)

    loop(4, project)
    pump(2)

    lane = lax.broadcasted_iota(jnp.int32, (1, 128), 1)
    block = 128

    def attend(pair):
        at = pl.ds(mul(pair, 128), 128)
        for r in range(NPOS // block):
            rows = pl.ds(r * block, block)
            count = (r + 1) * block
            q_pos = r * block + lax.broadcasted_iota(jnp.int32, (block, 1), 0)
            k_pos = lax.broadcasted_iota(jnp.int32, (1, count), 1)
            allowed = (segment(q_pos) == segment(k_pos)) & (k_pos <= q_pos)
            q = qb[rows, at]
            k = kb[0:count, at]
            v = vb[0:count, at]
            outs = []
            for head in range(2):
                mine = (lane < 64) if head == 0 else (lane >= 64)
                scores = dot_nt(jnp.where(mine, q, jnp.zeros_like(q)), k)
                scores = jnp.where(allowed, scores, FILLER)
                top = jnp.max(scores, axis=1, keepdims=True)
                weights = jnp.exp(ALPHA * (scores - top))
                probs = weights * (1.0 / jnp.sum(weights, axis=1, keepdims=True))
                probs = probs.astype(BF)
                pb[pair * 2 + head, rows, 0:count] = probs
                outs.append(dot_nn(probs, v))
            out = jnp.where(lane < 64, outs[0], outs[1])
            att[rows, at] = out
            attb[rows, at] = out.astype(BF)

    loop(2, attend)
    pump(2)
    loop(2, lambda i: attend(i + 2))
    other_rows = pl.ds(mul(1 - core, LEN), LEN)
    own_rows = pl.ds(mul(core, LEN), LEN)
    got_att = net.sibling(attb.at[other_rows, :], attx)
    pump_until((3, 4))
    got_wo = net.sibling(wo_own, wo.at[core])
    got_att.wait_recv()
    got_wo.wait_recv()

    def branch_tile(n):
        lanes = pl.ds(mul(n % 2, 256), 256)
        mine = wo[n // 2, pl.ds(2 * core, 2), :, :, :, lanes].reshape(OWN, 256)
        theirs = wo[n // 2, pl.ds(2 * (1 - core), 2), :, :, :, lanes].reshape(OWN, 256)
        at = pl.ds(mul(n, 256), 256)
        own[:, at] = dot_nn(attb[own_rows, :], mine) + dot_nn(attx[...], theirs)

    loop(4, branch_tile)

    def ln12(i):
        here = pl.ds(mul(i, chunk), chunk)
        first, first_inv = normalize(own[here, :] + vecs[ROW_OUT : ROW_OUT + 1, :])
        hat1[here, :] = first
        inv1[here, :] = jnp.broadcast_to(first_inv, (chunk, 128))
        middle = tok[here, :].astype(F32) + first * gain(1) + shift(1)
        mid[here, :] = middle
        second, second_inv = normalize(middle)
        hat2[here, :] = second
        inv2[here, :] = jnp.broadcast_to(second_inv, (chunk, 128))
        fin[core, here, :] = (second * gain(2) + shift(2)).astype(BF)

    loop(chunks, ln12)
    got_fin = net.sibling(fin.at[core], fin.at[core])
    pump(2)
    got_fin.wait_recv()
    pump_until((5, 6))

    root = math.sqrt(2.0 / math.pi)

    def up_tile(t):
        n = t // 2
        m = t % 2
        at = pl.ds(mul(n, 256), 256)
        rows = pl.ds(mul(m, 256), 256)
        weight = wu[:, :, :, :, at].reshape(WIDTH, 256)
        u = dot_nn(fin[m], weight) + vu[0:1, at]
        square = u * u
        inner = jnp.tanh(root * (u + 0.044715 * (square * u)))
        half = 0.5 * (1.0 + inner)
        act[rows, at] = (u * half).astype(BF)
        slope = 0.5 * u * (1.0 - inner * inner) * (root * (1.0 + (3 * 0.044715) * square))
        dge[rows, at] = (half + slope).astype(BF)

    loop(8, up_tile)
    pump(2)
    loop(8, lambda i: up_tile(i + 8))
    pump(len(events))

    def down_tile(rows, dst):
        def body(n):
            at = pl.ds(mul(n, 256), 256)
            weight = wd[:, :, :, :, at].reshape(HID, 256)
            dst[:, at] = dot_nn(act[rows, :], weight)

        loop(4, body)

    down_tile(other_rows, snd)
    got_part = net.sibling(snd, rcv)
    down_tile(own_rows, own)
    got_part.wait_recv()

    filled = ends[-1]

    def upstream_of(i):
        here = pl.ds(mul(i, chunk), chunk)
        position = core * LEN + i * chunk + lax.broadcasted_iota(jnp.int32, (chunk, 1), 0)
        return cot[here, :].astype(F32) * (position < filled).astype(F32)

    def top_tile(i):
        here = pl.ds(mul(i, chunk), chunk)
        value = own[here, :] + rcv[here, :] + vecs[ROW_DOWN : ROW_DOWN + 1, :]
        hat, inv = normalize(value)
        res_out[here, :] = (mid[here, :] + hat * gain(3) + shift(3)).astype(BF)
        upstream = upstream_of(i)
        grad = norm_back(hat, inv, gain(3), upstream).astype(BF)
        gff[core, here, :] = grad
        accumulate(ROW_GAIN + 3, upstream * hat)
        accumulate(ROW_SHIFT + 3, upstream)
        accumulate(ROW_DOWN, grad.astype(F32))

    loop(chunks, top_tile)
    got_gff = net.sibling(gff.at[core], gff.at[core])

    out_copies = []

    def deliver(stage, out_views):
        for src, dst in out_views:
            copy = pltpu.make_async_copy(src, dst, local_sems.at[21 + len(out_copies)])
            copy.start()
            out_copies.append((copy, net.sibling(src, dst)))

    def store_to(stage, row0):
        def done(offset, size, total):
            stage[row0 + offset : row0 + offset + size, :] = total

        return done

    wgrad = {}
    for name, ref, lanes, size, bufs, stage in (
        ("d", gd, full, 128, (rd_a, rd_b), st_d),
        ("u", gu, full, 64, (ru_a, ru_b), st_u),
        ("o", wu, pl.ds(3 * OWN, OWN), 64, (ro_a, ro_b), st_o),
        ("q", wu, pl.ds(0, 3 * OWN), 64, (rq_a, rq_b), st_q),
    ):
        half = size // 2
        wgrad[name] = [
            scatter_stages(net, ref, pl.ds(0, half), lanes, "xyz", bufs[0], store_to(stage, 0)),
            scatter_stages(
                net, ref, pl.ds(half, half), lanes, "yxz", bufs[1], store_to(stage, half)
            ),
        ]

    def ship(name, half):
        def views():
            if name == "d":
                rows = pl.ds(pl.multiple_of(core * 128 + half * 64, 64), 64)
                return [(st_d.at[half * 64 : half * 64 + 64, :], gd_out.at[rows, :])]
            rows = slice(half * 32, half * 32 + 32)
            if name == "u":
                return [
                    (
                        st_u.at[rows, pl.ds(i * 128, 128)],
                        gu_out.at[rows, lanes_of(i * 256 + core * 128, 128)],
                    )
                    for i in range(NZ * 4)
                ]
            if name == "o":
                return [(st_o.at[rows, :], go_out.at[rows, lanes_of(core * OWN, OWN)])]
            return [
                (
                    st_q.at[rows, pl.ds(p * OWN, OWN)],
                    gq_out.at[rows, lanes_of(p * WIDTH + core * OWN, OWN)],
                )
                for p in range(3)
            ]

        deliver(None, views())

    queue = []

    def launch(name):
        for half in range(2):
            wgrad[name][half][0]()

    def relay(name, stage):
        for half in range(2):
            wgrad[name][half][stage]()
            if stage == 3:
                ship(name, half)

    got_gff.wait_recv()

    def gdown_tile(t):
        k = t // 2
        z = k // 2
        y = k % 2
        at = pl.ds(mul(t % 2, 512), 512)
        left = act[:, pl.ds(mul(k, 256), 256)]
        grad = gff[:, :, at].reshape(NPOS, 512)
        gd[z, y, :, :, at] = dot_tn(left, grad).astype(BF).reshape(2, 128, 512)

    loop(16, gdown_tile)
    launch("d")

    def gpre_tile(t):
        k = t // 2
        m = t % 2
        at = pl.ds(mul(k, 256), 256)
        rows = pl.ds(mul(m, 256), 256)
        weight = wd[k // 2, k % 2].reshape(256, WIDTH)
        value = dot_nt(gff[m], weight) * dge[rows, at].astype(F32)
        value = value.astype(BF)
        dge[rows, at] = value
        acc_up[:, at] += jnp.sum(value.astype(F32).reshape(32, 8, 256), axis=0)

    loop(16, gpre_tile)

    def gup_tile(t):
        z = t // 4
        at = pl.ds(mul(t % 4, 512), 512)
        left = fin[:, :, pl.ds(mul(z, 256), 256)].reshape(NPOS, 256)
        gu[z, :, :, :, at] = dot_tn(left, dge[:, at]).astype(BF).reshape(2, 2, 64, 512)

    loop(16, gup_tile)
    launch("u")

    net.drain()

    def gfi_tile(rows, dst):
        def body(z):
            weight = wu[z].reshape(256, HID)
            dst[:, pl.ds(mul(z, 256), 256)] = dot_nt(dge[rows, :], weight)

        loop(NZ, body)

    gfi_tile(other_rows, snd)
    got_part = net.sibling(snd, rcv)
    gfi_tile(own_rows, own)
    relay("d", 1)
    got_part.wait_recv()

    def middle_tile(i):
        here = pl.ds(mul(i, chunk), chunk)
        grad_in = own[here, :] + rcv[here, :]
        second = hat2[here, :]
        accumulate(ROW_GAIN + 2, grad_in * second)
        accumulate(ROW_SHIFT + 2, grad_in)
        grad_mid = upstream_of(i) + norm_back(second, inv2[here, 0:1], gain(2), grad_in)
        mid[here, :] = grad_mid
        first = hat1[here, :]
        accumulate(ROW_GAIN + 1, grad_mid * first)
        accumulate(ROW_SHIFT + 1, grad_mid)
        grad = norm_back(first, inv1[here, 0:1], gain(1), grad_mid).astype(BF)
        gbr[core, here, :] = grad
        accumulate(ROW_OUT, grad.astype(F32))

    loop(chunks, middle_tile)
    got_gbr = net.sibling(gbr.at[core], gbr.at[core])
    relay("u", 1)
    got_gbr.wait_recv()

    go = wu.at[:, :, :, :, pl.ds(3 * OWN, OWN)]

    def gout_tile(k, cols, put):
        left = attb[:, pl.ds(mul(k, 256), 256)]
        grad = gbr[:, :, cols].reshape(NPOS, OWN)
        put(k, dot_tn(left, grad).astype(BF).reshape(2, 2, 64, OWN))

    def put_swap(k, value):
        swap[k] = value

    def put_own(k, value):
        wu[2 * core + k, :, :, :, pl.ds(3 * OWN, OWN)] = value

    loop(2, lambda k: gout_tile(k, lanes_of((1 - core) * OWN, OWN), put_swap))
    got_swap = net.sibling(swap, go.at[pl.ds(2 * core, 2)])
    loop(2, lambda k: gout_tile(k, lanes_of(core * OWN, OWN), put_own))

    def gatt_tile(t):
        k = t // 2
        m = t % 2
        left = wo[0, 2 * core + k].reshape(256, OWN)
        right = wo[1, 2 * core + k].reshape(256, OWN)
        value = dot_nt(gbr[m, :, 0:OWN], left) + dot_nt(gbr[m, :, OWN:WIDTH], right)
        dob[pl.ds(mul(m, 256), 256), pl.ds(mul(k, 256), 256)] = value.astype(BF)

    loop(4, gatt_tile)
    got_swap.wait_recv()
    launch("o")

    def attend_back(pair):
        at = pl.ds(mul(pair, 128), 128)
        sums = []
        for head in range(2):
            mine = (lane < 64) if head == 0 else (lane >= 64)
            queries_ = []
            for r in range(NPOS // block):
                rows = pl.ds(r * block, block)
                count = (r + 1) * block
                grad = dob[rows, at]
                grad = jnp.where(mine, grad, jnp.zeros_like(grad))
                delta = jnp.sum(grad.astype(F32) * att[rows, at], axis=1, keepdims=True)
                probs = pb[pair * 2 + head, rows, 0:count].astype(F32)
                grad_probs = dot_nt(grad, vb[0:count, at])
                scores = (ALPHA * probs * (grad_probs - delta)).astype(BF)
                dsb[rows, 0:count] = scores
                queries_.append(dot_nn(scores, kb[0:count, at]))
            keys_, values_ = [], []
            for r in range(NPOS // block):
                rows = pl.ds(r * block, NPOS - r * block)
                cols = pl.ds(r * block, block)
                keys_.append(dot_tn(dsb[rows, cols], qb[rows, at]))
                values_.append(dot_tn(pb[pair * 2 + head, rows, cols], dob[rows, at]))
            sums.append((queries_, keys_, values_))
        total_q = jnp.zeros((8, 128), F32)
        total_v = jnp.zeros((8, 128), F32)
        for r in range(NPOS // block):
            rows = pl.ds(r * block, block)
            merged = [
                jnp.where(lane < 64, sums[0][i][r], sums[1][i][r]).astype(BF) for i in range(3)
            ]
            grad_q = merged[0] * jnp.asarray(scale, BF)
            qb[rows, at] = grad_q
            kb[rows, at] = merged[1]
            vb[rows, at] = merged[2]
            total_q += jnp.sum(grad_q.astype(F32).reshape(block // 8, 8, 128), axis=0)
            total_v += jnp.sum(merged[2].astype(F32).reshape(block // 8, 8, 128), axis=0)
        acc_qv[0, :, at] = total_q
        acc_qv[1, :, at] = total_v

    loop(1, attend_back)
    relay("d", 2)
    loop(1, lambda i: attend_back(i + 1))
    loop(1, lambda i: attend_back(i + 2))
    relay("u", 2)
    loop(1, lambda i: attend_back(i + 3))
    relay("o", 1)

    def gqkv_tile(z):
        left = xin[:, :, pl.ds(mul(z, 256), 256)].reshape(NPOS, 256)
        for part, ref in enumerate((qb, kb, vb)):
            value = dot_tn(left, ref[...]).astype(BF)
            wu[z, :, :, :, pl.ds(part * OWN, OWN)] = value.reshape(2, 2, 64, OWN)

    loop(NZ, gqkv_tile)
    launch("q")
    net.drain()

    def gai_tile(rows, dst):
        def body(z):
            value = None
            for part, ref in enumerate((qb, kb, vb)):
                weight = wq[z, :, :, :, pl.ds(part * OWN, OWN)].reshape(256, OWN)
                term = dot_nt(ref[rows, :], weight)
                value = term if value is None else value + term
            dst[:, pl.ds(mul(z, 256), 256)] = value

        loop(NZ, body)

    gai_tile(other_rows, snd)
    got_part = net.sibling(snd, rcv)
    gai_tile(own_rows, own)
    relay("d", 3)
    relay("o", 2)
    got_part.wait_recv()

    def bottom_tile(i):
        here = pl.ds(mul(i, chunk), chunk)
        hat, inv = normalize(tok[here, :].astype(F32))
        grad_in = own[here, :] + rcv[here, :]
        accumulate(ROW_GAIN, grad_in * hat)
        accumulate(ROW_SHIFT, grad_in)
        gtok_out[here, :] = mid[here, :] + norm_back(hat, inv, gain(0), grad_in)

    loop(chunks, bottom_tile)

    for row in range(16):
        gvecs[row : row + 1, :] = jnp.sum(acc[row], axis=0, keepdims=True)
    row_id = lax.broadcasted_iota(jnp.int32, (16, 1), 0)
    for z in range(NZ):
        for y in range(2):
            base = gvecs[:, pl.ds((z * 2 + y) * 128, 128)]
            for x in range(2):
                at = pl.ds((y * 2 + x) * 128, 128)
                kind = 0 if z < 2 else 1
                qv_row = jnp.sum(acc_qv[kind, :, at], axis=0, keepdims=True)
                qv_row = jnp.where(core == z % 2, qv_row, 0.0)
                up_at = pl.ds((z * 4 + y * 2 + x) * 128, 128)
                up_row = jnp.sum(acc_up[:, up_at], axis=0, keepdims=True)
                value = base + jnp.where(row_id == 0, qv_row, 0.0)
                gv[z, y, x] = value + jnp.where(row_id == 1 + core, up_row, 0.0)

    def keep_vec(offset, size, total):
        gvec_out[offset : offset + size, :] = total

    vec = scatter_stages(net, gv, pl.ds(0, 16), full, "xyz", r_v, keep_vec)
    vec[0]()
    relay("q", 1)
    vec[1]()
    relay("u", 3)
    vec[2]()
    relay("o", 3)
    vec[3]()
    got_vec = net.sibling(gvec_out, vother)
    relay("q", 2)
    got_vec.wait()
    net.unsent = [copy for copy in net.unsent if copy is not got_vec]
    gvec_out[...] = gvec_out[...] + vother[...]
    relay("q", 3)
    for copy, remote in out_copies:
        copy.wait()
        remote.wait_recv()
    net.drain()


def scatter_bufs(rows, cols, dtype):
    return [
        pltpu.VMEM((NZ, 2, rows, cols), dtype),
        pltpu.VMEM((NZ, rows, cols), dtype),
        pltpu.VMEM((NZ - 1, rows, cols), dtype),
    ]


def fused(
    tokens,
    doc_lengths,
    cotangent,
    w_qkv,
    qv_bias,
    w_out,
    out_bias,
    w_up,
    up_bias,
    w_down,
    down_bias,
    norm_gain,
    norm_bias,
):
    right = lax.axis_index("dp") % 2 == 1
    narrow = jnp.concatenate([out_bias[None], down_bias[None], norm_gain, norm_bias], 0)
    blank = jnp.zeros_like(narrow)
    wide = jnp.where(
        right, jnp.concatenate([blank, narrow], 1), jnp.concatenate([narrow, blank], 1)
    )
    packed = jnp.concatenate(
        [qv_bias[None], up_bias.reshape(2, 128), wide, jnp.zeros((3, 128), BF)], 0
    )
    vmem = pl.BlockSpec(memory_space=pltpu.VMEM)
    anywhere = pl.BlockSpec(memory_space=pl.ANY)
    scratch = [
        pltpu.VMEM((NZ, 2, 2, 64, 3 * OWN), BF),
        pltpu.VMEM((2, NZ, 2, 2, 64, OWN), BF),
        pltpu.VMEM((NZ, 2, 2, 64, HID), BF),
        pltpu.VMEM((NZ, 2, 2, 128, WIDTH), BF),
        pltpu.VMEM((NZ, 2, 2, 16, 128), BF),
        pltpu.VMEM((16, WIDTH), F32),
        pltpu.VMEM((16, OWN), F32),
        pltpu.VMEM((8, HID), F32),
        pltpu.VMEM((2, LEN, WIDTH), BF),
        pltpu.VMEM((NPOS, OWN), BF),
        pltpu.VMEM((NPOS, OWN), BF),
        pltpu.VMEM((NPOS, OWN), BF),
        pltpu.VMEM((8, NPOS, NPOS), BF),
        pltpu.VMEM((NPOS, OWN), F32),
        pltpu.VMEM((NPOS, OWN), BF),
        pltpu.VMEM((LEN, OWN), BF),
        pltpu.VMEM((LEN, WIDTH), F32),
        pltpu.VMEM((LEN, WIDTH), F32),
        pltpu.VMEM((LEN, 128), F32),
        pltpu.VMEM((LEN, 128), F32),
        pltpu.VMEM((LEN, WIDTH), F32),
        pltpu.VMEM((2, LEN, WIDTH), BF),
        pltpu.VMEM((NPOS, HID), BF),
        pltpu.VMEM((NPOS, HID), BF),
        pltpu.VMEM((LEN, WIDTH), F32),
        pltpu.VMEM((LEN, WIDTH), F32),
        pltpu.VMEM((LEN, WIDTH), F32),
        pltpu.VMEM((2, LEN, WIDTH), BF),
        pltpu.VMEM((2, LEN, WIDTH), BF),
        pltpu.VMEM((NPOS, OWN), BF),
        pltpu.VMEM((NPOS, NPOS), BF),
        pltpu.VMEM((NZ, 2, 2, 64, HID), BF),
        pltpu.VMEM((NZ, 2, 2, 128, WIDTH), BF),
        pltpu.VMEM((2, 2, 2, 64, OWN), BF),
        pltpu.VMEM((16, 8, WIDTH), F32),
        pltpu.VMEM((2, 8, OWN), F32),
        pltpu.VMEM((8, HID), F32),
        pltpu.VMEM((16, WIDTH), F32),
        pltpu.VMEM((NZ, 2, 2, 16, 128), F32),
        pltpu.VMEM((16, 128), F32),
        [scatter_bufs(32, 3 * OWN, BF)] * 2,
        [scatter_bufs(32, OWN, BF)] * 2,
        [scatter_bufs(32, HID, BF)] * 2,
        [scatter_bufs(64, WIDTH, BF)] * 2,
        scatter_bufs(16, 128, F32),
        pltpu.VMEM((64, 3 * OWN), F32),
        pltpu.VMEM((64, OWN), F32),
        pltpu.VMEM((64, HID), F32),
        pltpu.VMEM((128, WIDTH), F32),
        pltpu.SemaphoreType.DMA((300,)),
        pltpu.SemaphoreType.DMA((70,)),
    ]
    outs = pl.pallas_call(
        layer_kernel,
        out_shape=[
            jax.ShapeDtypeStruct((LEN, WIDTH), BF),
            jax.ShapeDtypeStruct((LEN, WIDTH), F32),
            jax.ShapeDtypeStruct((64, 3 * WIDTH), F32),
            jax.ShapeDtypeStruct((64, WIDTH), F32),
            jax.ShapeDtypeStruct((64, 2 * HID), F32),
            jax.ShapeDtypeStruct((256, WIDTH), F32),
            jax.ShapeDtypeStruct((16, 128), F32),
        ],
        in_specs=[vmem, pl.BlockSpec(memory_space=pltpu.SMEM), vmem]
        + [anywhere] * 4
        + [vmem],
        out_specs=[vmem, vmem] + [anywhere] * 4 + [vmem],
        scratch_shapes=scratch,
        compiler_params=pltpu.CompilerParams(
            collective_id=0, has_side_effects=True, vmem_limit_bytes=63 * MIB
        ),
        name="layer",
    )(tokens[0], doc_lengths, cotangent[0], w_qkv, w_out, w_up, w_down, packed)
    result, grad_inputs, grad_qkv, grad_out, grad_up, grad_down, vec = outs
    part = jnp.where(right, vec[3:13, 64:], vec[3:13, :64])
    return (
        result[None],
        grad_inputs[None],
        grad_qkv,
        vec[0],
        grad_out,
        part[0],
        grad_up,
        vec[1:3].reshape(256),
        grad_down,
        part[1],
        part[2:6],
        part[6:10],
    )


def solution(mesh):
    placed = (
        P("dp", "blk", None),
        P("dp", None),
        P("dp", "blk", None),
        P("dp", None),
        P("dp"),
        P("dp", None),
        P("dp"),
        P("dp", None),
        P("dp"),
        P("dp", None),
        P("dp"),
        P(None, "dp"),
        P(None, "dp"),
    )
    sizes = (mesh.shape["dp"], mesh.shape["blk"])
    return jax.shard_map(
        fused if sizes == (NZ * 4, 2) else shards,
        mesh=mesh,
        in_specs=placed,
        out_specs=(
            P("dp", "blk", None),
            P("dp", "blk", None),
            P("dp", None),
            P("dp"),
            P("dp", None),
            P("dp"),
            P("dp", None),
            P("dp"),
            P("dp", None),
            P("dp"),
            P(None, "dp"),
            P(None, "dp"),
        ),
        check_vma=False,
    )
```

```python
import functools
import math

import jax
import jax.numpy as jnp
from jax import lax
from jax.experimental import pallas as pl
from jax.experimental.pallas import tpu as pltpu
from jax.sharding import PartitionSpec as P

HEADS = 16
ALPHA = 32


EPSILON = 1e-05
FILLER = -1000000000.0


def normalize(values):
    center = values - jnp.mean(values, axis=-1, keepdims=True)
    inverse = lax.rsqrt(jnp.mean(center * center, axis=-1, keepdims=True) + EPSILON)
    return (center * inverse, inverse)


def norm_back(normed, inverse, gain_row, upstream):
    scaled = upstream * gain_row
    return inverse * (
        scaled
        - jnp.mean(scaled, axis=-1, keepdims=True)
        - normed * jnp.mean(scaled * normed, axis=-1, keepdims=True)
    )


def segment_of(position, doc_ends):
    return jnp.sum((position[:, None] >= doc_ends[None, :]).astype(jnp.int32), axis=1)


def gelu_tanh(values):
    return jax.nn.gelu(values, approximate=True)


def shards(
    tokens,
    doc_lengths,
    cotangent,
    w_qkv,
    qv_bias,
    w_out,
    out_bias,
    w_up,
    up_bias,
    w_down,
    down_bias,
    norm_gain,
    norm_bias,
):
    inputs = tokens[0].astype(jnp.float32)
    length = inputs.shape[0]
    model_width = inputs.shape[1]
    block_count = lax.axis_size("blk")
    seq_len = length * block_count
    offset = lax.axis_index("blk") * length
    doc_ends = jnp.cumsum(doc_lengths[0])
    filled = doc_ends[-1]
    query_pos = offset + jnp.arange(length, dtype=jnp.int32)
    query_seg = segment_of(query_pos, doc_ends)
    valid_rows = (query_pos < filled).astype(jnp.float32)
    key_seg = segment_of(jnp.arange(seq_len, dtype=jnp.int32), doc_ends)
    last_query = offset + length - 1

    def block_meets(first_row, piece_rows):
        first_at = jnp.asarray(first_row, jnp.int32)
        first_seg = lax.dynamic_index_in_dim(key_seg, first_at, keepdims=False)
        last_seg = lax.dynamic_index_in_dim(key_seg, first_at + piece_rows - 1, keepdims=False)
        return (first_at <= last_query) & (first_seg <= query_seg[-1]) & (last_seg >= query_seg[0])

    gathered = (
        lax.all_gather(w_qkv, "dp", axis=0, tiled=True),
        lax.all_gather(qv_bias, "dp", axis=0, tiled=True),
        lax.all_gather(w_out, "dp", axis=0, tiled=True),
        lax.all_gather(out_bias, "dp", axis=0, tiled=True),
        lax.all_gather(w_up, "dp", axis=0, tiled=True),
        lax.all_gather(up_bias, "dp", axis=0, tiled=True),
        lax.all_gather(w_down, "dp", axis=0, tiled=True),
        lax.all_gather(down_bias, "dp", axis=0, tiled=True),
        lax.all_gather(norm_gain, "dp", axis=1, tiled=True),
        lax.all_gather(norm_bias, "dp", axis=1, tiled=True),
    )
    (
        qkv_weight,
        qv_shift,
        out_weight,
        out_shift,
        up_weight,
        up_shift,
        down_weight,
        down_shift,
        gain_all,
        shift_all,
    ) = gathered
    gain_rows = gain_all.astype(jnp.float32)
    shift_rows = shift_all.astype(jnp.float32)
    query_scale = 1.0 / (ALPHA * math.sqrt(model_width // HEADS))
    first_hat, first_inv = normalize(inputs)
    attn_in = (first_hat * gain_rows[0] + shift_rows[0]).astype(jnp.bfloat16)
    projected = jnp.dot(attn_in, qkv_weight, preferred_element_type=jnp.float32)
    qv_float = qv_shift.astype(jnp.float32)
    queries = ((projected[:, :model_width] + qv_float[:model_width]) * query_scale).astype(
        jnp.bfloat16
    )
    keys_own = projected[:, model_width : 2 * model_width].astype(jnp.bfloat16)
    values_own = (projected[:, 2 * model_width :] + qv_float[model_width:]).astype(jnp.bfloat16)
    query_heads = queries.reshape(length, HEADS, -1)

    def scores_of(key_piece, first_row):
        piece_rows = key_piece.shape[0]
        piece_pos = first_row + jnp.arange(piece_rows, dtype=jnp.int32)
        piece_seg = lax.dynamic_slice_in_dim(key_seg, jnp.asarray(first_row, jnp.int32), piece_rows)
        allowed_pairs = (query_seg[:, None] == piece_seg[None, :]) & (
            piece_pos[None, :] <= query_pos[:, None]
        )
        raw_scores = jnp.einsum(
            "qhd,khd->hqk",
            query_heads,
            key_piece.reshape(piece_rows, HEADS, -1),
            preferred_element_type=jnp.float32,
        )
        return (jnp.where(allowed_pairs[None], raw_scores, FILLER), allowed_pairs[None])

    head_dim = model_width // HEADS
    start_state = (
        jnp.full((HEADS, length), FILLER, jnp.float32),
        jnp.zeros((HEADS, length), jnp.float32),
        jnp.zeros((HEADS, length, head_dim), jnp.float32),
    )
    accumulate_first_row = jnp.int32(0)
    accumulate_key_piece = lax.all_gather(keys_own, "blk", axis=0, tiled=True)
    accumulate_value_piece = lax.all_gather(values_own, "blk", axis=0, tiled=True)
    piece_rows = accumulate_value_piece.shape[0]

    def update(state):
        row_top, row_total, summed = state
        masked, allowed_pairs = scores_of(accumulate_key_piece, accumulate_first_row)
        new_top = jnp.maximum(row_top, jnp.max(masked, axis=2))
        factor = jnp.exp(ALPHA * (row_top - new_top))
        weights = jnp.where(allowed_pairs, jnp.exp(ALPHA * (masked - new_top[:, :, None])), 0.0)
        summed = summed * factor[:, :, None] + jnp.einsum(
            "hqk,khd->hqd",
            weights,
            accumulate_value_piece.reshape(piece_rows, HEADS, -1),
            preferred_element_type=jnp.float32,
        )
        return (new_top, row_total * factor + jnp.sum(weights, axis=2), summed)

    def unchanged(state):
        return state

    softmax_state = lax.cond(
        block_meets(accumulate_first_row, piece_rows), update, unchanged, start_state
    )
    row_top, row_total, summed = softmax_state
    attended_heads = summed / row_total[:, :, None]
    attended = jnp.transpose(attended_heads, (1, 0, 2)).reshape(length, model_width)
    attn_low = attended.astype(jnp.bfloat16)
    branch = jnp.dot(attn_low, out_weight, preferred_element_type=jnp.float32) + out_shift.astype(
        jnp.float32
    )
    second_hat, second_inv = normalize(branch)
    middle = inputs + second_hat * gain_rows[1] + shift_rows[1]
    third_hat, third_inv = normalize(middle)
    ffn_in = (third_hat * gain_rows[2] + shift_rows[2]).astype(jnp.bfloat16)
    pre_act = jnp.dot(ffn_in, up_weight, preferred_element_type=jnp.float32) + up_shift.astype(
        jnp.float32
    )
    activated, gelu_pullback = jax.vjp(gelu_tanh, pre_act)
    act_low = activated.astype(jnp.bfloat16)
    ffn_out = jnp.dot(act_low, down_weight, preferred_element_type=jnp.float32) + down_shift.astype(
        jnp.float32
    )
    fourth_hat, fourth_inv = normalize(ffn_out)
    result = middle + fourth_hat * gain_rows[3] + shift_rows[3]
    qkv_again, out_again, up_again, down_again, gain_again = (
        lax.all_gather(w_qkv, "dp", axis=0, tiled=True),
        lax.all_gather(w_out, "dp", axis=0, tiled=True),
        lax.all_gather(w_up, "dp", axis=0, tiled=True),
        lax.all_gather(w_down, "dp", axis=0, tiled=True),
        lax.all_gather(norm_gain, "dp", axis=1, tiled=True),
    )
    back_gains = gain_again.astype(jnp.float32)
    upstream = cotangent[0].astype(jnp.float32) * valid_rows[:, None]
    grad_ffn = norm_back(fourth_hat, fourth_inv, back_gains[3], upstream).astype(jnp.bfloat16)
    grad_down = jnp.einsum("tf,td->fd", act_low, grad_ffn, preferred_element_type=jnp.float32)
    grad_act = jnp.einsum("td,fd->tf", grad_ffn, down_again, preferred_element_type=jnp.float32)
    grad_pre = gelu_pullback(grad_act)[0].astype(jnp.bfloat16)
    grad_up = jnp.einsum("td,tf->df", ffn_in, grad_pre, preferred_element_type=jnp.float32)
    grad_ffn_in = jnp.einsum("tf,df->td", grad_pre, up_again, preferred_element_type=jnp.float32)
    grad_middle = upstream + norm_back(third_hat, third_inv, back_gains[2], grad_ffn_in)
    grad_branch = norm_back(second_hat, second_inv, back_gains[1], grad_middle).astype(jnp.bfloat16)
    grad_out = jnp.einsum("td,te->de", attn_low, grad_branch, preferred_element_type=jnp.float32)
    grad_attn = jnp.einsum(
        "te,de->td", grad_branch, out_again, preferred_element_type=jnp.float32
    ).astype(jnp.bfloat16)
    grad_heads = grad_attn.reshape(length, HEADS, -1)
    row_delta = jnp.einsum(
        "qhd,hqd->hq", grad_heads, attended_heads, preferred_element_type=jnp.float32
    )
    keys_all, values_all = (
        lax.all_gather(keys_own, "blk", axis=0, tiled=True),
        lax.all_gather(values_own, "blk", axis=0, tiled=True),
    )
    grad_query = jnp.zeros((length, HEADS, head_dim), jnp.float32)
    key_terms = []
    for block_index in range(block_count):
        first_row = block_index * length
        key_piece = keys_all[first_row : first_row + length]
        value_piece = values_all[first_row : first_row + length]

        def block_grads(operands):
            key_block, value_block = operands
            value_heads = value_block.reshape(length, HEADS, -1)
            masked, allowed_pairs = scores_of(key_block, first_row)
            probabilities = (
                jnp.where(allowed_pairs, jnp.exp(ALPHA * (masked - row_top[:, :, None])), 0.0)
                / row_total[:, :, None]
            )
            grad_probs = jnp.einsum(
                "qhd,khd->hqk", grad_heads, value_heads, preferred_element_type=jnp.float32
            )
            grad_scores = ALPHA * probabilities * (grad_probs - row_delta[:, :, None])
            query_term = jnp.einsum(
                "hqk,khd->qhd",
                grad_scores,
                key_block.reshape(length, HEADS, -1),
                preferred_element_type=jnp.float32,
            )
            grad_key = jnp.einsum(
                "hqk,qhd->khd", grad_scores, query_heads, preferred_element_type=jnp.float32
            )
            grad_value = jnp.einsum(
                "hqk,qhd->khd", probabilities, grad_heads, preferred_element_type=jnp.float32
            )
            return (
                query_term,
                jnp.concatenate(
                    [
                        grad_key.reshape(length, model_width),
                        grad_value.reshape(length, model_width),
                    ],
                    1,
                ),
            )

        def block_zeros(operands):
            return (
                jnp.zeros((length, HEADS, head_dim), jnp.float32),
                jnp.zeros((length, 2 * model_width), jnp.float32),
            )

        query_term, key_term = lax.cond(
            block_meets(first_row, length), block_grads, block_zeros, (key_piece, value_piece)
        )
        grad_query = grad_query + query_term
        key_terms.append(key_term)
    key_grads = lax.psum_scatter(
        jnp.concatenate(key_terms, 0).astype(jnp.bfloat16), "blk", scatter_dimension=0, tiled=True
    ).astype(jnp.float32)
    grad_keys = key_grads[:, :model_width].astype(jnp.bfloat16)
    grad_values = key_grads[:, model_width:].astype(jnp.bfloat16)
    grad_queries = grad_query.reshape(length, model_width).astype(jnp.bfloat16) * jnp.asarray(
        query_scale, jnp.bfloat16
    )
    grad_projected = jnp.concatenate([grad_queries, grad_keys, grad_values], 1)
    grad_qkv = jnp.einsum("td,te->de", attn_in, grad_projected, preferred_element_type=jnp.float32)
    grad_qv = jnp.concatenate(
        [
            jnp.sum(grad_queries.astype(jnp.float32), axis=0),
            jnp.sum(grad_values.astype(jnp.float32), axis=0),
        ]
    )
    grad_attn_in = jnp.einsum(
        "te,de->td", grad_projected, qkv_again, preferred_element_type=jnp.float32
    )
    grad_inputs = grad_middle + norm_back(first_hat, first_inv, back_gains[0], grad_attn_in)
    grad_gains = jnp.stack(
        [
            jnp.sum(grad_attn_in * first_hat, axis=0),
            jnp.sum(grad_middle * second_hat, axis=0),
            jnp.sum(grad_ffn_in * third_hat, axis=0),
            jnp.sum(upstream * fourth_hat, axis=0),
        ]
    )
    grad_shifts = jnp.stack(
        [
            jnp.sum(grad_attn_in, axis=0),
            jnp.sum(grad_middle, axis=0),
            jnp.sum(grad_ffn_in, axis=0),
            jnp.sum(upstream, axis=0),
        ]
    )
    grad_out_shift = jnp.sum(grad_branch.astype(jnp.float32), axis=0)
    grad_up_shift = jnp.sum(grad_pre.astype(jnp.float32), axis=0)
    grad_down_shift = jnp.sum(grad_ffn.astype(jnp.float32), axis=0)
    shares = (
        lax.psum_scatter(grad_qkv, "dp", scatter_dimension=0, tiled=True),
        lax.psum_scatter(grad_qv, "dp", scatter_dimension=0, tiled=True),
        lax.psum_scatter(grad_out, "dp", scatter_dimension=0, tiled=True),
        lax.psum_scatter(grad_out_shift, "dp", scatter_dimension=0, tiled=True),
        lax.psum_scatter(grad_up, "dp", scatter_dimension=0, tiled=True),
        lax.psum_scatter(grad_up_shift, "dp", scatter_dimension=0, tiled=True),
        lax.psum_scatter(grad_down, "dp", scatter_dimension=0, tiled=True),
        lax.psum_scatter(grad_down_shift, "dp", scatter_dimension=0, tiled=True),
        lax.psum_scatter(grad_gains, "dp", scatter_dimension=1, tiled=True),
        lax.psum_scatter(grad_shifts, "dp", scatter_dimension=1, tiled=True),
    )
    totals = (
        lax.psum(shares[0].astype(jnp.bfloat16), "blk").astype(jnp.float32),
        lax.psum(shares[1].astype(jnp.bfloat16), "blk").astype(jnp.float32),
        lax.psum(shares[2].astype(jnp.bfloat16), "blk").astype(jnp.float32),
        lax.psum(shares[3].astype(jnp.bfloat16), "blk").astype(jnp.float32),
        lax.psum(shares[4].astype(jnp.bfloat16), "blk").astype(jnp.float32),
        lax.psum(shares[5].astype(jnp.bfloat16), "blk").astype(jnp.float32),
        lax.psum(shares[6].astype(jnp.bfloat16), "blk").astype(jnp.float32),
        lax.psum(shares[7].astype(jnp.bfloat16), "blk").astype(jnp.float32),
        lax.psum(shares[8].astype(jnp.bfloat16), "blk").astype(jnp.float32),
        lax.psum(shares[9].astype(jnp.bfloat16), "blk").astype(jnp.float32),
    )
    return (result.astype(jnp.bfloat16)[None], grad_inputs[None]) + tuple(totals)


NZ = 4
NPOS = 512
LEN = 256
WIDTH = 1024
OWN = 512
HID = 2048
BF = jnp.bfloat16
F32 = jnp.float32
MESH = pl.DeviceIdType.MESH
MIB = 1 << 20
ROW_OUT, ROW_DOWN, ROW_GAIN, ROW_SHIFT = 3, 4, 5, 9
GATHER = (
    ("v", 0, "zyx"), ("o", 0, "zyx"), ("q", 0, "zyx"), ("q", 1, "xzy"),
    ("o", 1, "zyx"), ("q", 2, "zyx"), ("q", 3, "zxy"), ("u", 0, "yzx"),
    ("u", 1, "xzy"), ("u", 2, "zyx"), ("u", 3, "zxy"), ("d", 0, "zyx"),
    ("u", 4, "yzx"), ("u", 5, "zxy"), ("d", 1, "yzx"), ("d", 2, "zxy"),
    ("u", 6, "zxy"), ("d", 3, "xzy"), ("u", 7, "zxy"), ("d", 4, "yzx"),
    ("d", 5, "zyx"), ("d", 6, "yzx"), ("d", 7, "xzy"),
)
GATHER_STEPS = (
    (0, 0), (1, 0), (2, 0), (0, 1), (3, 0), (0, 2), (3, 1), (6, 0),
    (1, 1), (0, 3), (4, 0), (-1, 0), (2, 1), (5, 0), (-1, 1), (1, 2),
    (2, 2), (4, 1), (7, 0), (1, 3), (6, 1), (9, 0), (7, 1), (10, 0),
    (4, 2), (5, 1), (8, 0), (2, 3), (5, 2), (8, 1), (11, 0), (3, 2),
    (9, 1), (12, 0), (10, 1), (13, 0), (4, 3), (12, 1), (15, 0), (6, 2),
    (7, 2), (9, 2), (11, 1), (14, 0), (13, 1), (16, 0), (10, 2), (14, 1),
    (17, 0), (15, 1), (18, 0), (5, 3), (8, 2), (3, 3), (6, 3), (-1, 2),
    (-1, 3), (17, 1), (20, 0), (11, 2), (9, 3), (16, 1), (12, 2), (19, 0),
    (-1, 4), (10, 3), (13, 2), (18, 1), (21, 0), (-1, 5), (7, 3), (15, 2),
    (19, 1), (22, 0), (-1, 6), (14, 2), (20, 1), (21, 1), (8, 3), (-1, 7),
    (11, 3), (16, 2), (17, 2), (22, 1), (-1, 8), (13, 3), (18, 2), (15, 3),
    (19, 2), (-1, 9), (12, 3), (-1, 10), (-1, 11), (-1, 12), (-1, 13), (20, 2),
    (-1, 14), (21, 2), (-1, 15), (22, 2), (14, 3), (16, 3), (-1, 16), (18, 3),
    (-1, 17), (-1, 18), (17, 3), (-1, 19), (19, 3), (20, 3), (-1, 20), (22, 3),
    (21, 3), (-1, 21),
)
SCATTER = (
    ("d", 0, "yzx"), ("d", 1, "xzy"), ("d", 2, "yzx"), ("d", 3, "xzy"),
    ("d", 4, "xzy"), ("d", 5, "xzy"), ("u", 0, "yxz"), ("u", 1, "yxz"),
    ("u", 2, "yzx"), ("d", 6, "yxz"), ("d", 7, "yxz"), ("u", 3, "xzy"),
    ("o", 0, "yxz"), ("u", 4, "xyz"), ("q", 0, "xzy"), ("u", 5, "xyz"),
    ("o", 1, "yxz"), ("q", 1, "xyz"), ("u", 6, "yxz"), ("u", 7, "yxz"),
    ("q", 2, "xyz"), ("q", 3, "xyz"), ("q", 4, "yxz"), ("q", 5, "yxz"),
    ("v", 0, "xyz"),
)
SCATTER_STEPS = (
    (-1, 0), (0, 0), (1, 0), (2, 0), (3, 0), (-1, 1), (4, 0), (5, 0),
    (-1, 2), (-1, 3), (-1, 4), (6, 0), (7, 0), (-1, 5), (0, 1), (2, 1),
    (8, 0), (10, 0), (-1, 6), (-1, 7), (-1, 8), (1, 1), (3, 1), (9, 0),
    (11, 0), (4, 1), (5, 1), (13, 0), (-1, 9), (0, 2), (-1, 10), (2, 2),
    (0, 3), (6, 1), (7, 1), (11, 1), (12, 0), (15, 0), (19, 0), (-1, 11),
    (2, 3), (8, 1), (10, 1), (13, 1), (16, 0), (18, 0), (-1, 12), (9, 1),
    (-1, 13), (6, 2), (7, 2), (-1, 14), (1, 2), (-1, 15), (3, 2), (14, 0),
    (10, 2), (17, 0), (-1, 16), (4, 2), (9, 2), (5, 2), (15, 1), (21, 0),
    (-1, 17), (1, 3), (23, 0), (-1, 18), (3, 3), (13, 2), (-1, 19), (4, 3),
    (5, 3), (6, 3), (7, 3), (12, 1), (14, 1), (17, 1), (10, 3), (11, 2),
    (19, 1), (8, 2), (9, 3), (15, 2), (12, 2), (13, 3), (16, 1), (11, 3),
    (18, 1), (8, 3), (20, 0), (21, 1), (19, 2), (22, 0), (24, 0), (17, 2),
    (23, 1), (14, 2), (21, 2), (15, 3), (16, 2), (12, 3), (24, 1), (14, 3),
    (18, 2), (22, 1), (19, 3), (24, 2), (17, 3), (23, 2), (20, 1), (22, 2),
    (24, 3), (21, 3), (16, 3), (20, 2), (18, 3), (23, 3), (22, 3), (20, 3),
)


def dot_nn(a, b):
    return lax.dot_general(a, b, (((1,), (0,)), ((), ())), preferred_element_type=F32)


def dot_nt(a, b):
    return lax.dot_general(a, b, (((1,), (1,)), ((), ())), preferred_element_type=F32)


def dot_tn(a, b):
    return lax.dot_general(a, b, (((0,), (0,)), ((), ())), preferred_element_type=F32)


def loop(count, body):
    lax.fori_loop(0, count, lambda index, carry: (body(index), carry)[1], 0)


def mul(index, size):
    return pl.multiple_of(index * size, size)


class Net:
    def __init__(self, sems):
        self.chip = lax.axis_index("dp")
        self.core = lax.axis_index("blk")
        self.z = self.chip // 4
        self.y = (self.chip // 2) % 2
        self.x = self.chip % 2
        self.sems = sems
        self.used = 0
        self.unsent = []

    def sem(self):
        self.used += 1
        return self.sems.at[self.used - 1]

    def chip_at(self, z, y, x):
        return z * 4 + y * 2 + x

    def peers(self, dim):
        if dim == "x":
            return [(1, self.z, self.y, 1 - self.x, self.core)]
        if dim == "y":
            return [(1, self.z, 1 - self.y, self.x, self.core)]
        if dim == "c":
            return [(1, self.z, self.y, self.x, 1 - self.core)]
        return [(k, (self.z + k) % NZ, self.y, self.x, self.core) for k in range(1, NZ)]

    def send(self, src, dst, recv, peer):
        _, z, y, x, core = peer
        copy = pltpu.make_async_remote_copy(
            src_ref=src,
            dst_ref=dst,
            send_sem=self.sem(),
            recv_sem=recv,
            device_id=(self.chip_at(z, y, x), core),
            device_id_type=MESH,
        )
        copy.start()
        self.unsent.append(copy)
        return copy

    def drain(self, waited):
        for copy in self.unsent:
            if not any(copy is other for other in waited):
                copy.wait_send()

    def sibling(self, src, dst):
        return self.send(src, dst, self.sem(), self.peers("c")[0])

    def barrier(self):
        barrier = pltpu.get_barrier_semaphore()
        count = 0
        for dim in "xyzc":
            for _, z, y, x, core in self.peers(dim):
                pl.semaphore_signal(
                    barrier, inc=1, device_id=(self.chip_at(z, y, x), core), device_id_type=MESH
                )
                count += 1
        pl.semaphore_wait(barrier, count)


def await_bytes(view, sem):
    pltpu.make_async_copy(view, view, sem).wait()


def view_of(net, ref, lanes, **given):
    where = {"z": net.z, "y": net.y, "x": net.x}
    where.update(given)
    return ref.at[where["z"], where["y"], where["x"], :, lanes]


ALL = slice(None)


def gather_stages(net, ref, lanes, order):
    first, second, third = order
    others = {"z": pl.ds(0, NZ - 1), "y": 1 - net.y, "x": 1 - net.x}
    got_first, got_second, got_near, got_far = net.sem(), net.sem(), net.sem(), net.sem()

    def pass_on(dim, sem, **held):
        blocks = view_of(net, ref, lanes, **held)
        for peer in net.peers(dim):
            net.send(blocks, blocks, sem, peer)

    def start():
        pass_on(first, got_first)

    def after_first():
        await_bytes(view_of(net, ref, lanes, **{first: others[first]}), got_first)
        pass_on(second, got_second, **{first: ALL})
        pass_on(third, got_near, **{first: ALL})

    def after_second():
        held = {first: ALL, second: others[second]}
        await_bytes(view_of(net, ref, lanes, **held), got_second)
        if second == "z":
            for peer in net.peers("z"):
                pass_on(third, got_far, **{first: ALL, "z": peer[1]})
        else:
            pass_on(third, got_far, **held)

    def finish():
        held = {first: ALL, third: others[third]}
        await_bytes(view_of(net, ref, lanes, **held), got_near)
        held[second] = others[second]
        await_bytes(view_of(net, ref, lanes, **held), got_far)

    return start, after_first, after_second, finish


def scatter_stages(net, ref, lanes, order, bufs, done):
    first, second, third = order
    wide, half, line = bufs
    got_wide, got_half, got_line = net.sem(), net.sem(), net.sem()
    dtype = wide.dtype
    rows, cols = wide.shape[-2:]
    step = min(rows, max(16, 32768 // cols))
    size = {"z": NZ, "y": 2, "x": 2}
    place = {"z": 0, "y": 1, "x": 2}
    mine = {"z": net.z, "y": net.y, "x": net.x}

    def coordinate(dim, peer):
        return peer[1 + place[dim]]

    def block_add(target, sources):
        for part in range(rows // step):
            here = pl.ds(part * step, step)
            total = ref[(*target, here, lanes)].astype(F32)
            for buf, at in sources:
                total = total + buf[(*at, here)].astype(F32)
            ref[(*target, here, lanes)] = total.astype(dtype)

    def target_of(**given):
        where = dict(mine)
        where.update(given)
        return (where["z"], where["y"], where["x"])

    def start():
        for peer in net.peers(first):
            there = {"z": ALL, "y": ALL, "x": ALL, first: coordinate(first, peer)}
            net.send(view_of(net, ref, lanes, **there), wide.at[peer[0] - 1], got_wide, peer)

    def after_first():
        await_bytes(wide, got_wide)
        left = [dim for dim in "zyx" if dim != first]

        def add(second_at, third_at):
            at = {second: second_at, third: third_at}
            place_in = (0, at[left[0]], at[left[1]])
            block_add(target_of(**at), [(wide, place_in)])

        for peer in net.peers(second):
            gone = coordinate(second, peer)
            loop(size[third], lambda other: add(gone, other))
            blocks = view_of(net, ref, lanes, **{second: gone, third: ALL})
            net.send(blocks, half.at[peer[0] - 1], got_half, peer)
        loop(size[third], lambda other: add(mine[second], other))

    def after_second():
        await_bytes(half, got_half)
        for peer in net.peers(third):
            gone = coordinate(third, peer)
            block_add(
                target_of(**{third: gone}), [(half, (k, gone)) for k in range(size[second] - 1)]
            )
            blocks = view_of(net, ref, lanes, **{third: gone})
            net.send(blocks, line.at[peer[0] - 1], got_line, peer)

    def finish():
        await_bytes(line, got_line)
        for part in range(rows // step):
            here = pl.ds(part * step, step)
            total = ref[(*target_of(), here, lanes)].astype(F32)
            for k in range(size[second] - 1):
                total = total + half[k, mine[third], here].astype(F32)
            for k in range(size[third] - 1):
                total = total + line[k, here].astype(F32)
            done(part * step, step, total)

    return start, after_first, after_second, finish


def pieces_of(plan, widths):
    counts = {}
    for group, _, _ in plan:
        counts[group] = counts.get(group, 0) + 1
    return [
        (group, index * (widths[group] // counts[group]), widths[group] // counts[group], order)
        for group, index, order in plan
    ]


def layer_kernel(
    tok,
    doc,
    cot,
    wq_in,
    wo_in,
    wu_in,
    wd_in,
    qv_in,
    up_in,
    out_in,
    down_in,
    gain_in,
    shift_in,
    res_out,
    gtok_out,
    gq_out,
    go_out,
    gu_out,
    gd_out,
    gvec_out,
    wq,
    wo,
    wu,
    wd,
    vbuf,
    pack,
    vecs,
    vq,
    vu,
    xin,
    qb,
    kb,
    vb,
    pb,
    att,
    attb,
    attx,
    hat1,
    hat2,
    inv1,
    inv2,
    mid,
    fin,
    act,
    dge,
    rcv,
    own,
    snd,
    gff,
    gbr,
    dob,
    dsb,
    gu,
    gd,
    swap,
    acc,
    acc_qv,
    acc_up,
    gvecs,
    gv,
    vother,
    piece_bufs,
    st_q,
    st_o,
    st_u,
    st_d,
    sems,
    local_sems,
):
    net = Net(sems)
    core = net.core
    me = (net.z, net.y, net.x)

    locals_ = []

    def fetch(src, dst):
        copy = pltpu.make_async_copy(src, dst, local_sems.at[len(locals_)])
        copy.start()
        locals_.append(copy)

    def lanes_of(start, size):
        return pl.ds(pl.multiple_of(start, 128), size)

    for part in range(3):
        fetch(
            wq_in.at[:, lanes_of(part * WIDTH + core * OWN, OWN)],
            wq.at[net.z, net.y, net.x, :, pl.ds(part * OWN, OWN)],
        )
    fetch(wo_in.at[:, lanes_of(core * OWN, OWN)], wo.at[core, net.z, net.y, net.x])
    for i in range(NZ * 4):
        fetch(
            wu_in.at[:, lanes_of(i * 256 + core * 128, 128)],
            wu.at[net.z, net.y, net.x, :, pl.ds(i * 128, 128)],
        )
    fetch(wd_in.at[pl.ds(mul(core, 128), 128), :], wd.at[net.z, net.y, net.x])
    pack[...] = jnp.zeros_like(pack)
    pack[0:1, :] = qv_in[...].astype(F32)
    pack[1:3, :] = up_in[...].astype(F32)
    for row, ref in (
        (ROW_OUT, out_in),
        (ROW_DOWN, down_in),
        (ROW_GAIN, gain_in),
        (ROW_SHIFT, shift_in),
    ):
        value = ref[...].astype(F32)
        rows = slice(row, row + value.shape[0])
        pack[rows, 0:64] = jnp.where(net.x == 0, value, 0.0)
        pack[rows, 64:128] = jnp.where(net.x == 1, value, 0.0)
    vbuf[net.z, net.y, net.x] = pack[...].astype(BF)
    wo_own = wo.at[core]
    plan = pieces_of(GATHER, {"v": 128, "q": 3 * OWN, "o": OWN, "u": HID, "d": WIDTH})
    sources = {"v": vbuf, "q": wq, "o": wo_own, "u": wu, "d": wd}
    gathers = [
        gather_stages(net, sources[group], pl.ds(lane0, count), order)
        for group, lane0, count, order in plan
    ]
    net.barrier()
    ready = {"v": 0, "q": 3, "o": 4, "u": 20, "d": 21}
    state = {"landed": 0}

    def gather(piece, stage):
        if stage == 0:
            while state["landed"] < ready[plan[piece][0]]:
                locals_[state["landed"]].wait()
                state["landed"] += 1
        gathers[piece][stage]()

    def spread_vectors():
        for z in range(NZ):
            for y in range(2):
                both = vbuf[z, y, 0].astype(F32) + vbuf[z, y, 1].astype(F32)
                vecs[:, pl.ds((z * 2 + y) * 128, 128)] = both
        for y in range(2):
            for x in range(2):
                at = pl.ds((y * 2 + x) * 128, 128)
                vq[0:8, at] = vbuf[core, y, x].astype(F32)[0:8]
                vq[8:16, at] = vbuf[core + 2, y, x].astype(F32)[0:8]
                for z in range(NZ):
                    block = vbuf[z, y, x].astype(F32)
                    vu[0:1, pl.ds((z * 4 + y * 2 + x) * 128, 128)] = jnp.where(
                        core == 0, block[1:2], block[2:3]
                    )
        acc[...] = jnp.zeros_like(acc)
        acc_up[...] = jnp.zeros_like(acc_up)

    def gain(n):
        return vecs[ROW_GAIN + n : ROW_GAIN + n + 1, :]

    def shift(n):
        return vecs[ROW_SHIFT + n : ROW_SHIFT + n + 1, :]

    def accumulate(row, value):
        parts = value.reshape(value.shape[0] // 8, 8, value.shape[1])
        acc[row] += jnp.sum(parts, axis=0)

    got = {}

    chunk = 32
    chunks = LEN // chunk

    def ln0(i):
        here = pl.ds(mul(i, chunk), chunk)
        hat, _ = normalize(tok[here, :].astype(F32))
        xin[core, here, :] = (hat * gain(0) + shift(0)).astype(BF)

    def attention_input():
        loop(chunks, ln0)
        got["x"] = net.sibling(xin.at[core], xin.at[core])

    ends = []
    end = jnp.int32(0)
    for j in range(8):
        end = end + doc[0, j]
        ends.append(end)

    def segment(position):
        total = jnp.zeros(position.shape, jnp.int32)
        for value in ends:
            total = total + (position >= value).astype(jnp.int32)
        return total

    scale = 1.0 / (ALPHA * 8.0)

    def project(t):
        n = t // 2
        m = t % 2
        tile = pl.ds(mul(n, 256), 256)
        rows = pl.ds(mul(m, 256), 256)

        def part(index, dst, bias, factor):
            weight = wq[:, :, :, :, pl.ds(pl.multiple_of(index * OWN + n * 256, 256), 256)]
            value = dot_nn(xin[m], weight.reshape(WIDTH, 256))
            if bias is not None:
                value = value + vq[bias : bias + 1, tile]
            if factor is not None:
                value = value * factor
            dst[rows, tile] = value.astype(BF)

        part(0, qb, 0, scale)
        part(1, kb, None, None)
        part(2, vb, 8, None)

    def projections():
        got["x"].wait_recv()
        loop(4, project)

    lane = lax.broadcasted_iota(jnp.int32, (1, 128), 1)
    block = 128

    def attend(pair):
        at = pl.ds(mul(pair, 128), 128)
        for r in range(NPOS // block):
            rows = pl.ds(r * block, block)
            count = (r + 1) * block
            q_pos = r * block + lax.broadcasted_iota(jnp.int32, (block, 1), 0)
            k_pos = lax.broadcasted_iota(jnp.int32, (1, count), 1)
            allowed = (segment(q_pos) == segment(k_pos)) & (k_pos <= q_pos)
            q = qb[rows, at]
            k = kb[0:count, at]
            v = vb[0:count, at]
            outs = []
            for head in range(2):
                mine = (lane < 64) if head == 0 else (lane >= 64)
                scores = dot_nt(jnp.where(mine, q, jnp.zeros_like(q)), k)
                scores = jnp.where(allowed, scores, FILLER)
                top = jnp.max(scores, axis=1, keepdims=True)
                weights = jnp.exp(ALPHA * (scores - top))
                probs = weights * (1.0 / jnp.sum(weights, axis=1, keepdims=True))
                probs = probs.astype(BF)
                pb[pair * 2 + head, rows, 0:count] = probs
                outs.append(dot_nn(probs, v))
            out = jnp.where(lane < 64, outs[0], outs[1])
            att[rows, at] = out
            attb[rows, at] = out.astype(BF)

    other_rows = pl.ds(mul(1 - core, LEN), LEN)
    own_rows = pl.ds(mul(core, LEN), LEN)

    def attend_last():
        attend(3)
        got["att"] = net.sibling(attb.at[other_rows, :], attx)

    def branch_tile(n):
        lanes = pl.ds(mul(n % 2, 256), 256)
        mine = wo[n // 2, pl.ds(2 * core, 2), :, :, :, lanes].reshape(OWN, 256)
        theirs = wo[n // 2, pl.ds(2 * (1 - core), 2), :, :, :, lanes].reshape(OWN, 256)
        at = pl.ds(mul(n, 256), 256)
        own[:, at] = dot_nn(attb[own_rows, :], mine) + dot_nn(attx[...], theirs)

    def branch_all():
        got["wo"] = net.sibling(wo_own, wo.at[core])
        got["att"].wait_recv()
        loop(2, lambda i: branch_tile(core * 2 + i))
        got["wo"].wait_recv()
        loop(2, lambda i: branch_tile((1 - core) * 2 + i))

    def ln12(i):
        here = pl.ds(mul(i, chunk), chunk)
        first, first_inv = normalize(own[here, :] + vecs[ROW_OUT : ROW_OUT + 1, :])
        hat1[here, :] = first
        inv1[here, :] = jnp.broadcast_to(first_inv, (chunk, 128))
        middle = tok[here, :].astype(F32) + first * gain(1) + shift(1)
        mid[here, :] = middle
        second, second_inv = normalize(middle)
        hat2[here, :] = second
        inv2[here, :] = jnp.broadcast_to(second_inv, (chunk, 128))
        fin[core, here, :] = (second * gain(2) + shift(2)).astype(BF)

    def norms_12():
        loop(chunks, ln12)
        got["fin"] = net.sibling(fin.at[core], fin.at[core])

    root = math.sqrt(2.0 / math.pi)

    def up_tile(t):
        n = t // 2
        m = t % 2
        at = pl.ds(mul(n, 256), 256)
        rows = pl.ds(mul(m, 256), 256)
        weight = wu[:, :, :, :, at].reshape(WIDTH, 256)
        u = dot_nn(fin[m], weight) + vu[0:1, at]
        square = u * u
        inner = jnp.tanh(root * (u + 0.044715 * (square * u)))
        half = 0.5 * (1.0 + inner)
        act[rows, at] = (u * half).astype(BF)
        slope = 0.5 * u * (1.0 - inner * inner) * (root * (1.0 + (3 * 0.044715) * square))
        dge[rows, at] = (half + slope).astype(BF)

    def up_piece(lane0, count):
        tiles = 2 * count // 256
        loop(tiles, lambda i: up_tile(i + 2 * lane0 // 256))

    got_parts = []

    def down_piece(lane0, count):
        at = pl.ds(lane0, count)
        weight = wd[:, :, :, :, at].reshape(HID, count)
        snd[:, at] = dot_nn(act[other_rows, :], weight)
        got_parts.append(net.sibling(snd.at[:, at], rcv.at[:, at]))
        own[:, at] = dot_nn(act[own_rows, :], weight)

    def tiles_of(width, count, body):
        return [functools.partial(body, lane0, count) for lane0 in range(0, width, count)]

    steps = [
        spread_vectors,
        attention_input,
        projections,
        lambda: loop(1, attend),
        lambda: loop(1, lambda i: attend(i + 1)),
        lambda: loop(1, lambda i: attend(i + 2)),
        attend_last,
        branch_all,
        norms_12,
        lambda: got["fin"].wait_recv(),
    ]
    steps += tiles_of(HID, 256, up_piece) + tiles_of(WIDTH, 256, down_piece)
    for piece, stage in GATHER_STEPS:
        if piece < 0:
            steps[stage]()
        else:
            gather(piece, stage)
    for part in got_parts:
        part.wait_recv()

    filled = ends[-1]

    def upstream_of(i):
        here = pl.ds(mul(i, chunk), chunk)
        position = core * LEN + i * chunk + lax.broadcasted_iota(jnp.int32, (chunk, 1), 0)
        return cot[here, :].astype(F32) * (position < filled).astype(F32)

    def top_tile(i):
        here = pl.ds(mul(i, chunk), chunk)
        value = own[here, :] + rcv[here, :] + vecs[ROW_DOWN : ROW_DOWN + 1, :]
        hat, inv = normalize(value)
        res_out[here, :] = (mid[here, :] + hat * gain(3) + shift(3)).astype(BF)
        upstream = upstream_of(i)
        grad = norm_back(hat, inv, gain(3), upstream).astype(BF)
        gff[core, here, :] = grad
        accumulate(ROW_GAIN + 3, upstream * hat)
        accumulate(ROW_SHIFT + 3, upstream)
        accumulate(ROW_DOWN, grad.astype(F32))

    parts = 2
    got_gff = []
    for part in range(parts):
        loop(chunks // parts, lambda i: top_tile(i + part * (chunks // parts)))
        rows = pl.ds(part * (LEN // parts), LEN // parts)
        got_gff.append(net.sibling(gff.at[core, rows], gff.at[core, rows]))

    out_copies = []

    def deliver(src, dst):
        copy = pltpu.make_async_copy(src, dst, local_sems.at[21 + len(out_copies)])
        copy.start()
        out_copies.append((copy, net.sibling(src, dst)))

    def ship(group, lane0, count):
        if group == "d":
            at = pl.ds(lane0, count)
            deliver(st_d.at[:, at], gd_out.at[pl.ds(mul(core, 128), 128), at])
        if group == "u":
            for i in range(lane0 // 128, (lane0 + count) // 128):
                deliver(
                    st_u.at[:, pl.ds(i * 128, 128)],
                    gu_out.at[:, lanes_of(i * 256 + core * 128, 128)],
                )
        if group == "o":
            deliver(
                st_o.at[:, pl.ds(lane0, count)], go_out.at[:, lanes_of(core * OWN + lane0, count)]
            )
        if group == "q":
            start = (lane0 // OWN) * WIDTH + lane0 % OWN
            deliver(
                st_q.at[:, pl.ds(lane0, count)], gq_out.at[:, lanes_of(core * OWN + start, count)]
            )

    plan = pieces_of(SCATTER, {"d": WIDTH, "u": HID, "o": OWN, "q": 3 * OWN, "v": 128})
    sums = {"d": gd, "u": gu, "o": wu, "q": wu, "v": gv}
    stage_of = {"d": st_d, "u": st_u, "o": st_o, "q": st_q, "v": gvec_out}

    def store_to(stage, lane0, count):
        def done(row0, size, total):
            stage[row0 : row0 + size, lane0 : lane0 + count] = total

        return done

    scatters = []
    for (group, lane0, count, order), bufs in zip(plan, piece_bufs, strict=True):
        base = 3 * OWN if group == "o" else 0
        scatters.append(
            scatter_stages(
                net,
                sums[group],
                pl.ds(base + lane0, count),
                order,
                bufs,
                store_to(stage_of[group], lane0, count),
            )
        )

    def scatter(piece, stage):
        scatters[piece][stage]()
        if stage == 3:
            ship(*plan[piece][:3])

    for part in got_gff:
        part.wait_recv()

    def gdown_piece(lane0, count):
        at = pl.ds(lane0, count)

        def tile(k):
            left = act[:, pl.ds(mul(k, 256), 256)]
            grad = gff[:, :, at].reshape(NPOS, count)
            gd[k // 2, k % 2, :, :, at] = dot_tn(left, grad).astype(BF).reshape(2, 128, count)

        loop(8, tile)

    def gpre_tile(t):
        k = t // 2
        m = t % 2
        at = pl.ds(mul(k, 256), 256)
        rows = pl.ds(mul(m, 256), 256)
        weight = wd[k // 2, k % 2].reshape(256, WIDTH)
        value = dot_nt(gff[m], weight) * dge[rows, at].astype(F32)
        value = value.astype(BF)
        dge[rows, at] = value
        acc_up[:, at] += jnp.sum(value.astype(F32).reshape(32, 8, 256), axis=0)

    def gup_piece(lane0, count):
        at = pl.ds(lane0, count)

        def tile(z):
            left = fin[:, :, pl.ds(mul(z, 256), 256)].reshape(NPOS, 256)
            gu[z, :, :, :, at] = dot_tn(left, dge[:, at]).astype(BF).reshape(2, 2, 64, count)

        loop(NZ, tile)

    def gfi_tile(rows, dst):
        def body(z):
            weight = wu[z].reshape(256, HID)
            dst[:, pl.ds(mul(z, 256), 256)] = dot_nt(dge[rows, :], weight)

        loop(NZ, body)

    def grad_ffn_in():
        for part in got_parts:
            part.wait_send()
        gfi_tile(other_rows, snd)
        got["gfi"] = net.sibling(snd, rcv)
        gfi_tile(own_rows, own)

    def middle_tile(i):
        here = pl.ds(mul(i, chunk), chunk)
        grad_in = own[here, :] + rcv[here, :]
        second = hat2[here, :]
        accumulate(ROW_GAIN + 2, grad_in * second)
        accumulate(ROW_SHIFT + 2, grad_in)
        grad_mid = upstream_of(i) + norm_back(second, inv2[here, 0:1], gain(2), grad_in)
        mid[here, :] = grad_mid
        first = hat1[here, :]
        accumulate(ROW_GAIN + 1, grad_mid * first)
        accumulate(ROW_SHIFT + 1, grad_mid)
        grad = norm_back(first, inv1[here, 0:1], gain(1), grad_mid).astype(BF)
        gbr[core, here, :] = grad
        accumulate(ROW_OUT, grad.astype(F32))

    def grad_middle():
        got["gfi"].wait_recv()
        loop(chunks, middle_tile)
        for copy in forward_sends:
            copy.wait_send()
        got["gbr"] = net.sibling(gbr.at[core], gbr.at[core])

    go = wu.at[:, :, :, :, pl.ds(3 * OWN, OWN)]

    def gout_tile(k, cols, put):
        left = attb[:, pl.ds(mul(k, 256), 256)]
        grad = gbr[:, :, cols].reshape(NPOS, OWN)
        put(k, dot_tn(left, grad).astype(BF).reshape(2, 2, 64, OWN))

    def put_swap(k, value):
        swap[k] = value

    def put_own(k, value):
        wu[2 * core + k, :, :, :, pl.ds(3 * OWN, OWN)] = value


    def gatt_tile(t):
        k = t // 2
        m = t % 2
        left = wo[0, 2 * core + k].reshape(256, OWN)
        right = wo[1, 2 * core + k].reshape(256, OWN)
        value = dot_nt(gbr[m, :, 0:OWN], left) + dot_nt(gbr[m, :, OWN:WIDTH], right)
        dob[pl.ds(mul(m, 256), 256), pl.ds(mul(k, 256), 256)] = value.astype(BF)

    def grad_out():
        got["gbr"].wait_recv()
        loop(2, lambda k: gout_tile(k, lanes_of((1 - core) * OWN, OWN), put_swap))
        got_swap = net.sibling(swap, go.at[pl.ds(2 * core, 2)])
        loop(2, lambda k: gout_tile(k, lanes_of(core * OWN, OWN), put_own))
        loop(4, gatt_tile)
        got_swap.wait_recv()

    def attend_back(pair):
        at = pl.ds(mul(pair, 128), 128)
        sums = []
        for head in range(2):
            mine = (lane < 64) if head == 0 else (lane >= 64)
            queries_ = []
            for r in range(NPOS // block):
                rows = pl.ds(r * block, block)
                count = (r + 1) * block
                grad = dob[rows, at]
                grad = jnp.where(mine, grad, jnp.zeros_like(grad))
                delta = jnp.sum(grad.astype(F32) * att[rows, at], axis=1, keepdims=True)
                probs = pb[pair * 2 + head, rows, 0:count].astype(F32)
                grad_probs = dot_nt(grad, vb[0:count, at])
                scores = (ALPHA * probs * (grad_probs - delta)).astype(BF)
                dsb[rows, 0:count] = scores
                queries_.append(dot_nn(scores, kb[0:count, at]))
            keys_, values_ = [], []
            for r in range(NPOS // block):
                rows = pl.ds(r * block, NPOS - r * block)
                cols = pl.ds(r * block, block)
                keys_.append(dot_tn(dsb[rows, cols], qb[rows, at]))
                values_.append(dot_tn(pb[pair * 2 + head, rows, cols], dob[rows, at]))
            sums.append((queries_, keys_, values_))
        total_q = jnp.zeros((8, 128), F32)
        total_v = jnp.zeros((8, 128), F32)
        for r in range(NPOS // block):
            rows = pl.ds(r * block, block)
            merged = [
                jnp.where(lane < 64, sums[0][i][r], sums[1][i][r]).astype(BF) for i in range(3)
            ]
            grad_q = merged[0] * jnp.asarray(scale, BF)
            qb[rows, at] = grad_q
            kb[rows, at] = merged[1]
            vb[rows, at] = merged[2]
            total_q += jnp.sum(grad_q.astype(F32).reshape(block // 8, 8, 128), axis=0)
            total_v += jnp.sum(merged[2].astype(F32).reshape(block // 8, 8, 128), axis=0)
        acc_qv[0, :, at] = total_q
        acc_qv[1, :, at] = total_v

    def gqkv_piece(lane0, count):
        ref = (qb, kb, vb)[lane0 // OWN]

        def tile(z):
            left = xin[:, :, pl.ds(mul(z, 256), 256)].reshape(NPOS, 256)
            value = dot_tn(left, ref[:, lane0 % OWN : lane0 % OWN + count]).astype(BF)
            wu[z, :, :, :, pl.ds(lane0, count)] = value.reshape(2, 2, 64, count)

        loop(NZ, tile)

    def gai_tile(rows, dst):
        def body(z):
            value = None
            for part, ref in enumerate((qb, kb, vb)):
                weight = wq[z, :, :, :, pl.ds(part * OWN, OWN)].reshape(256, OWN)
                term = dot_nt(ref[rows, :], weight)
                value = term if value is None else value + term
            dst[:, pl.ds(mul(z, 256), 256)] = value

        loop(NZ, body)

    def grad_attn_in():
        got["gfi"].wait_send()
        gai_tile(other_rows, snd)
        got["gai"] = net.sibling(snd, rcv)
        gai_tile(own_rows, own)

    def bottom_tile(i):
        here = pl.ds(mul(i, chunk), chunk)
        hat, inv = normalize(tok[here, :].astype(F32))
        grad_in = own[here, :] + rcv[here, :]
        accumulate(ROW_GAIN, grad_in * hat)
        accumulate(ROW_SHIFT, grad_in)
        gtok_out[here, :] = mid[here, :] + norm_back(hat, inv, gain(0), grad_in)

    def bottom():
        got["gai"].wait_recv()
        loop(chunks, bottom_tile)
        for row in range(16):
            gvecs[row : row + 1, :] = jnp.sum(acc[row], axis=0, keepdims=True)
        row_id = lax.broadcasted_iota(jnp.int32, (16, 1), 0)
        for z in range(NZ):
            for y in range(2):
                base = gvecs[:, pl.ds((z * 2 + y) * 128, 128)]
                for x in range(2):
                    at = pl.ds((y * 2 + x) * 128, 128)
                    kind = 0 if z < 2 else 1
                    qv_row = jnp.sum(acc_qv[kind, :, at], axis=0, keepdims=True)
                    qv_row = jnp.where(core == z % 2, qv_row, 0.0)
                    up_at = pl.ds((z * 4 + y * 2 + x) * 128, 128)
                    up_row = jnp.sum(acc_up[:, up_at], axis=0, keepdims=True)
                    value = base + jnp.where(row_id == 0, qv_row, 0.0)
                    gv[z, y, x] = value + jnp.where(row_id == 1 + core, up_row, 0.0)

    steps = tiles_of(WIDTH, 512, gdown_piece)
    steps += [
        lambda: loop(8, gpre_tile),
        lambda: loop(8, lambda i: gpre_tile(i + 8)),
    ]
    steps += tiles_of(HID, 512, gup_piece)
    steps += [grad_ffn_in, grad_middle, grad_out]
    steps += [functools.partial(loop, 1, lambda i, pair=p: attend_back(i + pair)) for p in range(4)]
    steps += tiles_of(3 * OWN, 512, gqkv_piece)
    steps += [grad_attn_in, bottom]
    forward_sends = [
        copy for copy in net.unsent if not any(copy is part for part in got_parts)
    ]
    net.unsent = []
    for piece, stage in SCATTER_STEPS:
        if piece < 0:
            steps[stage]()
        else:
            scatter(piece, stage)
    got_vec = net.sibling(gvec_out, vother)
    got_vec.wait_send()
    got_vec.wait_recv()
    gvec_out[...] = gvec_out[...] + vother[...]
    for copy, remote in out_copies:
        copy.wait()
        remote.wait_recv()
    net.drain((got["gfi"], got_vec))


def scatter_bufs(group, count, order):
    rows, dtype = {"d": (128, BF), "v": (16, F32)}.get(group, (64, BF))
    size = {"z": NZ, "y": 2, "x": 2}
    left = [size[dim] for dim in "zyx" if dim != order[0]]
    return [
        pltpu.VMEM((size[order[0]] - 1, *left, rows, count), dtype),
        pltpu.VMEM((size[order[1]] - 1, size[order[2]], rows, count), dtype),
        pltpu.VMEM((size[order[2]] - 1, rows, count), dtype),
    ]


SPLIT = 4


def hand_out_kernel(*refs):
    large, vec = refs[:6], refs[6]
    outs, small, held, sems = refs[7:13], refs[13:19], refs[19:25], refs[25]
    arrivals, copies = [], []
    for src, mid, dst in zip(large, held, outs, strict=True):
        rows = src.shape[0] // SPLIT
        for part in range(SPLIT):
            here = pl.ds(part * rows, rows)
            at = len(arrivals)
            arrivals.append(pltpu.make_async_copy(src.at[here], mid.at[here], sems.at[0, at]))
            copies.append(pltpu.make_async_copy(mid.at[here], dst.at[here], sems.at[1, at]))
            arrivals[-1].start()
    right = lax.axis_index("dp") % 2 == 1
    values = vec[...]
    half = jnp.where(right, values[:, 64:], values[:, :64])
    small[0][...] = values[0:1]
    small[1][...] = half[ROW_OUT : ROW_OUT + 1]
    small[2][...] = values[1:3]
    small[3][...] = half[ROW_DOWN : ROW_DOWN + 1]
    small[4][...] = half[ROW_GAIN : ROW_GAIN + 4]
    small[5][...] = half[ROW_SHIFT : ROW_SHIFT + 4]
    for arrival, copy in zip(arrivals, copies, strict=True):
        arrival.wait()
        copy.start()
    for copy in copies:
        copy.wait()


def fused(
    tokens,
    doc_lengths,
    cotangent,
    w_qkv,
    qv_bias,
    w_out,
    out_bias,
    w_up,
    up_bias,
    w_down,
    down_bias,
    norm_gain,
    norm_bias,
):
    vmem = pl.BlockSpec(memory_space=pltpu.VMEM)
    anywhere = pl.BlockSpec(memory_space=pl.ANY)
    scratch = [
        pltpu.VMEM((NZ, 2, 2, 64, 3 * OWN), BF),
        pltpu.VMEM((2, NZ, 2, 2, 64, OWN), BF),
        pltpu.VMEM((NZ, 2, 2, 64, HID), BF),
        pltpu.VMEM((NZ, 2, 2, 128, WIDTH), BF),
        pltpu.VMEM((NZ, 2, 2, 16, 128), BF),
        pltpu.VMEM((16, 128), F32),
        pltpu.VMEM((16, WIDTH), F32),
        pltpu.VMEM((16, OWN), F32),
        pltpu.VMEM((8, HID), F32),
        pltpu.VMEM((2, LEN, WIDTH), BF),
        pltpu.VMEM((NPOS, OWN), BF),
        pltpu.VMEM((NPOS, OWN), BF),
        pltpu.VMEM((NPOS, OWN), BF),
        pltpu.VMEM((8, NPOS, NPOS), BF),
        pltpu.VMEM((NPOS, OWN), F32),
        pltpu.VMEM((NPOS, OWN), BF),
        pltpu.VMEM((LEN, OWN), BF),
        pltpu.VMEM((LEN, WIDTH), F32),
        pltpu.VMEM((LEN, WIDTH), F32),
        pltpu.VMEM((LEN, 128), F32),
        pltpu.VMEM((LEN, 128), F32),
        pltpu.VMEM((LEN, WIDTH), F32),
        pltpu.VMEM((2, LEN, WIDTH), BF),
        pltpu.VMEM((NPOS, HID), BF),
        pltpu.VMEM((NPOS, HID), BF),
        pltpu.VMEM((LEN, WIDTH), F32),
        pltpu.VMEM((LEN, WIDTH), F32),
        pltpu.VMEM((LEN, WIDTH), F32),
        pltpu.VMEM((2, LEN, WIDTH), BF),
        pltpu.VMEM((2, LEN, WIDTH), BF),
        pltpu.VMEM((NPOS, OWN), BF),
        pltpu.VMEM((NPOS, NPOS), BF),
        pltpu.VMEM((NZ, 2, 2, 64, HID), BF),
        pltpu.VMEM((NZ, 2, 2, 128, WIDTH), BF),
        pltpu.VMEM((2, 2, 2, 64, OWN), BF),
        pltpu.VMEM((16, 8, WIDTH), F32),
        pltpu.VMEM((2, 8, OWN), F32),
        pltpu.VMEM((8, HID), F32),
        pltpu.VMEM((16, WIDTH), F32),
        pltpu.VMEM((NZ, 2, 2, 16, 128), F32),
        pltpu.VMEM((16, 128), F32),
        [
            scatter_bufs(group, count, order)
            for group, _, count, order in pieces_of(
                SCATTER, {"d": WIDTH, "u": HID, "o": OWN, "q": 3 * OWN, "v": 128}
            )
        ],
        pltpu.VMEM((64, 3 * OWN), F32),
        pltpu.VMEM((64, OWN), F32),
        pltpu.VMEM((64, HID), F32),
        pltpu.VMEM((128, WIDTH), F32),
        pltpu.SemaphoreType.DMA((700,)),
        pltpu.SemaphoreType.DMA((80,)),
    ]
    outs = pl.pallas_call(
        layer_kernel,
        out_shape=[
            jax.ShapeDtypeStruct((LEN, WIDTH), BF),
            jax.ShapeDtypeStruct((LEN, WIDTH), F32),
            jax.ShapeDtypeStruct((64, 3 * WIDTH), F32),
            jax.ShapeDtypeStruct((64, WIDTH), F32),
            jax.ShapeDtypeStruct((64, 2 * HID), F32),
            jax.ShapeDtypeStruct((256, WIDTH), F32),
            jax.ShapeDtypeStruct((16, 128), F32),
        ],
        in_specs=[vmem, pl.BlockSpec(memory_space=pltpu.SMEM), vmem]
        + [anywhere] * 4
        + [vmem] * 6,
        out_specs=[vmem, vmem] + [anywhere] * 4 + [vmem],
        scratch_shapes=scratch,
        compiler_params=pltpu.CompilerParams(
            collective_id=0, has_side_effects=True, vmem_limit_bytes=63 * MIB
        ),
        name="layer",
    )(
        tokens[0],
        doc_lengths,
        cotangent[0],
        w_qkv,
        w_out,
        w_up,
        w_down,
        qv_bias.reshape(1, 128),
        up_bias.reshape(2, 128),
        out_bias.reshape(1, 64),
        down_bias.reshape(1, 64),
        norm_gain,
        norm_bias,
    )
    *large, vec = outs
    done = pl.pallas_call(
        hand_out_kernel,
        out_shape=[jax.ShapeDtypeStruct(array.shape, array.dtype) for array in large]
        + [
            jax.ShapeDtypeStruct((1, 128), F32),
            jax.ShapeDtypeStruct((1, 64), F32),
            jax.ShapeDtypeStruct((2, 128), F32),
            jax.ShapeDtypeStruct((1, 64), F32),
            jax.ShapeDtypeStruct((4, 64), F32),
            jax.ShapeDtypeStruct((4, 64), F32),
        ],
        in_specs=[anywhere] * 6 + [vmem],
        out_specs=[anywhere] * 6 + [vmem] * 6,
        scratch_shapes=[pltpu.VMEM(array.shape, array.dtype) for array in large]
        + [pltpu.SemaphoreType.DMA((2, 6 * SPLIT))],
        name="hand_out",
    )(*large, vec)
    result, grad_inputs, grad_qkv, grad_out, grad_up, grad_down = done[:6]
    grad_qv, grad_out_shift, grad_up_shift, grad_down_shift, grad_gain, grad_shift = done[6:]
    return (
        result[None],
        grad_inputs[None],
        grad_qkv,
        grad_qv.reshape(128),
        grad_out,
        grad_out_shift.reshape(64),
        grad_up,
        grad_up_shift.reshape(256),
        grad_down,
        grad_down_shift.reshape(64),
        grad_gain,
        grad_shift,
    )


def solution(mesh):
    placed = (
        P("dp", "blk", None),
        P("dp", None),
        P("dp", "blk", None),
        P("dp", None),
        P("dp"),
        P("dp", None),
        P("dp"),
        P("dp", None),
        P("dp"),
        P("dp", None),
        P("dp"),
        P(None, "dp"),
        P(None, "dp"),
    )
    sizes = (mesh.shape["dp"], mesh.shape["blk"])
    return jax.shard_map(
        fused if sizes == (NZ * 4, 2) else shards,
        mesh=mesh,
        in_specs=placed,
        out_specs=(
            P("dp", "blk", None),
            P("dp", "blk", None),
            P("dp", None),
            P("dp"),
            P("dp", None),
            P("dp"),
            P("dp", None),
            P("dp"),
            P("dp", None),
            P("dp"),
            P(None, "dp"),
            P(None, "dp"),
        ),
        check_vma=False,
    )
```

```python
import functools
import math

import jax
import jax.numpy as jnp
from jax import lax
from jax.experimental import pallas as pl
from jax.experimental.pallas import tpu as pltpu
from jax.sharding import PartitionSpec as P

HEADS = 16
ALPHA = 32


EPSILON = 1e-05
FILLER = -1000000000.0


def normalize(values):
    center = values - jnp.mean(values, axis=-1, keepdims=True)
    inverse = lax.rsqrt(jnp.mean(center * center, axis=-1, keepdims=True) + EPSILON)
    return (center * inverse, inverse)


def norm_back(normed, inverse, gain_row, upstream):
    scaled = upstream * gain_row
    return inverse * (
        scaled
        - jnp.mean(scaled, axis=-1, keepdims=True)
        - normed * jnp.mean(scaled * normed, axis=-1, keepdims=True)
    )


def segment_of(position, doc_ends):
    return jnp.sum((position[:, None] >= doc_ends[None, :]).astype(jnp.int32), axis=1)


def gelu_tanh(values):
    return jax.nn.gelu(values, approximate=True)


def shards(
    tokens,
    doc_lengths,
    cotangent,
    w_qkv,
    qv_bias,
    w_out,
    out_bias,
    w_up,
    up_bias,
    w_down,
    down_bias,
    norm_gain,
    norm_bias,
):
    inputs = tokens[0].astype(jnp.float32)
    length = inputs.shape[0]
    model_width = inputs.shape[1]
    block_count = lax.axis_size("blk")
    seq_len = length * block_count
    offset = lax.axis_index("blk") * length
    doc_ends = jnp.cumsum(doc_lengths[0])
    filled = doc_ends[-1]
    query_pos = offset + jnp.arange(length, dtype=jnp.int32)
    query_seg = segment_of(query_pos, doc_ends)
    valid_rows = (query_pos < filled).astype(jnp.float32)
    key_seg = segment_of(jnp.arange(seq_len, dtype=jnp.int32), doc_ends)
    last_query = offset + length - 1

    def block_meets(first_row, piece_rows):
        first_at = jnp.asarray(first_row, jnp.int32)
        first_seg = lax.dynamic_index_in_dim(key_seg, first_at, keepdims=False)
        last_seg = lax.dynamic_index_in_dim(key_seg, first_at + piece_rows - 1, keepdims=False)
        return (first_at <= last_query) & (first_seg <= query_seg[-1]) & (last_seg >= query_seg[0])

    gathered = (
        lax.all_gather(w_qkv, "dp", axis=0, tiled=True),
        lax.all_gather(qv_bias, "dp", axis=0, tiled=True),
        lax.all_gather(w_out, "dp", axis=0, tiled=True),
        lax.all_gather(out_bias, "dp", axis=0, tiled=True),
        lax.all_gather(w_up, "dp", axis=0, tiled=True),
        lax.all_gather(up_bias, "dp", axis=0, tiled=True),
        lax.all_gather(w_down, "dp", axis=0, tiled=True),
        lax.all_gather(down_bias, "dp", axis=0, tiled=True),
        lax.all_gather(norm_gain, "dp", axis=1, tiled=True),
        lax.all_gather(norm_bias, "dp", axis=1, tiled=True),
    )
    (
        qkv_weight,
        qv_shift,
        out_weight,
        out_shift,
        up_weight,
        up_shift,
        down_weight,
        down_shift,
        gain_all,
        shift_all,
    ) = gathered
    gain_rows = gain_all.astype(jnp.float32)
    shift_rows = shift_all.astype(jnp.float32)
    query_scale = 1.0 / (ALPHA * math.sqrt(model_width // HEADS))
    first_hat, first_inv = normalize(inputs)
    attn_in = (first_hat * gain_rows[0] + shift_rows[0]).astype(jnp.bfloat16)
    projected = jnp.dot(attn_in, qkv_weight, preferred_element_type=jnp.float32)
    qv_float = qv_shift.astype(jnp.float32)
    queries = ((projected[:, :model_width] + qv_float[:model_width]) * query_scale).astype(
        jnp.bfloat16
    )
    keys_own = projected[:, model_width : 2 * model_width].astype(jnp.bfloat16)
    values_own = (projected[:, 2 * model_width :] + qv_float[model_width:]).astype(jnp.bfloat16)
    query_heads = queries.reshape(length, HEADS, -1)

    def scores_of(key_piece, first_row):
        piece_rows = key_piece.shape[0]
        piece_pos = first_row + jnp.arange(piece_rows, dtype=jnp.int32)
        piece_seg = lax.dynamic_slice_in_dim(key_seg, jnp.asarray(first_row, jnp.int32), piece_rows)
        allowed_pairs = (query_seg[:, None] == piece_seg[None, :]) & (
            piece_pos[None, :] <= query_pos[:, None]
        )
        raw_scores = jnp.einsum(
            "qhd,khd->hqk",
            query_heads,
            key_piece.reshape(piece_rows, HEADS, -1),
            preferred_element_type=jnp.float32,
        )
        return (jnp.where(allowed_pairs[None], raw_scores, FILLER), allowed_pairs[None])

    head_dim = model_width // HEADS
    start_state = (
        jnp.full((HEADS, length), FILLER, jnp.float32),
        jnp.zeros((HEADS, length), jnp.float32),
        jnp.zeros((HEADS, length, head_dim), jnp.float32),
    )
    accumulate_first_row = jnp.int32(0)
    accumulate_key_piece = lax.all_gather(keys_own, "blk", axis=0, tiled=True)
    accumulate_value_piece = lax.all_gather(values_own, "blk", axis=0, tiled=True)
    piece_rows = accumulate_value_piece.shape[0]

    def update(state):
        row_top, row_total, summed = state
        masked, allowed_pairs = scores_of(accumulate_key_piece, accumulate_first_row)
        new_top = jnp.maximum(row_top, jnp.max(masked, axis=2))
        factor = jnp.exp(ALPHA * (row_top - new_top))
        weights = jnp.where(allowed_pairs, jnp.exp(ALPHA * (masked - new_top[:, :, None])), 0.0)
        summed = summed * factor[:, :, None] + jnp.einsum(
            "hqk,khd->hqd",
            weights,
            accumulate_value_piece.reshape(piece_rows, HEADS, -1),
            preferred_element_type=jnp.float32,
        )
        return (new_top, row_total * factor + jnp.sum(weights, axis=2), summed)

    def unchanged(state):
        return state

    softmax_state = lax.cond(
        block_meets(accumulate_first_row, piece_rows), update, unchanged, start_state
    )
    row_top, row_total, summed = softmax_state
    attended_heads = summed / row_total[:, :, None]
    attended = jnp.transpose(attended_heads, (1, 0, 2)).reshape(length, model_width)
    attn_low = attended.astype(jnp.bfloat16)
    branch = jnp.dot(attn_low, out_weight, preferred_element_type=jnp.float32) + out_shift.astype(
        jnp.float32
    )
    second_hat, second_inv = normalize(branch)
    middle = inputs + second_hat * gain_rows[1] + shift_rows[1]
    third_hat, third_inv = normalize(middle)
    ffn_in = (third_hat * gain_rows[2] + shift_rows[2]).astype(jnp.bfloat16)
    pre_act = jnp.dot(ffn_in, up_weight, preferred_element_type=jnp.float32) + up_shift.astype(
        jnp.float32
    )
    activated, gelu_pullback = jax.vjp(gelu_tanh, pre_act)
    act_low = activated.astype(jnp.bfloat16)
    ffn_out = jnp.dot(act_low, down_weight, preferred_element_type=jnp.float32) + down_shift.astype(
        jnp.float32
    )
    fourth_hat, fourth_inv = normalize(ffn_out)
    result = middle + fourth_hat * gain_rows[3] + shift_rows[3]
    qkv_again, out_again, up_again, down_again, gain_again = (
        lax.all_gather(w_qkv, "dp", axis=0, tiled=True),
        lax.all_gather(w_out, "dp", axis=0, tiled=True),
        lax.all_gather(w_up, "dp", axis=0, tiled=True),
        lax.all_gather(w_down, "dp", axis=0, tiled=True),
        lax.all_gather(norm_gain, "dp", axis=1, tiled=True),
    )
    back_gains = gain_again.astype(jnp.float32)
    upstream = cotangent[0].astype(jnp.float32) * valid_rows[:, None]
    grad_ffn = norm_back(fourth_hat, fourth_inv, back_gains[3], upstream).astype(jnp.bfloat16)
    grad_down = jnp.einsum("tf,td->fd", act_low, grad_ffn, preferred_element_type=jnp.float32)
    grad_act = jnp.einsum("td,fd->tf", grad_ffn, down_again, preferred_element_type=jnp.float32)
    grad_pre = gelu_pullback(grad_act)[0].astype(jnp.bfloat16)
    grad_up = jnp.einsum("td,tf->df", ffn_in, grad_pre, preferred_element_type=jnp.float32)
    grad_ffn_in = jnp.einsum("tf,df->td", grad_pre, up_again, preferred_element_type=jnp.float32)
    grad_middle = upstream + norm_back(third_hat, third_inv, back_gains[2], grad_ffn_in)
    grad_branch = norm_back(second_hat, second_inv, back_gains[1], grad_middle).astype(jnp.bfloat16)
    grad_out = jnp.einsum("td,te->de", attn_low, grad_branch, preferred_element_type=jnp.float32)
    grad_attn = jnp.einsum(
        "te,de->td", grad_branch, out_again, preferred_element_type=jnp.float32
    ).astype(jnp.bfloat16)
    grad_heads = grad_attn.reshape(length, HEADS, -1)
    row_delta = jnp.einsum(
        "qhd,hqd->hq", grad_heads, attended_heads, preferred_element_type=jnp.float32
    )
    keys_all, values_all = (
        lax.all_gather(keys_own, "blk", axis=0, tiled=True),
        lax.all_gather(values_own, "blk", axis=0, tiled=True),
    )
    grad_query = jnp.zeros((length, HEADS, head_dim), jnp.float32)
    key_terms = []
    for block_index in range(block_count):
        first_row = block_index * length
        key_piece = keys_all[first_row : first_row + length]
        value_piece = values_all[first_row : first_row + length]

        def block_grads(operands):
            key_block, value_block = operands
            value_heads = value_block.reshape(length, HEADS, -1)
            masked, allowed_pairs = scores_of(key_block, first_row)
            probabilities = (
                jnp.where(allowed_pairs, jnp.exp(ALPHA * (masked - row_top[:, :, None])), 0.0)
                / row_total[:, :, None]
            )
            grad_probs = jnp.einsum(
                "qhd,khd->hqk", grad_heads, value_heads, preferred_element_type=jnp.float32
            )
            grad_scores = ALPHA * probabilities * (grad_probs - row_delta[:, :, None])
            query_term = jnp.einsum(
                "hqk,khd->qhd",
                grad_scores,
                key_block.reshape(length, HEADS, -1),
                preferred_element_type=jnp.float32,
            )
            grad_key = jnp.einsum(
                "hqk,qhd->khd", grad_scores, query_heads, preferred_element_type=jnp.float32
            )
            grad_value = jnp.einsum(
                "hqk,qhd->khd", probabilities, grad_heads, preferred_element_type=jnp.float32
            )
            return (
                query_term,
                jnp.concatenate(
                    [
                        grad_key.reshape(length, model_width),
                        grad_value.reshape(length, model_width),
                    ],
                    1,
                ),
            )

        def block_zeros(operands):
            return (
                jnp.zeros((length, HEADS, head_dim), jnp.float32),
                jnp.zeros((length, 2 * model_width), jnp.float32),
            )

        query_term, key_term = lax.cond(
            block_meets(first_row, length), block_grads, block_zeros, (key_piece, value_piece)
        )
        grad_query = grad_query + query_term
        key_terms.append(key_term)
    key_grads = lax.psum_scatter(
        jnp.concatenate(key_terms, 0).astype(jnp.bfloat16), "blk", scatter_dimension=0, tiled=True
    ).astype(jnp.float32)
    grad_keys = key_grads[:, :model_width].astype(jnp.bfloat16)
    grad_values = key_grads[:, model_width:].astype(jnp.bfloat16)
    grad_queries = grad_query.reshape(length, model_width).astype(jnp.bfloat16) * jnp.asarray(
        query_scale, jnp.bfloat16
    )
    grad_projected = jnp.concatenate([grad_queries, grad_keys, grad_values], 1)
    grad_qkv = jnp.einsum("td,te->de", attn_in, grad_projected, preferred_element_type=jnp.float32)
    grad_qv = jnp.concatenate(
        [
            jnp.sum(grad_queries.astype(jnp.float32), axis=0),
            jnp.sum(grad_values.astype(jnp.float32), axis=0),
        ]
    )
    grad_attn_in = jnp.einsum(
        "te,de->td", grad_projected, qkv_again, preferred_element_type=jnp.float32
    )
    grad_inputs = grad_middle + norm_back(first_hat, first_inv, back_gains[0], grad_attn_in)
    grad_gains = jnp.stack(
        [
            jnp.sum(grad_attn_in * first_hat, axis=0),
            jnp.sum(grad_middle * second_hat, axis=0),
            jnp.sum(grad_ffn_in * third_hat, axis=0),
            jnp.sum(upstream * fourth_hat, axis=0),
        ]
    )
    grad_shifts = jnp.stack(
        [
            jnp.sum(grad_attn_in, axis=0),
            jnp.sum(grad_middle, axis=0),
            jnp.sum(grad_ffn_in, axis=0),
            jnp.sum(upstream, axis=0),
        ]
    )
    grad_out_shift = jnp.sum(grad_branch.astype(jnp.float32), axis=0)
    grad_up_shift = jnp.sum(grad_pre.astype(jnp.float32), axis=0)
    grad_down_shift = jnp.sum(grad_ffn.astype(jnp.float32), axis=0)
    shares = (
        lax.psum_scatter(grad_qkv, "dp", scatter_dimension=0, tiled=True),
        lax.psum_scatter(grad_qv, "dp", scatter_dimension=0, tiled=True),
        lax.psum_scatter(grad_out, "dp", scatter_dimension=0, tiled=True),
        lax.psum_scatter(grad_out_shift, "dp", scatter_dimension=0, tiled=True),
        lax.psum_scatter(grad_up, "dp", scatter_dimension=0, tiled=True),
        lax.psum_scatter(grad_up_shift, "dp", scatter_dimension=0, tiled=True),
        lax.psum_scatter(grad_down, "dp", scatter_dimension=0, tiled=True),
        lax.psum_scatter(grad_down_shift, "dp", scatter_dimension=0, tiled=True),
        lax.psum_scatter(grad_gains, "dp", scatter_dimension=1, tiled=True),
        lax.psum_scatter(grad_shifts, "dp", scatter_dimension=1, tiled=True),
    )
    totals = (
        lax.psum(shares[0].astype(jnp.bfloat16), "blk").astype(jnp.float32),
        lax.psum(shares[1].astype(jnp.bfloat16), "blk").astype(jnp.float32),
        lax.psum(shares[2].astype(jnp.bfloat16), "blk").astype(jnp.float32),
        lax.psum(shares[3].astype(jnp.bfloat16), "blk").astype(jnp.float32),
        lax.psum(shares[4].astype(jnp.bfloat16), "blk").astype(jnp.float32),
        lax.psum(shares[5].astype(jnp.bfloat16), "blk").astype(jnp.float32),
        lax.psum(shares[6].astype(jnp.bfloat16), "blk").astype(jnp.float32),
        lax.psum(shares[7].astype(jnp.bfloat16), "blk").astype(jnp.float32),
        lax.psum(shares[8].astype(jnp.bfloat16), "blk").astype(jnp.float32),
        lax.psum(shares[9].astype(jnp.bfloat16), "blk").astype(jnp.float32),
    )
    return (result.astype(jnp.bfloat16)[None], grad_inputs[None]) + tuple(totals)


NZ = 4
NPOS = 512
LEN = 256
WIDTH = 1024
OWN = 512
FF4 = 1024
BF = jnp.bfloat16
F32 = jnp.float32
MESH = pl.DeviceIdType.MESH
MIB = 1 << 20
ROW_OUT, ROW_DOWN, ROW_GAIN, ROW_SHIFT = 3, 4, 5, 9
GATHER = (
    ("v", 0, "zyx"), ("q", 0, "zxy"), ("q", 1, "zyx"), ("q", 2, "zyx"),
    ("q", 3, "zyx"), ("u", 0, "zy"), ("o", 0, "zyx"), ("d", 0, "zy"),
    ("u", 1, "zy"), ("d", 1, "zy"), ("u", 2, "zy"), ("d", 2, "yz"),
    ("u", 3, "yz"), ("d", 3, "zy"),
)
GATHER_STEPS = (
    (0, 0), (1, 0), (0, 1), (2, 0), (0, 2), (1, 1), (3, 0), (0, 3),
    (-1, 0), (-1, 1), (2, 1), (4, 0), (1, 2), (3, 1), (5, 0), (7, 0),
    (4, 1), (6, 0), (2, 2), (5, 1), (10, 0), (10, 1), (12, 0), (1, 3),
    (3, 2), (4, 2), (7, 1), (8, 0), (9, 0), (12, 1), (2, 3), (8, 1),
    (12, 2), (6, 1), (7, 2), (3, 3), (4, 3), (-1, 2), (5, 2), (-1, 3),
    (-1, 4), (6, 2), (10, 2), (-1, 5), (5, 3), (-1, 6), (9, 1), (11, 0),
    (8, 2), (6, 3), (10, 3), (-1, 7), (-1, 8), (11, 1), (12, 3), (13, 0),
    (9, 2), (8, 3), (-1, 11), (-1, 12), (-1, 9), (-1, 10), (-1, 13), (13, 1),
    (-1, 14), (-1, 15), (-1, 16), (11, 2), (-1, 17), (-1, 18), (-1, 19), (13, 2),
    (-1, 20), (-1, 21), (-1, 22), (-1, 23),
)
SCATTER = (
    ("d", 0, "zy"), ("d", 1, "yz"), ("o", 0, "xyz"), ("u", 0, "zy"),
    ("u", 1, "yz"), ("d", 2, "yz"), ("q", 0, "yxz"), ("q", 1, "xyz"),
    ("q", 2, "xyz"), ("u", 2, "yz"), ("q", 3, "xyz"), ("q", 4, "xyz"),
    ("q", 5, "yxz"), ("d", 3, "yz"), ("u", 3, "yz"), ("v", 0, "xyz"),
)
SCATTER_STEPS = (
    (-1, 0), (-1, 1), (-1, 2), (-1, 3), (-1, 4), (-1, 7), (-1, 8), (-1, 11),
    (-1, 5), (0, 0), (1, 0), (-1, 12), (-1, 6), (5, 0), (-1, 9), (4, 0),
    (-1, 10), (1, 1), (3, 0), (0, 1), (-1, 13), (5, 1), (13, 0), (-1, 14),
    (0, 2), (4, 1), (9, 0), (14, 0), (-1, 15), (2, 0), (-1, 16), (-1, 17),
    (1, 2), (-1, 18), (-1, 19), (-1, 20), (6, 0), (7, 0), (13, 1), (-1, 21),
    (8, 0), (-1, 22), (-1, 23), (2, 1), (5, 2), (9, 1), (11, 0), (14, 1),
    (-1, 24), (4, 2), (3, 1), (6, 1), (12, 0), (7, 1), (3, 2), (15, 0),
    (4, 3), (2, 2), (13, 2), (8, 1), (10, 0), (3, 3), (9, 2), (6, 2),
    (14, 2), (15, 1), (7, 2), (11, 1), (8, 2), (12, 1), (9, 3), (14, 3),
    (15, 2), (2, 3), (10, 1), (11, 2), (12, 2), (6, 3), (7, 3), (10, 2),
    (15, 3), (8, 3), (11, 3), (12, 3), (10, 3),
)
WIDTHS = {"v": 128, "q": 3 * OWN, "o": OWN, "u": FF4, "d": WIDTH}


def dot_nn(a, b):
    return lax.dot_general(a, b, (((1,), (0,)), ((), ())), preferred_element_type=F32)


def dot_nt(a, b):
    return lax.dot_general(a, b, (((1,), (1,)), ((), ())), preferred_element_type=F32)


def dot_tn(a, b):
    return lax.dot_general(a, b, (((0,), (0,)), ((), ())), preferred_element_type=F32)


def loop(count, body):
    lax.fori_loop(0, count, lambda index, carry: (body(index), carry)[1], 0)


def mul(index, size):
    return pl.multiple_of(index * size, size)


class Net:
    def __init__(self, sems):
        self.chip = lax.axis_index("dp")
        self.core = lax.axis_index("blk")
        self.z = self.chip // 4
        self.y = (self.chip // 2) % 2
        self.x = self.chip % 2
        self.sems = sems
        self.used = 0
        self.unsent = []

    def sem(self):
        self.used += 1
        return self.sems.at[self.used - 1]

    def chip_at(self, z, y, x):
        return z * 4 + y * 2 + x

    def peers(self, dim):
        if dim == "x":
            return [(1, self.z, self.y, 1 - self.x, self.core)]
        if dim == "y":
            return [(1, self.z, 1 - self.y, self.x, self.core)]
        if dim == "c":
            return [(1, self.z, self.y, self.x, 1 - self.core)]
        return [(k, (self.z + k) % NZ, self.y, self.x, self.core) for k in range(1, NZ)]

    def send(self, src, dst, recv, peer):
        _, z, y, x, core = peer
        copy = pltpu.make_async_remote_copy(
            src_ref=src,
            dst_ref=dst,
            send_sem=self.sem(),
            recv_sem=recv,
            device_id=(self.chip_at(z, y, x), core),
            device_id_type=MESH,
        )
        copy.start()
        self.unsent.append(copy)
        return copy

    @staticmethod
    def drain(sends, waited):
        for copy in sends:
            if not any(copy is other for other in waited):
                copy.wait_send()

    def sibling(self, src, dst):
        return self.send(src, dst, self.sem(), self.peers("c")[0])

    def greet(self):
        barrier = pltpu.get_barrier_semaphore()
        count = 0
        for dim in "xyzc":
            for _, z, y, x, core in self.peers(dim):
                pl.semaphore_signal(
                    barrier, inc=1, device_id=(self.chip_at(z, y, x), core), device_id_type=MESH
                )
                count += 1
        return lambda: pl.semaphore_wait(barrier, count)


def await_bytes(view, sem):
    pltpu.make_async_copy(view, view, sem).wait()


def view_of(net, ref, lanes, **given):
    where = {"z": net.z, "y": net.y, "x": net.x}
    where.update(given)
    return ref.at[where["z"], where["y"], where["x"], :, lanes]


ALL = slice(None)


def gather_stages(net, ref, lanes, order):
    first, second, third = order
    others = {"z": pl.ds(0, NZ - 1), "y": 1 - net.y, "x": 1 - net.x}
    got_first, got_second, got_near, got_far = net.sem(), net.sem(), net.sem(), net.sem()

    def pass_on(dim, sem, **held):
        blocks = view_of(net, ref, lanes, **held)
        for peer in net.peers(dim):
            net.send(blocks, blocks, sem, peer)

    def start():
        pass_on(first, got_first)

    def after_first():
        await_bytes(view_of(net, ref, lanes, **{first: others[first]}), got_first)
        pass_on(second, got_second, **{first: ALL})
        pass_on(third, got_near, **{first: ALL})

    def after_second():
        held = {first: ALL, second: others[second]}
        await_bytes(view_of(net, ref, lanes, **held), got_second)
        if second == "z":
            for peer in net.peers("z"):
                pass_on(third, got_far, **{first: ALL, "z": peer[1]})
        else:
            pass_on(third, got_far, **held)

    def finish():
        held = {first: ALL, third: others[third]}
        await_bytes(view_of(net, ref, lanes, **held), got_near)
        held[second] = others[second]
        await_bytes(view_of(net, ref, lanes, **held), got_far)

    return start, after_first, after_second, finish


def scatter_stages(net, ref, lanes, order, bufs, done):
    first, second, third = order
    wide, half, line = bufs
    got_wide, got_half, got_line = net.sem(), net.sem(), net.sem()
    dtype = wide.dtype
    rows, cols = wide.shape[-2:]
    step = min(rows, max(16, 32768 // cols))
    size = {"z": NZ, "y": 2, "x": 2}
    place = {"z": 0, "y": 1, "x": 2}
    mine = {"z": net.z, "y": net.y, "x": net.x}

    def coordinate(dim, peer):
        return peer[1 + place[dim]]

    def block_add(target, sources):
        for part in range(rows // step):
            here = pl.ds(part * step, step)
            total = ref[(*target, here, lanes)].astype(F32)
            for buf, at in sources:
                total = total + buf[(*at, here)].astype(F32)
            ref[(*target, here, lanes)] = total.astype(dtype)

    def target_of(**given):
        where = dict(mine)
        where.update(given)
        return (where["z"], where["y"], where["x"])

    def start():
        for peer in net.peers(first):
            there = {"z": ALL, "y": ALL, "x": ALL, first: coordinate(first, peer)}
            net.send(view_of(net, ref, lanes, **there), wide.at[peer[0] - 1], got_wide, peer)

    def after_first():
        await_bytes(wide, got_wide)
        left = [dim for dim in "zyx" if dim != first]

        def add(second_at, third_at):
            at = {second: second_at, third: third_at}
            place_in = (0, at[left[0]], at[left[1]])
            block_add(target_of(**at), [(wide, place_in)])

        for peer in net.peers(second):
            gone = coordinate(second, peer)
            loop(size[third], lambda other: add(gone, other))
            blocks = view_of(net, ref, lanes, **{second: gone, third: ALL})
            net.send(blocks, half.at[peer[0] - 1], got_half, peer)
        loop(size[third], lambda other: add(mine[second], other))

    def after_second():
        await_bytes(half, got_half)
        for peer in net.peers(third):
            gone = coordinate(third, peer)
            block_add(
                target_of(**{third: gone}), [(half, (k, gone)) for k in range(size[second] - 1)]
            )
            blocks = view_of(net, ref, lanes, **{third: gone})
            net.send(blocks, line.at[peer[0] - 1], got_line, peer)

    def finish():
        await_bytes(line, got_line)
        for part in range(rows // step):
            here = pl.ds(part * step, step)
            total = ref[(*target_of(), here, lanes)].astype(F32)
            for k in range(size[second] - 1):
                total = total + half[k, mine[third], here].astype(F32)
            for k in range(size[third] - 1):
                total = total + line[k, here].astype(F32)
            done(part * step, step, total)

    return start, after_first, after_second, finish


def plane_gather_stages(net, ref, lanes, order):
    first, second = order
    others = {"z": pl.ds(0, NZ - 1), "y": 1 - net.y}
    got_first, got_second = net.sem(), net.sem()

    def place(**given):
        where = {"z": net.z, "y": net.y}
        where.update(given)
        return ref.at[where["z"], where["y"], :, lanes]

    def pass_on(dim, sem, **held):
        for peer in net.peers(dim):
            net.send(place(**held), place(**held), sem, peer)

    def start():
        pass_on(first, got_first)

    def after_first():
        await_bytes(place(**{first: others[first]}), got_first)
        pass_on(second, got_second, **{first: ALL})

    def finish():
        await_bytes(place(**{first: ALL, second: others[second]}), got_second)

    return [start, after_first, finish]


def plane_scatter_stages(net, ref, lanes, order, bufs, emit):
    first, second = order
    wide, line = bufs[:2]
    got_wide, got_line = net.sem(), net.sem()
    rows, cols = wide.shape[-2:]
    step = min(rows, max(16, 32768 // cols))
    size = {"z": NZ, "y": 2}
    place = {"z": 1, "y": 2}
    mine = {"z": net.z, "y": net.y}

    def at(**given):
        where = dict(mine)
        where.update(given)
        return (where["z"], where["y"])

    def start():
        for peer in net.peers(first):
            there = at(**{first: peer[place[first]], second: ALL})
            net.send(ref.at[(*there, ALL, lanes)], wide.at[peer[0] - 1], got_wide, peer)

    def total(where, slot, here):
        value = ref[(*where, here, lanes)].astype(F32)
        for k in range(size[first] - 1):
            value = value + wide[k, slot, here].astype(F32)
        return value

    def after_first():
        await_bytes(wide, got_wide)
        for peer in net.peers(second):
            gone = peer[place[second]]
            there = at(**{second: gone})

            def add(part):
                here = pl.ds(mul(part, step), step)
                ref[(*there, here, lanes)] = total(there, gone, here).astype(BF)

            loop(rows // step, add)
            net.send(ref.at[(*there, ALL, lanes)], line.at[peer[0] - 1], got_line, peer)

    def final(here):
        value = total(at(), mine[second], here)
        for k in range(size[second] - 1):
            value = value + line[k, here].astype(F32)
        return value

    def finish():
        await_bytes(line, got_line)
        emit(final)

    return [start, after_first, finish]


def pieces_of(plan, widths):
    counts = {}
    for group, _, _ in plan:
        counts[group] = counts.get(group, 0) + 1
    return [
        (group, index * (widths[group] // counts[group]), widths[group] // counts[group], order)
        for group, index, order in plan
    ]


def layer_kernel(
    tok_in,
    doc,
    cot_in,
    wq_in,
    wo_in,
    wu_in,
    wd_in,
    qv_in,
    up_in,
    out_in,
    down_in,
    gain_in,
    shift_in,
    res_out,
    gtok_out,
    gq_out,
    go_out,
    gu_out,
    gd_out,
    gvec_out,
    wq,
    wo,
    wu,
    wux,
    wd,
    vbuf,
    tok,
    cot,
    pack,
    vecs,
    vq,
    vu,
    xin,
    qb,
    kb,
    vb,
    pb,
    att,
    attb,
    attx,
    hat1,
    hat2,
    inv1,
    inv2,
    mid,
    fin,
    act,
    dge,
    rcv,
    own,
    snd,
    own_x,
    snd_s,
    rcv_s,
    snd_x,
    rcv_x,
    gff,
    gbr,
    dob,
    dsb,
    gqo,
    gu,
    gd,
    swap,
    acc,
    acc_qv,
    acc_up,
    gvecs,
    gv,
    vother,
    piece_bufs,
    st_q,
    st_o,
    st_u,
    st_ux,
    r_ux,
    st_d,
    sems,
    local_sems,
):
    net = Net(sems)
    core = net.core
    greeted = net.greet()

    locals_ = []

    def fetch(src, dst):
        copy = pltpu.make_async_copy(src, dst, local_sems.at[len(locals_)])
        copy.start()
        locals_.append(copy)

    def lanes_of(start, size):
        return pl.ds(pl.multiple_of(start, 128), size)

    for part in range(3):
        fetch(
            wq_in.at[:, lanes_of(part * WIDTH + core * OWN, OWN)],
            wq.at[net.z, net.y, net.x, :, pl.ds(part * OWN, OWN)],
        )
    fetch(wo_in.at[:, lanes_of(core * OWN, OWN)], wo.at[core, net.z, net.y, net.x])
    for zy in range(8):
        fetch(
            wu_in.at[:, lanes_of((zy * 2 + 1 - net.x) * 256 + core * 128, 128)],
            wux.at[:, pl.ds(zy * 128, 128)],
        )
    own_half = pl.ds(mul(net.x, 64), 64)
    for zy in range(8):
        fetch(
            wu_in.at[:, lanes_of((zy * 2 + net.x) * 256 + core * 128, 128)],
            wu.at[net.z, net.y, own_half, pl.ds(zy * 128, 128)],
        )
    fetch(wd_in.at[pl.ds(mul(core, 128), 128), :], wd.at[net.z, net.y])
    fetch(tok_in, tok)
    fetch(cot_in, cot)
    pack[...] = jnp.zeros_like(pack)
    pack[0:1, :] = qv_in[...].astype(F32)
    pack[1:3, :] = up_in[...].astype(F32)
    for row, ref in (
        (ROW_OUT, out_in),
        (ROW_DOWN, down_in),
        (ROW_GAIN, gain_in),
        (ROW_SHIFT, shift_in),
    ):
        value = ref[...].astype(F32)
        rows = slice(row, row + value.shape[0])
        pack[rows, 0:64] = jnp.where(net.x == 0, value, 0.0)
        pack[rows, 64:128] = jnp.where(net.x == 1, value, 0.0)
    vbuf[net.z, net.y, net.x] = pack[...].astype(BF)
    wo_own = wo.at[core]
    plan = pieces_of(GATHER, WIDTHS)
    sources = {"v": vbuf, "q": wq, "o": wo_own}

    def stages_of(group, lanes, order):
        if group == "d":
            return plane_gather_stages(net, wd, lanes, order)
        if group == "u":
            passing = plane_gather_stages(net, wu, lanes, order)
            got_x = net.sem()

            def cross():
                net.send(
                    wux.at[:, lanes],
                    wu.at[net.z, net.y, own_half, lanes],
                    got_x,
                    net.peers("x")[0],
                )

            def crossed():
                await_bytes(wux.at[:, lanes], got_x)
                passing[0]()

            return [cross, crossed, *passing[1:]]
        return gather_stages(net, sources[group], lanes, order)

    gathers = [
        stages_of(group, pl.ds(lane0, count), order) for group, lane0, count, order in plan
    ]
    greeted()
    ready = {("q", 0): 3, ("o", 0): 4, ("u", 0): 12, ("u", 1): 20, ("d", 0): 21}
    state = {"landed": 0}
    got_wo = []

    def gather(piece, stage):
        while state["landed"] < ready.get((plan[piece][0], stage), 0):
            locals_[state["landed"]].wait()
            state["landed"] += 1
        gathers[piece][stage]()
        group, lane0, count, _ = plan[piece]
        if group == "o" and stage == 3:
            half = wo_own.at[:, :, :, :, pl.ds(lane0, count)]
            got_wo.append(net.sibling(half, half))

    def spread_vectors():
        for z in range(NZ):
            for y in range(2):
                both = vbuf[z, y, 0].astype(F32) + vbuf[z, y, 1].astype(F32)
                vecs[:, pl.ds((z * 2 + y) * 128, 128)] = both
        for y in range(2):
            for x in range(2):
                at = pl.ds((y * 2 + x) * 128, 128)
                vq[0:8, at] = vbuf[core, y, x].astype(F32)[0:8]
                vq[8:16, at] = vbuf[core + 2, y, x].astype(F32)[0:8]
        for z in range(NZ):
            for y in range(2):
                block = vbuf[z, y, net.x].astype(F32)
                vu[0:1, pl.ds((z * 2 + y) * 128, 128)] = jnp.where(
                    core == 0, block[1:2], block[2:3]
                )
        acc[...] = jnp.zeros_like(acc)
        acc_up[...] = jnp.zeros_like(acc_up)

    def gain(n):
        return vecs[ROW_GAIN + n : ROW_GAIN + n + 1, :]

    def shift(n):
        return vecs[ROW_SHIFT + n : ROW_SHIFT + n + 1, :]

    def accumulate(row, value):
        parts = value.reshape(value.shape[0] // 8, 8, value.shape[1])
        acc[row] += jnp.sum(parts, axis=0)

    got = {}

    chunk = 32
    chunks = LEN // chunk

    def ln0(i):
        here = pl.ds(mul(i, chunk), chunk)
        hat, _ = normalize(tok[here, :].astype(F32))
        xin[core, here, :] = (hat * gain(0) + shift(0)).astype(BF)

    def attention_input():
        locals_[21].wait()
        loop(chunks, ln0)
        got["x"] = net.sibling(xin.at[core], xin.at[core])

    ends = []
    end = jnp.int32(0)
    for j in range(8):
        end = end + doc[0, j]
        ends.append(end)

    def segment(position):
        total = jnp.zeros(position.shape, jnp.int32)
        for value in ends:
            total = total + (position >= value).astype(jnp.int32)
        return total

    scale = 1.0 / (ALPHA * 8.0)

    def project(t):
        n = t // 2
        m = t % 2
        tile = pl.ds(mul(n, 256), 256)
        rows = pl.ds(mul(m, 256), 256)

        def part(index, dst, bias, factor):
            weight = wq[:, :, :, :, pl.ds(pl.multiple_of(index * OWN + n * 256, 256), 256)]
            value = dot_nn(xin[m], weight.reshape(WIDTH, 256))
            if bias is not None:
                value = value + vq[bias : bias + 1, tile]
            if factor is not None:
                value = value * factor
            dst[rows, tile] = value.astype(BF)

        part(0, qb, 0, scale)
        part(1, kb, None, None)
        part(2, vb, 8, None)

    def projections():
        got["x"].wait_recv()
        loop(4, project)

    lane = lax.broadcasted_iota(jnp.int32, (1, 128), 1)
    block = 128

    def attend(pair):
        at = pl.ds(mul(pair, 128), 128)
        for r in range(NPOS // block):
            rows = pl.ds(r * block, block)
            count = (r + 1) * block
            q_pos = r * block + lax.broadcasted_iota(jnp.int32, (block, 1), 0)
            k_pos = lax.broadcasted_iota(jnp.int32, (1, count), 1)
            allowed = (segment(q_pos) == segment(k_pos)) & (k_pos <= q_pos)
            q = qb[rows, at]
            k = kb[0:count, at]
            v = vb[0:count, at]
            outs = []
            for head in range(2):
                mine = (lane < 64) if head == 0 else (lane >= 64)
                scores = dot_nt(jnp.where(mine, q, jnp.zeros_like(q)), k)
                scores = jnp.where(allowed, scores, FILLER)
                top = jnp.max(scores, axis=1, keepdims=True)
                weights = jnp.exp(ALPHA * (scores - top))
                probs = weights * (1.0 / jnp.sum(weights, axis=1, keepdims=True))
                probs = probs.astype(BF)
                pb[pair * 2 + head, rows, 0:count] = probs
                outs.append(dot_nn(probs, v))
            out = jnp.where(lane < 64, outs[0], outs[1])
            att[rows, at] = out
            attb[rows, at] = out.astype(BF)

    other_rows = pl.ds(mul(1 - core, LEN), LEN)
    own_rows = pl.ds(mul(core, LEN), LEN)

    def attend_last():
        attend(3)
        got["att"] = net.sibling(attb.at[other_rows, :], attx)

    own_group = net.x * 2 + core
    across_group = (1 - net.x) * 2 + core

    def branch_tile(n):
        lanes = pl.ds(mul(n % 2, 256), 256)
        mine = wo[n // 2, pl.ds(2 * core, 2), :, :, :, lanes].reshape(OWN, 256)
        theirs = wo[n // 2, pl.ds(2 * (1 - core), 2), :, :, :, lanes].reshape(OWN, 256)
        at = pl.ds(mul(n, 256), 256)
        own[:, at] = dot_nn(attb[own_rows, :], mine) + dot_nn(attx[...], theirs)

    def branch_all():
        got["att"].wait_recv()
        loop(2, lambda i: branch_tile(core * 2 + i))
        for part in got_wo:
            part.wait_recv()
        loop(2, lambda i: branch_tile((1 - core) * 2 + i))

    def ln12(i):
        here = pl.ds(mul(i, chunk), chunk)
        first, first_inv = normalize(own[here, :] + vecs[ROW_OUT : ROW_OUT + 1, :])
        hat1[here, :] = first
        inv1[here, :] = jnp.broadcast_to(first_inv, (chunk, 128))
        middle = tok[here, :].astype(F32) + first * gain(1) + shift(1)
        mid[here, :] = middle
        second, second_inv = normalize(middle)
        hat2[here, :] = second
        inv2[here, :] = jnp.broadcast_to(second_inv, (chunk, 128))
        fin[own_group, here, :] = (second * gain(2) + shift(2)).astype(BF)

    class Share:
        def __init__(self, ref):
            self.ref = ref
            self.beside, self.across, self.passed = [], [], []

        def send(self, half):
            rows = pl.ds(half * 128, 128)
            view = self.ref.at[own_group, rows]
            self.beside.append(net.sibling(view, view))
            self.across.append(net.send(view, view, net.sem(), net.peers("x")[0]))

        def pass_on(self, half):
            self.across[half].wait_recv()
            view = self.ref.at[across_group, pl.ds(half * 128, 128)]
            self.passed.append(net.sibling(view, view))

        def wait(self, copies):
            for copy in copies:
                copy.wait_recv()

    class Reduce:
        def __init__(self, product):
            self.product = product
            self.beside, self.across = [], []

        def group_rows(self, group):
            return pl.ds(mul(group, LEN), LEN)

        def multiply(self, n):
            at = pl.ds(n * 256, 256)
            for xg in range(2):
                value = self.product(self.group_rows(xg * 2 + 1 - core), n)
                snd_s[xg, :, at] = value.astype(BF)
            self.beside.append(net.sibling(snd_s.at[:, :, at], rcv_s.at[:, :, at]))
            own_x[:, at] = self.product(self.group_rows(across_group), n)
            own[:, at] = self.product(self.group_rows(own_group), n)

        def cross(self, n):
            at = pl.ds(n * 256, 256)
            self.beside[n].wait_recv()

            def add(i):
                here = pl.ds(mul(i, 64), 64)
                over = own_x[here, at] + rcv_s[1 - net.x, here, at].astype(F32)
                snd_x[here, at] = over.astype(BF)
                own[here, at] += rcv_s[net.x, here, at].astype(F32)

            loop(4, add)
            self.across.append(
                net.send(snd_x.at[:, at], rcv_x.at[:, at], net.sem(), net.peers("x")[0])
            )

        def wait(self):
            for copy in self.across:
                copy.wait_recv()

        def free(self):
            for copy in self.beside + self.across:
                copy.wait_send()

    share_fin, share_gff = Share(fin), Share(gff)

    def norms_12():
        for half in range(2):
            loop(chunks // 2, lambda i: ln12(i + half * (chunks // 2)))
            share_fin.send(half)

    root = math.sqrt(2.0 / math.pi)

    def up_tile(n, group):
        at = pl.ds(mul(n, 256), 256)
        rows = pl.ds(mul(group, LEN), LEN)
        u = dot_nn(fin[group], wu[:, :, :, at].reshape(WIDTH, 256)) + vu[0:1, at]
        square = u * u
        inner = jnp.tanh(root * (u + 0.044715 * (square * u)))
        half = 0.5 * (1.0 + inner)
        act[rows, at] = (u * half).astype(BF)
        slope = 0.5 * u * (1.0 - inner * inner) * (root * (1.0 + (3 * 0.044715) * square))
        dge[rows, at] = (half + slope).astype(BF)

    def up_group(group):
        loop(4, lambda n: up_tile(n, group))

    def up_beside():
        share_fin.wait(share_fin.beside)
        up_group(net.x * 2 + 1 - core)

    def up_last():
        share_fin.wait(share_fin.passed)
        up_group((1 - net.x) * 2 + 1 - core)

    def down_product(rows, n):
        return dot_nn(act[rows, :], wd[:, :, :, pl.ds(n * 256, 256)].reshape(FF4, 256))

    down = Reduce(down_product)

    def tiles_of(width, count, body):
        return [functools.partial(body, lane0, count) for lane0 in range(0, width, count)]

    steps = [
        spread_vectors,
        attention_input,
        projections,
        lambda: loop(1, attend),
        lambda: loop(1, lambda i: attend(i + 1)),
        lambda: loop(1, lambda i: attend(i + 2)),
        attend_last,
        branch_all,
        norms_12,
        lambda: share_fin.pass_on(0),
        lambda: share_fin.pass_on(1),
    ]
    steps += [
        lambda: up_group(own_group),
        up_beside,
        lambda: up_group(across_group),
        up_last,
        functools.partial(down.multiply, 0),
        functools.partial(down.multiply, 1),
        functools.partial(down.cross, 0),
        functools.partial(down.multiply, 2),
        functools.partial(down.cross, 1),
        functools.partial(down.multiply, 3),
        functools.partial(down.cross, 2),
        functools.partial(down.cross, 3),
    ]
    filled = ends[-1]

    def upstream_of(i):
        here = pl.ds(mul(i, chunk), chunk)
        position = core * LEN + i * chunk + lax.broadcasted_iota(jnp.int32, (chunk, 1), 0)
        return cot[here, :].astype(F32) * (position < filled).astype(F32)

    def top_tile(i):
        here = pl.ds(mul(i, chunk), chunk)
        value = own[here, :] + rcv_x[here, :].astype(F32) + vecs[ROW_DOWN : ROW_DOWN + 1, :]
        hat, inv = normalize(value)
        res_out[here, :] = (mid[here, :] + hat * gain(3) + shift(3)).astype(BF)
        upstream = upstream_of(i)
        grad = norm_back(hat, inv, gain(3), upstream).astype(BF)
        gff[own_group, here, :] = grad
        accumulate(ROW_GAIN + 3, upstream * hat)
        accumulate(ROW_SHIFT + 3, upstream)
        accumulate(ROW_DOWN, grad.astype(F32))

    def top():
        locals_[22].wait()
        down.wait()
        for half in range(2):
            loop(chunks // 2, lambda i: top_tile(i + half * (chunks // 2)))
            share_gff.send(half)

    steps.append(top)
    for piece, stage in GATHER_STEPS:
        if piece < 0:
            steps[stage]()
        else:
            gather(piece, stage)


    out_copies = []

    def deliver(src, dst):
        copy = pltpu.make_async_copy(src, dst, local_sems.at[23 + len(out_copies)])
        copy.start()
        out_copies.append((copy, net.sibling(src, dst)))

    def ship(group, lane0, count):
        if group == "d":
            at = pl.ds(lane0, count)
            deliver(st_d.at[:, at], gd_out.at[pl.ds(mul(core, 128), 128), at])
        if group == "u":
            for part in range(2):
                for zy in range(lane0 // 128, (lane0 + count) // 128):
                    deliver(
                        st_u.at[part, :, pl.ds(zy * 128, 128)],
                        gu_out.at[:, lanes_of((zy * 2 + part) * 256 + core * 128, 128)],
                    )
        if group == "o":
            deliver(
                st_o.at[:, pl.ds(lane0, count)], go_out.at[:, lanes_of(core * OWN + lane0, count)]
            )
        if group == "q":
            start = (lane0 // OWN) * WIDTH + lane0 % OWN
            deliver(
                st_q.at[:, pl.ds(lane0, count)], gq_out.at[:, lanes_of(core * OWN + start, count)]
            )

    plan = pieces_of(SCATTER, WIDTHS)
    sums = {"o": gqo, "q": gqo, "v": gv}
    stage_of = {"o": st_o, "q": st_q, "v": gvec_out}

    def store_to(stage, lane0, count):
        def done(row0, size, total):
            stage[row0 : row0 + size, lane0 : lane0 + count] = total

        return done

    def sums_of(group, lane0, count, order, bufs):
        lanes = pl.ds(lane0, count)
        if group == "d":

            def keep(total):
                for part in range(4):
                    here = pl.ds(part * 32, 32)
                    st_d[here, lanes] = total(here)

            return plane_scatter_stages(net, gd, lanes, order, bufs, keep)
        if group == "u":
            got_x = net.sem()

            def cross(total):
                for part in range(2):
                    here = pl.ds(part * 32, 32)
                    theirs = pl.multiple_of((1 - net.x) * 64 + part * 32, 32)
                    st_ux[here, lanes] = total(pl.ds(theirs, 32)).astype(BF)
                net.send(st_ux.at[:, lanes], r_ux.at[:, lanes], got_x, net.peers("x")[0])
                for part in range(2):
                    here = pl.ds(part * 32, 32)
                    mine = pl.multiple_of(net.x * 64 + part * 32, 32)
                    st_u[net.x, here, lanes] = total(pl.ds(mine, 32))

            def crossed():
                await_bytes(r_ux.at[:, lanes], got_x)
                st_u[1 - net.x, :, lanes] = r_ux[:, lanes].astype(F32)

            return [*plane_scatter_stages(net, gu, lanes, order, bufs, cross), crossed]
        base = 3 * OWN if group == "o" else 0
        return scatter_stages(
            net,
            sums[group],
            pl.ds(base + lane0, count),
            order,
            bufs,
            store_to(stage_of[group], lane0, count),
        )

    scatters = [
        sums_of(*piece, bufs) for piece, bufs in zip(plan, piece_bufs, strict=True)
    ]

    def scatter(piece, stage):
        scatters[piece][stage]()
        if stage == len(scatters[piece]) - 1:
            ship(*plan[piece][:3])

    def gdown_piece(lane0, count):
        at = pl.ds(lane0, count)

        def tile(z):
            left = act[:, pl.ds(mul(z, 256), 256)]
            grad = gff[:, :, at].reshape(4 * LEN, count)
            gd[z, :, :, at] = dot_tn(left, grad).astype(BF).reshape(2, 128, count)

        loop(NZ, tile)

    def gpre_tile(group, z):
        at = pl.ds(mul(z, 256), 256)
        rows = pl.ds(mul(group, LEN), LEN)
        weight = wd[z].reshape(256, WIDTH)
        value = dot_nt(gff[group], weight) * dge[rows, at].astype(F32)
        value = value.astype(BF)
        dge[rows, at] = value
        acc_up[:, at] += jnp.sum(value.astype(F32).reshape(32, 8, 256), axis=0)

    def gpre_group(group):
        loop(NZ, functools.partial(gpre_tile, group))

    def gpre_beside():
        share_gff.wait(share_gff.beside)
        gpre_group(net.x * 2 + 1 - core)

    def gpre_last():
        share_gff.wait(share_gff.passed)
        gpre_group((1 - net.x) * 2 + 1 - core)

    def gup_piece(lane0, count):
        at = pl.ds(lane0, count)

        def tile(z):
            left = fin[:, :, pl.ds(mul(z, 256), 256)].reshape(4 * LEN, 256)
            gu[z, :, :, at] = dot_tn(left, dge[:, at]).astype(BF).reshape(2, 128, count)

        loop(NZ, tile)

    def grad_ffn_in_product(rows, n):
        return dot_nt(dge[rows, :], wu[n].reshape(256, FF4))

    gfi = Reduce(grad_ffn_in_product)

    def grad_ffn_in():
        down.free()
        for n in range(4):
            gfi.multiply(n)

    def grad_ffn_in_cross():
        for n in range(4):
            gfi.cross(n)

    def middle_tile(i):
        here = pl.ds(mul(i, chunk), chunk)
        grad_in = own[here, :] + rcv_x[here, :].astype(F32)
        second = hat2[here, :]
        accumulate(ROW_GAIN + 2, grad_in * second)
        accumulate(ROW_SHIFT + 2, grad_in)
        grad_mid = upstream_of(i) + norm_back(second, inv2[here, 0:1], gain(2), grad_in)
        mid[here, :] = grad_mid
        first = hat1[here, :]
        accumulate(ROW_GAIN + 1, grad_mid * first)
        accumulate(ROW_SHIFT + 1, grad_mid)
        grad = norm_back(first, inv1[here, 0:1], gain(1), grad_mid).astype(BF)
        gbr[core, here, :] = grad
        accumulate(ROW_OUT, grad.astype(F32))

    def grad_middle():
        gfi.wait()
        loop(chunks, middle_tile)
        got["gbr"] = net.sibling(gbr.at[core], gbr.at[core])

    go = gqo.at[:, :, :, :, pl.ds(3 * OWN, OWN)]

    def gout_tile(k, cols, put):
        left = attb[:, pl.ds(mul(k, 256), 256)]
        grad = gbr[:, :, cols].reshape(NPOS, OWN)
        put(k, dot_tn(left, grad).astype(BF).reshape(2, 2, 64, OWN))

    def put_swap(k, value):
        swap[k] = value

    def put_own(k, value):
        gqo[2 * core + k, :, :, :, pl.ds(3 * OWN, OWN)] = value


    def gatt_tile(t):
        k = t // 2
        m = t % 2
        left = wo[0, 2 * core + k].reshape(256, OWN)
        right = wo[1, 2 * core + k].reshape(256, OWN)
        value = dot_nt(gbr[m, :, 0:OWN], left) + dot_nt(gbr[m, :, OWN:WIDTH], right)
        dob[pl.ds(mul(m, 256), 256), pl.ds(mul(k, 256), 256)] = value.astype(BF)

    def grad_out():
        got["gbr"].wait_recv()
        loop(2, lambda k: gout_tile(k, lanes_of((1 - core) * OWN, OWN), put_swap))
        got["swap"] = net.sibling(swap, go.at[pl.ds(2 * core, 2)])
        loop(2, lambda k: gout_tile(k, lanes_of(core * OWN, OWN), put_own))
        loop(4, gatt_tile)

    def attend_back(pair):
        at = pl.ds(mul(pair, 128), 128)
        sums = []
        for head in range(2):
            mine = (lane < 64) if head == 0 else (lane >= 64)
            queries_ = []
            for r in range(NPOS // block):
                rows = pl.ds(r * block, block)
                count = (r + 1) * block
                grad = dob[rows, at]
                grad = jnp.where(mine, grad, jnp.zeros_like(grad))
                delta = jnp.sum(grad.astype(F32) * att[rows, at], axis=1, keepdims=True)
                probs = pb[pair * 2 + head, rows, 0:count].astype(F32)
                grad_probs = dot_nt(grad, vb[0:count, at])
                scores = (ALPHA * probs * (grad_probs - delta)).astype(BF)
                dsb[rows, 0:count] = scores
                queries_.append(dot_nn(scores, kb[0:count, at]))
            keys_, values_ = [], []
            for r in range(NPOS // block):
                rows = pl.ds(r * block, NPOS - r * block)
                cols = pl.ds(r * block, block)
                keys_.append(dot_tn(dsb[rows, cols], qb[rows, at]))
                values_.append(dot_tn(pb[pair * 2 + head, rows, cols], dob[rows, at]))
            sums.append((queries_, keys_, values_))
        total_q = jnp.zeros((8, 128), F32)
        total_v = jnp.zeros((8, 128), F32)
        for r in range(NPOS // block):
            rows = pl.ds(r * block, block)
            merged = [
                jnp.where(lane < 64, sums[0][i][r], sums[1][i][r]).astype(BF) for i in range(3)
            ]
            grad_q = merged[0] * jnp.asarray(scale, BF)
            qb[rows, at] = grad_q
            kb[rows, at] = merged[1]
            vb[rows, at] = merged[2]
            total_q += jnp.sum(grad_q.astype(F32).reshape(block // 8, 8, 128), axis=0)
            total_v += jnp.sum(merged[2].astype(F32).reshape(block // 8, 8, 128), axis=0)
        acc_qv[0, :, at] = total_q
        acc_qv[1, :, at] = total_v

    def gqkv_piece(lane0, count):
        ref = (qb, kb, vb)[lane0 // OWN]

        def tile(z):
            left = xin[:, :, pl.ds(mul(z, 256), 256)].reshape(NPOS, 256)
            value = dot_tn(left, ref[:, lane0 % OWN : lane0 % OWN + count]).astype(BF)
            gqo[z, :, :, :, pl.ds(lane0, count)] = value.reshape(2, 2, 64, count)

        loop(NZ, tile)

    def gai_tile(rows, dst):
        def body(z):
            value = None
            for part, ref in enumerate((qb, kb, vb)):
                weight = wq[z, :, :, :, pl.ds(part * OWN, OWN)].reshape(256, OWN)
                term = dot_nt(ref[rows, :], weight)
                value = term if value is None else value + term
            dst[:, pl.ds(mul(z, 256), 256)] = value

        loop(NZ, body)

    def grad_attn_in():
        gai_tile(other_rows, snd)
        got["gai"] = net.sibling(snd, rcv)
        gai_tile(own_rows, own)

    def bottom_tile(i):
        here = pl.ds(mul(i, chunk), chunk)
        hat, inv = normalize(tok[here, :].astype(F32))
        grad_in = own[here, :] + rcv[here, :]
        accumulate(ROW_GAIN, grad_in * hat)
        accumulate(ROW_SHIFT, grad_in)
        gtok_out[here, :] = mid[here, :] + norm_back(hat, inv, gain(0), grad_in)

    def bottom():
        got["gai"].wait_recv()
        loop(chunks, bottom_tile)
        for row in range(16):
            gvecs[row : row + 1, :] = jnp.sum(acc[row], axis=0, keepdims=True)
        row_id = lax.broadcasted_iota(jnp.int32, (16, 1), 0)
        for z in range(NZ):
            for y in range(2):
                base = gvecs[:, pl.ds((z * 2 + y) * 128, 128)]
                for x in range(2):
                    at = pl.ds((y * 2 + x) * 128, 128)
                    kind = 0 if z < 2 else 1
                    qv_row = jnp.sum(acc_qv[kind, :, at], axis=0, keepdims=True)
                    qv_row = jnp.where(core == z % 2, qv_row, 0.0)
                    up_at = pl.ds((z * 2 + y) * 128, 128)
                    up_row = jnp.sum(acc_up[:, up_at], axis=0, keepdims=True)
                    up_row = jnp.where(net.x == x, up_row, 0.0)
                    value = base + jnp.where(row_id == 0, qv_row, 0.0)
                    gv[z, y, x] = value + jnp.where(row_id == 1 + core, up_row, 0.0)

    steps = [
        lambda: None,
        lambda: gpre_group(own_group),
        gpre_beside,
        lambda: share_gff.pass_on(0),
        lambda: share_gff.pass_on(1),
        *tiles_of(WIDTH, 512, gdown_piece),
        lambda: gpre_group(across_group),
        gpre_last,
        *tiles_of(FF4, 512, gup_piece),
        grad_ffn_in,
        grad_ffn_in_cross,
        grad_middle,
        grad_out,
        lambda: got["swap"].wait_recv(),
    ]
    steps += [functools.partial(loop, 1, lambda i, pair=p: attend_back(i + pair)) for p in range(4)]
    steps += tiles_of(3 * OWN, 512, gqkv_piece)
    steps += [grad_attn_in, bottom]
    for piece, stage in SCATTER_STEPS:
        if piece < 0:
            steps[stage]()
        else:
            scatter(piece, stage)
    got_vec = net.sibling(gvec_out, vother)
    got_vec.wait_send()
    got_vec.wait_recv()
    gvec_out[...] = gvec_out[...] + vother[...]
    for copy, remote in out_copies:
        copy.wait()
        remote.wait_recv()
    net.drain(net.unsent, (*down.beside, *down.across, got_vec))


def scatter_bufs(group, count, order):
    rows, dtype = {"v": (16, F32)}.get(group, (64, BF))
    size = {"z": NZ, "y": 2, "x": 2}
    if group in "du":
        first, second = order
        return [
            pltpu.VMEM((size[first] - 1, size[second], 128, count), BF),
            pltpu.VMEM((size[second] - 1, 128, count), BF),
        ]
    first, second, third = order
    left = [size[dim] for dim in "zyx" if dim != first]
    return [
        pltpu.VMEM((size[first] - 1, *left, rows, count), dtype),
        pltpu.VMEM((size[second] - 1, size[third], rows, count), dtype),
        pltpu.VMEM((size[third] - 1, rows, count), dtype),
    ]


SPLIT = 4


def hand_out_kernel(*refs):
    large, vec = refs[:6], refs[6]
    outs, small, held, sems = refs[7:13], refs[13:19], refs[19:25], refs[25]
    arrivals, copies = [], []
    for src, mid, dst in zip(large, held, outs, strict=True):
        rows = src.shape[0] // SPLIT
        for part in range(SPLIT):
            here = pl.ds(part * rows, rows)
            at = len(arrivals)
            arrivals.append(pltpu.make_async_copy(src.at[here], mid.at[here], sems.at[0, at]))
            copies.append(pltpu.make_async_copy(mid.at[here], dst.at[here], sems.at[1, at]))
            arrivals[-1].start()
    right = lax.axis_index("dp") % 2 == 1
    values = vec[...]
    half = jnp.where(right, values[:, 64:], values[:, :64])
    small[0][...] = values[0:1]
    small[1][...] = half[ROW_OUT : ROW_OUT + 1]
    small[2][...] = values[1:3]
    small[3][...] = half[ROW_DOWN : ROW_DOWN + 1]
    small[4][...] = half[ROW_GAIN : ROW_GAIN + 4]
    small[5][...] = half[ROW_SHIFT : ROW_SHIFT + 4]
    for arrival, copy in zip(arrivals, copies, strict=True):
        arrival.wait()
        copy.start()
    for copy in copies:
        copy.wait()


def fused(
    tokens,
    doc_lengths,
    cotangent,
    w_qkv,
    qv_bias,
    w_out,
    out_bias,
    w_up,
    up_bias,
    w_down,
    down_bias,
    norm_gain,
    norm_bias,
):
    vmem = pl.BlockSpec(memory_space=pltpu.VMEM)
    anywhere = pl.BlockSpec(memory_space=pl.ANY)
    scratch = [
        pltpu.VMEM((NZ, 2, 2, 64, 3 * OWN), BF),
        pltpu.VMEM((2, NZ, 2, 2, 64, OWN), BF),
        pltpu.VMEM((NZ, 2, 128, FF4), BF),
        pltpu.VMEM((64, FF4), BF),
        pltpu.VMEM((NZ, 2, 128, WIDTH), BF),
        pltpu.VMEM((NZ, 2, 2, 16, 128), BF),
        pltpu.VMEM((LEN, WIDTH), BF),
        pltpu.VMEM((LEN, WIDTH), BF),
        pltpu.VMEM((16, 128), F32),
        pltpu.VMEM((16, WIDTH), F32),
        pltpu.VMEM((16, OWN), F32),
        pltpu.VMEM((8, FF4), F32),
        pltpu.VMEM((2, LEN, WIDTH), BF),
        pltpu.VMEM((NPOS, OWN), BF),
        pltpu.VMEM((NPOS, OWN), BF),
        pltpu.VMEM((NPOS, OWN), BF),
        pltpu.VMEM((8, NPOS, NPOS), BF),
        pltpu.VMEM((NPOS, OWN), F32),
        pltpu.VMEM((NPOS, OWN), BF),
        pltpu.VMEM((LEN, OWN), BF),
        pltpu.VMEM((LEN, WIDTH), F32),
        pltpu.VMEM((LEN, WIDTH), F32),
        pltpu.VMEM((LEN, 128), F32),
        pltpu.VMEM((LEN, 128), F32),
        pltpu.VMEM((LEN, WIDTH), F32),
        pltpu.VMEM((4, LEN, WIDTH), BF),
        pltpu.VMEM((4 * LEN, FF4), BF),
        pltpu.VMEM((4 * LEN, FF4), BF),
        pltpu.VMEM((LEN, WIDTH), F32),
        pltpu.VMEM((LEN, WIDTH), F32),
        pltpu.VMEM((LEN, WIDTH), F32),
        pltpu.VMEM((LEN, WIDTH), F32),
        pltpu.VMEM((2, LEN, WIDTH), BF),
        pltpu.VMEM((2, LEN, WIDTH), BF),
        pltpu.VMEM((LEN, WIDTH), BF),
        pltpu.VMEM((LEN, WIDTH), BF),
        pltpu.VMEM((4, LEN, WIDTH), BF),
        pltpu.VMEM((2, LEN, WIDTH), BF),
        pltpu.VMEM((NPOS, OWN), BF),
        pltpu.VMEM((NPOS, NPOS), BF),
        pltpu.VMEM((NZ, 2, 2, 64, 4 * OWN), BF),
        pltpu.VMEM((NZ, 2, 128, FF4), BF),
        pltpu.VMEM((NZ, 2, 128, WIDTH), BF),
        pltpu.VMEM((2, 2, 2, 64, OWN), BF),
        pltpu.VMEM((16, 8, WIDTH), F32),
        pltpu.VMEM((2, 8, OWN), F32),
        pltpu.VMEM((8, FF4), F32),
        pltpu.VMEM((16, WIDTH), F32),
        pltpu.VMEM((NZ, 2, 2, 16, 128), F32),
        pltpu.VMEM((16, 128), F32),
        [
            scatter_bufs(group, count, order)
            for group, _, count, order in pieces_of(SCATTER, WIDTHS)
        ],
        pltpu.VMEM((64, 3 * OWN), F32),
        pltpu.VMEM((64, OWN), F32),
        pltpu.VMEM((2, 64, FF4), F32),
        pltpu.VMEM((64, FF4), BF),
        pltpu.VMEM((64, FF4), BF),
        pltpu.VMEM((128, WIDTH), F32),
        pltpu.SemaphoreType.DMA((800,)),
        pltpu.SemaphoreType.DMA((90,)),
    ]
    outs = pl.pallas_call(
        layer_kernel,
        out_shape=[
            jax.ShapeDtypeStruct((LEN, WIDTH), BF),
            jax.ShapeDtypeStruct((LEN, WIDTH), F32),
            jax.ShapeDtypeStruct((64, 3 * WIDTH), F32),
            jax.ShapeDtypeStruct((64, WIDTH), F32),
            jax.ShapeDtypeStruct((64, 4 * FF4), F32),
            jax.ShapeDtypeStruct((256, WIDTH), F32),
            jax.ShapeDtypeStruct((16, 128), F32),
        ],
        in_specs=[anywhere, pl.BlockSpec(memory_space=pltpu.SMEM), anywhere]
        + [anywhere] * 4
        + [vmem] * 6,
        out_specs=[vmem, vmem] + [anywhere] * 4 + [vmem],
        scratch_shapes=scratch,
        compiler_params=pltpu.CompilerParams(
            collective_id=0, has_side_effects=True, vmem_limit_bytes=63 * MIB
        ),
        name="layer",
    )(
        tokens[0],
        doc_lengths,
        cotangent[0],
        w_qkv,
        w_out,
        w_up,
        w_down,
        qv_bias.reshape(1, 128),
        up_bias.reshape(2, 128),
        out_bias.reshape(1, 64),
        down_bias.reshape(1, 64),
        norm_gain,
        norm_bias,
    )
    *large, vec = outs
    done = pl.pallas_call(
        hand_out_kernel,
        out_shape=[jax.ShapeDtypeStruct(array.shape, array.dtype) for array in large]
        + [
            jax.ShapeDtypeStruct((1, 128), F32),
            jax.ShapeDtypeStruct((1, 64), F32),
            jax.ShapeDtypeStruct((2, 128), F32),
            jax.ShapeDtypeStruct((1, 64), F32),
            jax.ShapeDtypeStruct((4, 64), F32),
            jax.ShapeDtypeStruct((4, 64), F32),
        ],
        in_specs=[anywhere] * 6 + [vmem],
        out_specs=[anywhere] * 6 + [vmem] * 6,
        scratch_shapes=[pltpu.VMEM(array.shape, array.dtype) for array in large]
        + [pltpu.SemaphoreType.DMA((2, 6 * SPLIT))],
        name="hand_out",
    )(*large, vec)
    result, grad_inputs, grad_qkv, grad_out, grad_up, grad_down = done[:6]
    grad_qv, grad_out_shift, grad_up_shift, grad_down_shift, grad_gain, grad_shift = done[6:]
    return (
        result[None],
        grad_inputs[None],
        grad_qkv,
        grad_qv.reshape(128),
        grad_out,
        grad_out_shift.reshape(64),
        grad_up,
        grad_up_shift.reshape(256),
        grad_down,
        grad_down_shift.reshape(64),
        grad_gain,
        grad_shift,
    )


def solution(mesh):
    placed = (
        P("dp", "blk", None),
        P("dp", None),
        P("dp", "blk", None),
        P("dp", None),
        P("dp"),
        P("dp", None),
        P("dp"),
        P("dp", None),
        P("dp"),
        P("dp", None),
        P("dp"),
        P(None, "dp"),
        P(None, "dp"),
    )
    sizes = (mesh.shape["dp"], mesh.shape["blk"])
    return jax.shard_map(
        fused if sizes == (NZ * 4, 2) else shards,
        mesh=mesh,
        in_specs=placed,
        out_specs=(
            P("dp", "blk", None),
            P("dp", "blk", None),
            P("dp", None),
            P("dp"),
            P("dp", None),
            P("dp"),
            P("dp", None),
            P("dp"),
            P("dp", None),
            P("dp"),
            P(None, "dp"),
            P(None, "dp"),
        ),
        check_vma=False,
    )
```

```python
import functools
import math

import jax
import jax.numpy as jnp
from jax import lax
from jax.experimental import pallas as pl
from jax.experimental.pallas import tpu as pltpu
from jax.sharding import PartitionSpec as P

HEADS = 16
ALPHA = 32


EPSILON = 1e-05
FILLER = -1000000000.0


def normalize(values):
    center = values - jnp.mean(values, axis=-1, keepdims=True)
    inverse = lax.rsqrt(jnp.mean(center * center, axis=-1, keepdims=True) + EPSILON)
    return (center * inverse, inverse)


def norm_back(normed, inverse, gain_row, upstream):
    scaled = upstream * gain_row
    return inverse * (
        scaled
        - jnp.mean(scaled, axis=-1, keepdims=True)
        - normed * jnp.mean(scaled * normed, axis=-1, keepdims=True)
    )


def segment_of(position, doc_ends):
    return jnp.sum((position[:, None] >= doc_ends[None, :]).astype(jnp.int32), axis=1)


def gelu_tanh(values):
    return jax.nn.gelu(values, approximate=True)


def shards(
    tokens,
    doc_lengths,
    cotangent,
    w_qkv,
    qv_bias,
    w_out,
    out_bias,
    w_up,
    up_bias,
    w_down,
    down_bias,
    norm_gain,
    norm_bias,
):
    inputs = tokens[0].astype(jnp.float32)
    length = inputs.shape[0]
    model_width = inputs.shape[1]
    block_count = lax.axis_size("blk")
    seq_len = length * block_count
    offset = lax.axis_index("blk") * length
    doc_ends = jnp.cumsum(doc_lengths[0])
    filled = doc_ends[-1]
    query_pos = offset + jnp.arange(length, dtype=jnp.int32)
    query_seg = segment_of(query_pos, doc_ends)
    valid_rows = (query_pos < filled).astype(jnp.float32)
    key_seg = segment_of(jnp.arange(seq_len, dtype=jnp.int32), doc_ends)
    last_query = offset + length - 1

    def block_meets(first_row, piece_rows):
        first_at = jnp.asarray(first_row, jnp.int32)
        first_seg = lax.dynamic_index_in_dim(key_seg, first_at, keepdims=False)
        last_seg = lax.dynamic_index_in_dim(key_seg, first_at + piece_rows - 1, keepdims=False)
        return (first_at <= last_query) & (first_seg <= query_seg[-1]) & (last_seg >= query_seg[0])

    gathered = (
        lax.all_gather(w_qkv, "dp", axis=0, tiled=True),
        lax.all_gather(qv_bias, "dp", axis=0, tiled=True),
        lax.all_gather(w_out, "dp", axis=0, tiled=True),
        lax.all_gather(out_bias, "dp", axis=0, tiled=True),
        lax.all_gather(w_up, "dp", axis=0, tiled=True),
        lax.all_gather(up_bias, "dp", axis=0, tiled=True),
        lax.all_gather(w_down, "dp", axis=0, tiled=True),
        lax.all_gather(down_bias, "dp", axis=0, tiled=True),
        lax.all_gather(norm_gain, "dp", axis=1, tiled=True),
        lax.all_gather(norm_bias, "dp", axis=1, tiled=True),
    )
    (
        qkv_weight,
        qv_shift,
        out_weight,
        out_shift,
        up_weight,
        up_shift,
        down_weight,
        down_shift,
        gain_all,
        shift_all,
    ) = gathered
    gain_rows = gain_all.astype(jnp.float32)
    shift_rows = shift_all.astype(jnp.float32)
    query_scale = 1.0 / (ALPHA * math.sqrt(model_width // HEADS))
    first_hat, first_inv = normalize(inputs)
    attn_in = (first_hat * gain_rows[0] + shift_rows[0]).astype(jnp.bfloat16)
    projected = jnp.dot(attn_in, qkv_weight, preferred_element_type=jnp.float32)
    qv_float = qv_shift.astype(jnp.float32)
    queries = ((projected[:, :model_width] + qv_float[:model_width]) * query_scale).astype(
        jnp.bfloat16
    )
    keys_own = projected[:, model_width : 2 * model_width].astype(jnp.bfloat16)
    values_own = (projected[:, 2 * model_width :] + qv_float[model_width:]).astype(jnp.bfloat16)
    query_heads = queries.reshape(length, HEADS, -1)

    def scores_of(key_piece, first_row):
        piece_rows = key_piece.shape[0]
        piece_pos = first_row + jnp.arange(piece_rows, dtype=jnp.int32)
        piece_seg = lax.dynamic_slice_in_dim(key_seg, jnp.asarray(first_row, jnp.int32), piece_rows)
        allowed_pairs = (query_seg[:, None] == piece_seg[None, :]) & (
            piece_pos[None, :] <= query_pos[:, None]
        )
        raw_scores = jnp.einsum(
            "qhd,khd->hqk",
            query_heads,
            key_piece.reshape(piece_rows, HEADS, -1),
            preferred_element_type=jnp.float32,
        )
        return (jnp.where(allowed_pairs[None], raw_scores, FILLER), allowed_pairs[None])

    head_dim = model_width // HEADS
    start_state = (
        jnp.full((HEADS, length), FILLER, jnp.float32),
        jnp.zeros((HEADS, length), jnp.float32),
        jnp.zeros((HEADS, length, head_dim), jnp.float32),
    )
    accumulate_first_row = jnp.int32(0)
    accumulate_key_piece = lax.all_gather(keys_own, "blk", axis=0, tiled=True)
    accumulate_value_piece = lax.all_gather(values_own, "blk", axis=0, tiled=True)
    piece_rows = accumulate_value_piece.shape[0]

    def update(state):
        row_top, row_total, summed = state
        masked, allowed_pairs = scores_of(accumulate_key_piece, accumulate_first_row)
        new_top = jnp.maximum(row_top, jnp.max(masked, axis=2))
        factor = jnp.exp(ALPHA * (row_top - new_top))
        weights = jnp.where(allowed_pairs, jnp.exp(ALPHA * (masked - new_top[:, :, None])), 0.0)
        summed = summed * factor[:, :, None] + jnp.einsum(
            "hqk,khd->hqd",
            weights,
            accumulate_value_piece.reshape(piece_rows, HEADS, -1),
            preferred_element_type=jnp.float32,
        )
        return (new_top, row_total * factor + jnp.sum(weights, axis=2), summed)

    def unchanged(state):
        return state

    softmax_state = lax.cond(
        block_meets(accumulate_first_row, piece_rows), update, unchanged, start_state
    )
    row_top, row_total, summed = softmax_state
    attended_heads = summed / row_total[:, :, None]
    attended = jnp.transpose(attended_heads, (1, 0, 2)).reshape(length, model_width)
    attn_low = attended.astype(jnp.bfloat16)
    branch = jnp.dot(attn_low, out_weight, preferred_element_type=jnp.float32) + out_shift.astype(
        jnp.float32
    )
    second_hat, second_inv = normalize(branch)
    middle = inputs + second_hat * gain_rows[1] + shift_rows[1]
    third_hat, third_inv = normalize(middle)
    ffn_in = (third_hat * gain_rows[2] + shift_rows[2]).astype(jnp.bfloat16)
    pre_act = jnp.dot(ffn_in, up_weight, preferred_element_type=jnp.float32) + up_shift.astype(
        jnp.float32
    )
    activated, gelu_pullback = jax.vjp(gelu_tanh, pre_act)
    act_low = activated.astype(jnp.bfloat16)
    ffn_out = jnp.dot(act_low, down_weight, preferred_element_type=jnp.float32) + down_shift.astype(
        jnp.float32
    )
    fourth_hat, fourth_inv = normalize(ffn_out)
    result = middle + fourth_hat * gain_rows[3] + shift_rows[3]
    qkv_again, out_again, up_again, down_again, gain_again = (
        lax.all_gather(w_qkv, "dp", axis=0, tiled=True),
        lax.all_gather(w_out, "dp", axis=0, tiled=True),
        lax.all_gather(w_up, "dp", axis=0, tiled=True),
        lax.all_gather(w_down, "dp", axis=0, tiled=True),
        lax.all_gather(norm_gain, "dp", axis=1, tiled=True),
    )
    back_gains = gain_again.astype(jnp.float32)
    upstream = cotangent[0].astype(jnp.float32) * valid_rows[:, None]
    grad_ffn = norm_back(fourth_hat, fourth_inv, back_gains[3], upstream).astype(jnp.bfloat16)
    grad_down = jnp.einsum("tf,td->fd", act_low, grad_ffn, preferred_element_type=jnp.float32)
    grad_act = jnp.einsum("td,fd->tf", grad_ffn, down_again, preferred_element_type=jnp.float32)
    grad_pre = gelu_pullback(grad_act)[0].astype(jnp.bfloat16)
    grad_up = jnp.einsum("td,tf->df", ffn_in, grad_pre, preferred_element_type=jnp.float32)
    grad_ffn_in = jnp.einsum("tf,df->td", grad_pre, up_again, preferred_element_type=jnp.float32)
    grad_middle = upstream + norm_back(third_hat, third_inv, back_gains[2], grad_ffn_in)
    grad_branch = norm_back(second_hat, second_inv, back_gains[1], grad_middle).astype(jnp.bfloat16)
    grad_out = jnp.einsum("td,te->de", attn_low, grad_branch, preferred_element_type=jnp.float32)
    grad_attn = jnp.einsum(
        "te,de->td", grad_branch, out_again, preferred_element_type=jnp.float32
    ).astype(jnp.bfloat16)
    grad_heads = grad_attn.reshape(length, HEADS, -1)
    row_delta = jnp.einsum(
        "qhd,hqd->hq", grad_heads, attended_heads, preferred_element_type=jnp.float32
    )
    keys_all, values_all = (
        lax.all_gather(keys_own, "blk", axis=0, tiled=True),
        lax.all_gather(values_own, "blk", axis=0, tiled=True),
    )
    grad_query = jnp.zeros((length, HEADS, head_dim), jnp.float32)
    key_terms = []
    for block_index in range(block_count):
        first_row = block_index * length
        key_piece = keys_all[first_row : first_row + length]
        value_piece = values_all[first_row : first_row + length]

        def block_grads(operands):
            key_block, value_block = operands
            value_heads = value_block.reshape(length, HEADS, -1)
            masked, allowed_pairs = scores_of(key_block, first_row)
            probabilities = (
                jnp.where(allowed_pairs, jnp.exp(ALPHA * (masked - row_top[:, :, None])), 0.0)
                / row_total[:, :, None]
            )
            grad_probs = jnp.einsum(
                "qhd,khd->hqk", grad_heads, value_heads, preferred_element_type=jnp.float32
            )
            grad_scores = ALPHA * probabilities * (grad_probs - row_delta[:, :, None])
            query_term = jnp.einsum(
                "hqk,khd->qhd",
                grad_scores,
                key_block.reshape(length, HEADS, -1),
                preferred_element_type=jnp.float32,
            )
            grad_key = jnp.einsum(
                "hqk,qhd->khd", grad_scores, query_heads, preferred_element_type=jnp.float32
            )
            grad_value = jnp.einsum(
                "hqk,qhd->khd", probabilities, grad_heads, preferred_element_type=jnp.float32
            )
            return (
                query_term,
                jnp.concatenate(
                    [
                        grad_key.reshape(length, model_width),
                        grad_value.reshape(length, model_width),
                    ],
                    1,
                ),
            )

        def block_zeros(operands):
            return (
                jnp.zeros((length, HEADS, head_dim), jnp.float32),
                jnp.zeros((length, 2 * model_width), jnp.float32),
            )

        query_term, key_term = lax.cond(
            block_meets(first_row, length), block_grads, block_zeros, (key_piece, value_piece)
        )
        grad_query = grad_query + query_term
        key_terms.append(key_term)
    key_grads = lax.psum_scatter(
        jnp.concatenate(key_terms, 0).astype(jnp.bfloat16), "blk", scatter_dimension=0, tiled=True
    ).astype(jnp.float32)
    grad_keys = key_grads[:, :model_width].astype(jnp.bfloat16)
    grad_values = key_grads[:, model_width:].astype(jnp.bfloat16)
    grad_queries = grad_query.reshape(length, model_width).astype(jnp.bfloat16) * jnp.asarray(
        query_scale, jnp.bfloat16
    )
    grad_projected = jnp.concatenate([grad_queries, grad_keys, grad_values], 1)
    grad_qkv = jnp.einsum("td,te->de", attn_in, grad_projected, preferred_element_type=jnp.float32)
    grad_qv = jnp.concatenate(
        [
            jnp.sum(grad_queries.astype(jnp.float32), axis=0),
            jnp.sum(grad_values.astype(jnp.float32), axis=0),
        ]
    )
    grad_attn_in = jnp.einsum(
        "te,de->td", grad_projected, qkv_again, preferred_element_type=jnp.float32
    )
    grad_inputs = grad_middle + norm_back(first_hat, first_inv, back_gains[0], grad_attn_in)
    grad_gains = jnp.stack(
        [
            jnp.sum(grad_attn_in * first_hat, axis=0),
            jnp.sum(grad_middle * second_hat, axis=0),
            jnp.sum(grad_ffn_in * third_hat, axis=0),
            jnp.sum(upstream * fourth_hat, axis=0),
        ]
    )
    grad_shifts = jnp.stack(
        [
            jnp.sum(grad_attn_in, axis=0),
            jnp.sum(grad_middle, axis=0),
            jnp.sum(grad_ffn_in, axis=0),
            jnp.sum(upstream, axis=0),
        ]
    )
    grad_out_shift = jnp.sum(grad_branch.astype(jnp.float32), axis=0)
    grad_up_shift = jnp.sum(grad_pre.astype(jnp.float32), axis=0)
    grad_down_shift = jnp.sum(grad_ffn.astype(jnp.float32), axis=0)
    shares = (
        lax.psum_scatter(grad_qkv, "dp", scatter_dimension=0, tiled=True),
        lax.psum_scatter(grad_qv, "dp", scatter_dimension=0, tiled=True),
        lax.psum_scatter(grad_out, "dp", scatter_dimension=0, tiled=True),
        lax.psum_scatter(grad_out_shift, "dp", scatter_dimension=0, tiled=True),
        lax.psum_scatter(grad_up, "dp", scatter_dimension=0, tiled=True),
        lax.psum_scatter(grad_up_shift, "dp", scatter_dimension=0, tiled=True),
        lax.psum_scatter(grad_down, "dp", scatter_dimension=0, tiled=True),
        lax.psum_scatter(grad_down_shift, "dp", scatter_dimension=0, tiled=True),
        lax.psum_scatter(grad_gains, "dp", scatter_dimension=1, tiled=True),
        lax.psum_scatter(grad_shifts, "dp", scatter_dimension=1, tiled=True),
    )
    totals = (
        lax.psum(shares[0].astype(jnp.bfloat16), "blk").astype(jnp.float32),
        lax.psum(shares[1].astype(jnp.bfloat16), "blk").astype(jnp.float32),
        lax.psum(shares[2].astype(jnp.bfloat16), "blk").astype(jnp.float32),
        lax.psum(shares[3].astype(jnp.bfloat16), "blk").astype(jnp.float32),
        lax.psum(shares[4].astype(jnp.bfloat16), "blk").astype(jnp.float32),
        lax.psum(shares[5].astype(jnp.bfloat16), "blk").astype(jnp.float32),
        lax.psum(shares[6].astype(jnp.bfloat16), "blk").astype(jnp.float32),
        lax.psum(shares[7].astype(jnp.bfloat16), "blk").astype(jnp.float32),
        lax.psum(shares[8].astype(jnp.bfloat16), "blk").astype(jnp.float32),
        lax.psum(shares[9].astype(jnp.bfloat16), "blk").astype(jnp.float32),
    )
    return (result.astype(jnp.bfloat16)[None], grad_inputs[None]) + tuple(totals)


NZ = 4
NPOS = 512
LEN = 256
WIDTH = 1024
OWN = 512
FF4 = 1024
BF = jnp.bfloat16
F32 = jnp.float32
MESH = pl.DeviceIdType.MESH
MIB = 1 << 20
ROW_OUT, ROW_DOWN, ROW_GAIN, ROW_SHIFT = 3, 4, 5, 9
GATHER = (
    ("v", 0, "zyx"), ("q", 0, "zxy"), ("q", 1, "zyx"), ("q", 2, "zxy"),
    ("q", 3, "zyx"), ("o", 0, "zyx"), ("u", 0, "zy"), ("u", 1, "zy"),
    ("d", 0, "zy"), ("u", 2, "yz"), ("d", 1, "zy"), ("d", 2, "zy"),
    ("u", 3, "zy"), ("d", 3, "zy"),
)
GATHER_STEPS = (
    (0, 0), (1, 0), (0, 1), (2, 0), (0, 2), (1, 1), (3, 0), (0, 3),
    (-1, 0), (-1, 1), (2, 1), (4, 0), (1, 2), (3, 1), (5, 0), (7, 0),
    (4, 1), (6, 0), (2, 2), (7, 1), (8, 0), (6, 1), (5, 1), (9, 0),
    (3, 2), (1, 3), (9, 1), (12, 0), (4, 2), (2, 3), (12, 1), (9, 2),
    (7, 2), (8, 1), (10, 0), (11, 0), (3, 3), (5, 2), (6, 2), (4, 3),
    (-1, 2), (-1, 3), (-1, 4), (5, 3), (-1, 5), (-1, 7), (-1, 6), (6, 3),
    (7, 3), (8, 2), (12, 2), (-1, 8), (10, 1), (13, 0), (11, 1), (-1, 9),
    (12, 3), (9, 3), (-1, 10), (-1, 11), (-1, 12), (13, 1), (-1, 13), (-1, 14),
    (-1, 15), (10, 2), (-1, 16), (11, 2), (-1, 17), (-1, 18), (-1, 19), (13, 2),
    (-1, 20), (-1, 21), (-1, 22), (-1, 23),
)
SCATTER = (
    ("o", 0, "xyz"), ("d", 0, "zy"), ("d", 1, "yz"), ("d", 2, "yz"),
    ("u", 0, "yz"), ("u", 1, "zy"), ("q", 0, "xyz"), ("d", 3, "yz"),
    ("q", 1, "xyz"), ("q", 2, "xyz"), ("q", 3, "yxz"), ("u", 2, "yz"),
    ("q", 4, "yxz"), ("u", 3, "yz"), ("q", 5, "xyz"), ("v", 0, "xyz"),
)
SCATTER_STEPS = (
    (-1, 0), (-1, 1), (-1, 2), (-1, 25), (-1, 26), (-1, 27), (-1, 3), (-1, 4),
    (-1, 7), (-1, 8), (-1, 11), (-1, 5), (1, 0), (2, 0), (-1, 12), (-1, 6),
    (3, 0), (7, 0), (-1, 9), (5, 0), (-1, 10), (2, 1), (4, 0), (-1, 13),
    (-1, 14), (1, 1), (3, 1), (7, 1), (11, 0), (13, 0), (-1, 15), (0, 0),
    (-1, 16), (-1, 17), (1, 2), (4, 1), (-1, 18), (-1, 19), (-1, 20), (2, 2),
    (6, 0), (-1, 21), (9, 0), (10, 0), (-1, 22), (-1, 23), (0, 1), (11, 1),
    (5, 1), (8, 0), (13, 1), (-1, 24), (15, 0), (3, 2), (10, 1), (5, 2),
    (7, 2), (6, 1), (0, 2), (4, 2), (15, 1), (9, 1), (5, 3), (12, 0),
    (14, 0), (6, 2), (15, 2), (4, 3), (10, 2), (11, 2), (8, 1), (13, 2),
    (9, 2), (15, 3), (11, 3), (14, 1), (12, 1), (13, 3), (8, 2), (6, 3),
    (10, 3), (14, 2), (0, 3), (12, 2), (9, 3), (8, 3), (14, 3), (12, 3),
)
WIDTHS = {"v": 128, "q": 3 * OWN, "o": OWN, "u": FF4, "d": WIDTH}


def dot_nn(a, b):
    return lax.dot_general(a, b, (((1,), (0,)), ((), ())), preferred_element_type=F32)


def dot_nt(a, b):
    return lax.dot_general(a, b, (((1,), (1,)), ((), ())), preferred_element_type=F32)


def dot_tn(a, b):
    return lax.dot_general(a, b, (((0,), (0,)), ((), ())), preferred_element_type=F32)


def loop(count, body):
    lax.fori_loop(0, count, lambda index, carry: (body(index), carry)[1], 0)


def mul(index, size):
    return pl.multiple_of(index * size, size)


class Net:
    def __init__(self, sems):
        self.chip = lax.axis_index("dp")
        self.core = lax.axis_index("blk")
        self.z = self.chip // 4
        self.y = (self.chip // 2) % 2
        self.x = self.chip % 2
        self.sems = sems
        self.used = 0
        self.unsent = []

    def sem(self):
        self.used += 1
        return self.sems.at[self.used - 1]

    def chip_at(self, z, y, x):
        return z * 4 + y * 2 + x

    def peers(self, dim):
        if dim == "x":
            return [(1, self.z, self.y, 1 - self.x, self.core)]
        if dim == "y":
            return [(1, self.z, 1 - self.y, self.x, self.core)]
        if dim == "c":
            return [(1, self.z, self.y, self.x, 1 - self.core)]
        return [(k, (self.z + k) % NZ, self.y, self.x, self.core) for k in range(1, NZ)]

    def send(self, src, dst, recv, peer):
        _, z, y, x, core = peer
        copy = pltpu.make_async_remote_copy(
            src_ref=src,
            dst_ref=dst,
            send_sem=self.sem(),
            recv_sem=recv,
            device_id=(self.chip_at(z, y, x), core),
            device_id_type=MESH,
        )
        copy.start()
        self.unsent.append(copy)
        return copy

    @staticmethod
    def drain(sends, waited):
        for copy in sends:
            if not any(copy is other for other in waited):
                copy.wait_send()

    def sibling(self, src, dst):
        return self.send(src, dst, self.sem(), self.peers("c")[0])

    def greet(self):
        barrier = pltpu.get_barrier_semaphore()
        count = 0
        for dim in "xyzc":
            for _, z, y, x, core in self.peers(dim):
                pl.semaphore_signal(
                    barrier, inc=1, device_id=(self.chip_at(z, y, x), core), device_id_type=MESH
                )
                count += 1
        return lambda: pl.semaphore_wait(barrier, count)


def await_bytes(view, sem):
    pltpu.make_async_copy(view, view, sem).wait()


def view_of(net, ref, lanes, **given):
    where = {"z": net.z, "y": net.y, "x": net.x}
    where.update(given)
    return ref.at[where["z"], where["y"], where["x"], :, lanes]


ALL = slice(None)


def gather_stages(net, ref, lanes, order):
    first, second, third = order
    others = {"z": pl.ds(0, NZ - 1), "y": 1 - net.y, "x": 1 - net.x}
    got_first, got_second, got_near, got_far = net.sem(), net.sem(), net.sem(), net.sem()

    def pass_on(dim, sem, **held):
        blocks = view_of(net, ref, lanes, **held)
        for peer in net.peers(dim):
            net.send(blocks, blocks, sem, peer)

    def start():
        pass_on(first, got_first)

    def after_first():
        await_bytes(view_of(net, ref, lanes, **{first: others[first]}), got_first)
        pass_on(second, got_second, **{first: ALL})
        pass_on(third, got_near, **{first: ALL})

    def after_second():
        held = {first: ALL, second: others[second]}
        await_bytes(view_of(net, ref, lanes, **held), got_second)
        if second == "z":
            for peer in net.peers("z"):
                pass_on(third, got_far, **{first: ALL, "z": peer[1]})
        else:
            pass_on(third, got_far, **held)

    def finish():
        held = {first: ALL, third: others[third]}
        await_bytes(view_of(net, ref, lanes, **held), got_near)
        held[second] = others[second]
        await_bytes(view_of(net, ref, lanes, **held), got_far)

    return start, after_first, after_second, finish


def scatter_stages(net, ref, lanes, order, bufs, done):
    first, second, third = order
    wide, half, line = bufs
    got_wide, got_half, got_line = net.sem(), net.sem(), net.sem()
    dtype = wide.dtype
    rows, cols = wide.shape[-2:]
    step = min(rows, max(16, 32768 // cols))
    size = {"z": NZ, "y": 2, "x": 2}
    place = {"z": 0, "y": 1, "x": 2}
    mine = {"z": net.z, "y": net.y, "x": net.x}

    def coordinate(dim, peer):
        return peer[1 + place[dim]]

    def block_add(target, sources):
        for part in range(rows // step):
            here = pl.ds(part * step, step)
            total = ref[(*target, here, lanes)].astype(F32)
            for buf, at in sources:
                total = total + buf[(*at, here)].astype(F32)
            ref[(*target, here, lanes)] = total.astype(dtype)

    def target_of(**given):
        where = dict(mine)
        where.update(given)
        return (where["z"], where["y"], where["x"])

    def start():
        for peer in net.peers(first):
            there = {"z": ALL, "y": ALL, "x": ALL, first: coordinate(first, peer)}
            net.send(view_of(net, ref, lanes, **there), wide.at[peer[0] - 1], got_wide, peer)

    def after_first():
        await_bytes(wide, got_wide)
        left = [dim for dim in "zyx" if dim != first]

        def add(second_at, third_at):
            at = {second: second_at, third: third_at}
            place_in = (0, at[left[0]], at[left[1]])
            block_add(target_of(**at), [(wide, place_in)])

        for peer in net.peers(second):
            gone = coordinate(second, peer)
            loop(size[third], lambda other: add(gone, other))
            blocks = view_of(net, ref, lanes, **{second: gone, third: ALL})
            net.send(blocks, half.at[peer[0] - 1], got_half, peer)
        loop(size[third], lambda other: add(mine[second], other))

    def after_second():
        await_bytes(half, got_half)
        for peer in net.peers(third):
            gone = coordinate(third, peer)
            block_add(
                target_of(**{third: gone}), [(half, (k, gone)) for k in range(size[second] - 1)]
            )
            blocks = view_of(net, ref, lanes, **{third: gone})
            net.send(blocks, line.at[peer[0] - 1], got_line, peer)

    def finish():
        await_bytes(line, got_line)
        for part in range(rows // step):
            here = pl.ds(part * step, step)
            total = ref[(*target_of(), here, lanes)].astype(F32)
            for k in range(size[second] - 1):
                total = total + half[k, mine[third], here].astype(F32)
            for k in range(size[third] - 1):
                total = total + line[k, here].astype(F32)
            done(part * step, step, total)

    return start, after_first, after_second, finish


def plane_gather_stages(net, ref, lanes, order):
    first, second = order
    others = {"z": pl.ds(0, NZ - 1), "y": 1 - net.y}
    got_first, got_second = net.sem(), net.sem()

    def place(**given):
        where = {"z": net.z, "y": net.y}
        where.update(given)
        return ref.at[where["z"], where["y"], :, lanes]

    def pass_on(dim, sem, **held):
        for peer in net.peers(dim):
            net.send(place(**held), place(**held), sem, peer)

    def start():
        pass_on(first, got_first)

    def after_first():
        await_bytes(place(**{first: others[first]}), got_first)
        pass_on(second, got_second, **{first: ALL})

    def finish():
        await_bytes(place(**{first: ALL, second: others[second]}), got_second)

    return [start, after_first, finish]


def plane_scatter_stages(net, ref, lanes, order, bufs, emit):
    first, second = order
    wide, line = bufs[:2]
    got_wide, got_line = net.sem(), net.sem()
    rows, cols = wide.shape[-2:]
    step = min(rows, max(16, 32768 // cols))
    size = {"z": NZ, "y": 2}
    place = {"z": 1, "y": 2}
    mine = {"z": net.z, "y": net.y}

    def at(**given):
        where = dict(mine)
        where.update(given)
        return (where["z"], where["y"])

    def start():
        for peer in net.peers(first):
            there = at(**{first: peer[place[first]], second: ALL})
            net.send(ref.at[(*there, ALL, lanes)], wide.at[peer[0] - 1], got_wide, peer)

    def total(where, slot, here):
        value = ref[(*where, here, lanes)].astype(F32)
        for k in range(size[first] - 1):
            value = value + wide[k, slot, here].astype(F32)
        return value

    def after_first():
        await_bytes(wide, got_wide)
        for peer in net.peers(second):
            gone = peer[place[second]]
            there = at(**{second: gone})

            def add(part):
                here = pl.ds(mul(part, step), step)
                ref[(*there, here, lanes)] = total(there, gone, here).astype(BF)

            loop(rows // step, add)
            net.send(ref.at[(*there, ALL, lanes)], line.at[peer[0] - 1], got_line, peer)

    def final(here):
        value = total(at(), mine[second], here)
        for k in range(size[second] - 1):
            value = value + line[k, here].astype(F32)
        return value

    def finish():
        await_bytes(line, got_line)
        emit(final)

    return [start, after_first, finish]


def pieces_of(plan, widths):
    counts = {}
    for group, _, _ in plan:
        counts[group] = counts.get(group, 0) + 1
    return [
        (group, index * (widths[group] // counts[group]), widths[group] // counts[group], order)
        for group, index, order in plan
    ]


def layer_kernel(
    tok_in,
    doc,
    cot_in,
    wq_in,
    wo_in,
    wu_in,
    wd_in,
    qv_in,
    up_in,
    out_in,
    down_in,
    gain_in,
    shift_in,
    res_out,
    gtok_out,
    gq_out,
    go_out,
    gu_out,
    gd_out,
    gvec_out,
    wq,
    wo,
    wu,
    wux,
    wd,
    vbuf,
    tok,
    cot,
    pack,
    vecs,
    vq,
    vu,
    xin,
    qb,
    kb,
    vb,
    pb,
    bias,
    att,
    attb,
    attx,
    hat1,
    hat2,
    inv1,
    inv2,
    mid,
    fin,
    act,
    dge,
    rcv,
    own,
    snd,
    own_x,
    snd_s,
    rcv_s,
    snd_x,
    rcv_x,
    gff,
    gbr,
    dob,
    dsb,
    gqo,
    gu,
    gd,
    swap,
    acc,
    acc_qv,
    acc_up,
    gvecs,
    gv,
    vother,
    piece_bufs,
    st_q,
    st_o,
    st_u,
    st_ux,
    r_ux,
    st_d,
    sems,
    local_sems,
):
    net = Net(sems)
    core = net.core
    greeted = net.greet()

    locals_ = []

    def fetch(src, dst):
        copy = pltpu.make_async_copy(src, dst, local_sems.at[len(locals_)])
        copy.start()
        locals_.append(copy)

    def lanes_of(start, size):
        return pl.ds(pl.multiple_of(start, 128), size)

    for part in range(3):
        fetch(
            wq_in.at[:, lanes_of(part * WIDTH + core * OWN, OWN)],
            wq.at[net.z, net.y, net.x, :, pl.ds(part * OWN, OWN)],
        )
    fetch(wo_in.at[:, lanes_of(core * OWN, OWN)], wo.at[core, net.z, net.y, net.x])
    for zy in range(8):
        fetch(
            wu_in.at[:, lanes_of((zy * 2 + 1 - net.x) * 256 + core * 128, 128)],
            wux.at[:, pl.ds(zy * 128, 128)],
        )
    own_half = pl.ds(mul(net.x, 64), 64)
    for zy in range(8):
        fetch(
            wu_in.at[:, lanes_of((zy * 2 + net.x) * 256 + core * 128, 128)],
            wu.at[net.z, net.y, own_half, pl.ds(zy * 128, 128)],
        )
    fetch(wd_in.at[pl.ds(mul(core, 128), 128), :], wd.at[net.z, net.y])
    fetch(tok_in, tok)
    fetch(cot_in, cot)
    pack[...] = jnp.zeros_like(pack)
    pack[0:1, :] = qv_in[...].astype(F32)
    pack[1:3, :] = up_in[...].astype(F32)
    for row, ref in (
        (ROW_OUT, out_in),
        (ROW_DOWN, down_in),
        (ROW_GAIN, gain_in),
        (ROW_SHIFT, shift_in),
    ):
        value = ref[...].astype(F32)
        rows = slice(row, row + value.shape[0])
        pack[rows, 0:64] = jnp.where(net.x == 0, value, 0.0)
        pack[rows, 64:128] = jnp.where(net.x == 1, value, 0.0)
    vbuf[net.z, net.y, net.x] = pack[...].astype(BF)
    wo_own = wo.at[core]
    plan = pieces_of(GATHER, WIDTHS)
    sources = {"v": vbuf, "q": wq, "o": wo_own}

    def stages_of(group, lanes, order):
        if group == "d":
            return plane_gather_stages(net, wd, lanes, order)
        if group == "u":
            passing = plane_gather_stages(net, wu, lanes, order)
            got_x = net.sem()

            def cross():
                net.send(
                    wux.at[:, lanes],
                    wu.at[net.z, net.y, own_half, lanes],
                    got_x,
                    net.peers("x")[0],
                )

            def crossed():
                await_bytes(wux.at[:, lanes], got_x)
                passing[0]()

            return [cross, crossed, *passing[1:]]
        return gather_stages(net, sources[group], lanes, order)

    gathers = [
        stages_of(group, pl.ds(lane0, count), order) for group, lane0, count, order in plan
    ]
    greeted()
    ready = {("q", 0): 3, ("o", 0): 4, ("u", 0): 12, ("u", 1): 20, ("d", 0): 21}
    state = {"landed": 0}
    got_wo = []

    def gather(piece, stage):
        while state["landed"] < ready.get((plan[piece][0], stage), 0):
            locals_[state["landed"]].wait()
            state["landed"] += 1
        gathers[piece][stage]()
        group, lane0, count, _ = plan[piece]
        if group == "o" and stage == 3:
            half = wo_own.at[:, :, :, :, pl.ds(lane0, count)]
            got_wo.append(net.sibling(half, half))

    def spread_vectors():
        for z in range(NZ):
            for y in range(2):
                both = vbuf[z, y, 0].astype(F32) + vbuf[z, y, 1].astype(F32)
                vecs[:, pl.ds((z * 2 + y) * 128, 128)] = both
        for y in range(2):
            for x in range(2):
                at = pl.ds((y * 2 + x) * 128, 128)
                vq[0:8, at] = vbuf[core, y, x].astype(F32)[0:8]
                vq[8:16, at] = vbuf[core + 2, y, x].astype(F32)[0:8]
        for z in range(NZ):
            for y in range(2):
                block = vbuf[z, y, net.x].astype(F32)
                vu[0:1, pl.ds((z * 2 + y) * 128, 128)] = jnp.where(
                    core == 0, block[1:2], block[2:3]
                )
        acc[...] = jnp.zeros_like(acc)
        acc_up[...] = jnp.zeros_like(acc_up)

    def gain(n):
        return vecs[ROW_GAIN + n : ROW_GAIN + n + 1, :]

    def shift(n):
        return vecs[ROW_SHIFT + n : ROW_SHIFT + n + 1, :]

    def accumulate(row, value):
        parts = value.reshape(value.shape[0] // 8, 8, value.shape[1])
        acc[row] += jnp.sum(parts, axis=0)

    got = {}

    chunk = 32
    chunks = LEN // chunk

    def ln0(i):
        here = pl.ds(mul(i, chunk), chunk)
        hat, _ = normalize(tok[here, :].astype(F32))
        xin[core, here, :] = (hat * gain(0) + shift(0)).astype(BF)

    def attention_input():
        locals_[21].wait()
        loop(chunks, ln0)
        got["x"] = net.sibling(xin.at[core], xin.at[core])

    ends = []
    end = jnp.int32(0)
    for j in range(8):
        end = end + doc[0, j]
        ends.append(end)

    def segment(position):
        total = jnp.zeros(position.shape, jnp.int32)
        for value in ends:
            total = total + (position >= value).astype(jnp.int32)
        return total

    scale = 1.0 / (ALPHA * 8.0)

    def project(t):
        n = t // 2
        m = t % 2
        tile = pl.ds(mul(n, 256), 256)
        rows = pl.ds(mul(m, 256), 256)

        def part(index, dst, bias, factor):
            weight = wq[:, :, :, :, pl.ds(pl.multiple_of(index * OWN + n * 256, 256), 256)]
            value = dot_nn(xin[m], weight.reshape(WIDTH, 256))
            if bias is not None:
                value = value + vq[bias : bias + 1, tile]
            if factor is not None:
                value = value * factor
            dst[rows, tile] = value.astype(BF)

        part(0, qb, 0, scale)
        part(1, kb, None, None)
        part(2, vb, 8, None)

    def projections():
        got["x"].wait_recv()
        loop(4, project)

    lane = lax.broadcasted_iota(jnp.int32, (1, 128), 1)
    block = 128

    def masks():
        for r in range(NPOS // block):
            count = (r + 1) * block
            q_pos = r * block + lax.broadcasted_iota(jnp.int32, (block, 1), 0)
            k_pos = lax.broadcasted_iota(jnp.int32, (1, count), 1)
            allowed = (segment(q_pos) == segment(k_pos)) & (k_pos <= q_pos)
            bias[r * block : (r + 1) * block, 0:count] = jnp.where(allowed, 0.0, FILLER)

    def attend(half, pair):
        at = pl.ds(mul(pair, 128), 128)
        for r in (half, half + 2):
            rows = pl.ds(r * block, block)
            count = (r + 1) * block
            q = qb[rows, at]
            k = kb[0:count, at]
            v = vb[0:count, at]
            outs = []
            for head in range(2):
                mine = (lane < 64) if head == 0 else (lane >= 64)
                scores = dot_nt(jnp.where(mine, q, jnp.zeros_like(q)), k) + bias[rows, 0:count]
                top = jnp.max(scores, axis=1, keepdims=True)
                weights = jnp.exp2((scores - top) * (ALPHA * math.log2(math.e)))
                summed = dot_nn(weights.astype(BF), jnp.where(mine, v, jnp.ones_like(v)))
                turned = pltpu.roll(summed, 64, 1)
                inverse = 1.0 / jnp.where(mine, turned, summed)
                wide = jnp.concatenate([inverse] * (r + 1), axis=1)
                pb[pair * 2 + head, rows, 0:count] = (weights * wide).astype(BF)
                outs.append(summed * inverse)
            out = jnp.where(lane < 64, outs[0], outs[1])
            att[rows, at] = out
            attb[rows, at] = out.astype(BF)

    other_rows = pl.ds(mul(1 - core, LEN), LEN)
    own_rows = pl.ds(mul(core, LEN), LEN)
    got_att = []

    def half_rows(of_core, half):
        return pl.ds(pl.multiple_of(of_core * LEN + half * block, block), block)

    def attend_some(half, pair0):
        loop(2, lambda i: attend(half, i + pair0))
        if pair0 == 2:
            sent = attb.at[half_rows(1 - core, half), :]
            got_att.append(net.sibling(sent, attx.at[pl.ds(half * block, block), :]))

    own_group = net.x * 2 + core
    across_group = (1 - net.x) * 2 + core

    def branch_tile(half, n):
        lanes = pl.ds(mul(n % 2, 256), 256)
        mine = wo[n // 2, pl.ds(2 * core, 2), :, :, :, lanes].reshape(OWN, 256)
        theirs = wo[n // 2, pl.ds(2 * (1 - core), 2), :, :, :, lanes].reshape(OWN, 256)
        at = pl.ds(mul(n, 256), 256)
        here = pl.ds(half * block, block)
        value = dot_nn(attb[half_rows(core, half), :], mine)
        own[here, at] = value + dot_nn(attx[here, :], theirs)

    def ln12(i):
        here = pl.ds(mul(i, chunk), chunk)
        first, first_inv = normalize(own[here, :] + vecs[ROW_OUT : ROW_OUT + 1, :])
        hat1[here, :] = first
        inv1[here, :] = jnp.broadcast_to(first_inv, (chunk, 128))
        middle = tok[here, :].astype(F32) + first * gain(1) + shift(1)
        mid[here, :] = middle
        second, second_inv = normalize(middle)
        hat2[here, :] = second
        inv2[here, :] = jnp.broadcast_to(second_inv, (chunk, 128))
        fin[own_group, here, :] = (second * gain(2) + shift(2)).astype(BF)

    class Share:
        def __init__(self, ref):
            self.ref = ref
            self.beside, self.across, self.passed = [], [], []

        def send(self, half):
            rows = pl.ds(half * 128, 128)
            view = self.ref.at[own_group, rows]
            self.beside.append(net.sibling(view, view))
            self.across.append(net.send(view, view, net.sem(), net.peers("x")[0]))

        def pass_on(self, half):
            self.across[half].wait_recv()
            view = self.ref.at[across_group, pl.ds(half * 128, 128)]
            self.passed.append(net.sibling(view, view))

        def wait_beside(self):
            for copy in self.beside:
                copy.wait_recv()

        def wait_passed(self):
            for copy in self.passed:
                copy.wait_recv()
            self.passed = []

    class Reduce:
        def __init__(self, product):
            self.product = product
            self.beside, self.across = [], []

        def group_rows(self, group):
            return pl.ds(mul(group, LEN), LEN)

        def multiply_here(self, n):
            at = pl.ds(n * 256, 256)
            value = self.product(self.group_rows(net.x * 2 + 1 - core), n)
            snd_s[net.x, :, at] = value.astype(BF)
            own[:, at] = self.product(self.group_rows(own_group), n)

        def multiply_there(self, n):
            at = pl.ds(n * 256, 256)
            value = self.product(self.group_rows((1 - net.x) * 2 + 1 - core), n)
            snd_s[1 - net.x, :, at] = value.astype(BF)
            self.beside.append(net.sibling(snd_s.at[:, :, at], rcv_s.at[:, :, at]))
            own_x[:, at] = self.product(self.group_rows(across_group), n)

        def multiply(self, n):
            self.multiply_here(n)
            self.multiply_there(n)

        def cross(self, n):
            at = pl.ds(n * 256, 256)
            self.beside[n].wait_recv()

            def add(i):
                here = pl.ds(mul(i, 64), 64)
                over = own_x[here, at] + rcv_s[1 - net.x, here, at].astype(F32)
                snd_x[here, at] = over.astype(BF)
                own[here, at] += rcv_s[net.x, here, at].astype(F32)

            loop(4, add)
            self.across.append(
                net.send(snd_x.at[:, at], rcv_x.at[:, at], net.sem(), net.peers("x")[0])
            )

        def wait(self):
            for copy in self.across:
                copy.wait_recv()

        def free(self):
            for copy in self.beside + self.across:
                copy.wait_send()

    share_fin, share_gff = Share(fin), Share(gff)

    def branch_half(half):
        got_att[half].wait_recv()
        if half == 0:
            loop(2, lambda i: branch_tile(half, core * 2 + i))
            for part in got_wo:
                part.wait_recv()
            loop(2, lambda i: branch_tile(half, (1 - core) * 2 + i))
        else:
            loop(4, functools.partial(branch_tile, half))
        loop(chunks // 2, lambda i: ln12(i + half * (chunks // 2)))
        share_fin.send(half)

    root = math.sqrt(2.0 / math.pi)

    def up_tile(n, group):
        at = pl.ds(mul(n, 256), 256)
        rows = pl.ds(mul(group, LEN), LEN)
        u = dot_nn(fin[group], wu[:, :, :, at].reshape(WIDTH, 256)) + vu[0:1, at]
        square = u * u
        inner = jnp.tanh(root * (u + 0.044715 * (square * u)))
        half = 0.5 * (1.0 + inner)
        act[rows, at] = (u * half).astype(BF)
        slope = 0.5 * u * (1.0 - inner * inner) * (root * (1.0 + (3 * 0.044715) * square))
        dge[rows, at] = (half + slope).astype(BF)

    def up_group(group):
        loop(4, lambda n: up_tile(n, group))

    def up_beside():
        share_fin.wait_beside()
        up_group(net.x * 2 + 1 - core)

    def up_last():
        share_fin.wait_passed()
        up_group((1 - net.x) * 2 + 1 - core)

    def down_product(rows, n):
        return dot_nn(act[rows, :], wd[:, :, :, pl.ds(n * 256, 256)].reshape(FF4, 256))

    down = Reduce(down_product)

    def tiles_of(width, count, body):
        return [functools.partial(body, lane0, count) for lane0 in range(0, width, count)]

    def attention_input_and_masks():
        attention_input()
        masks()

    steps = [
        spread_vectors,
        attention_input_and_masks,
        projections,
        lambda: attend_some(0, 0),
        lambda: attend_some(0, 2),
        lambda: attend_some(1, 0),
        lambda: attend_some(1, 2),
        lambda: branch_half(0),
        lambda: branch_half(1),
        lambda: share_fin.pass_on(0),
        lambda: share_fin.pass_on(1),
    ]
    steps += [
        lambda: up_group(own_group),
        up_beside,
        lambda: up_group(across_group),
        up_last,
        functools.partial(down.multiply, 0),
        functools.partial(down.multiply, 1),
        functools.partial(down.cross, 0),
        functools.partial(down.multiply, 2),
        functools.partial(down.cross, 1),
        functools.partial(down.multiply, 3),
        functools.partial(down.cross, 2),
        functools.partial(down.cross, 3),
    ]
    filled = ends[-1]

    def upstream_of(i):
        here = pl.ds(mul(i, chunk), chunk)
        position = core * LEN + i * chunk + lax.broadcasted_iota(jnp.int32, (chunk, 1), 0)
        return cot[here, :].astype(F32) * (position < filled).astype(F32)

    def top_tile(i):
        here = pl.ds(mul(i, chunk), chunk)
        value = own[here, :] + rcv_x[here, :].astype(F32) + vecs[ROW_DOWN : ROW_DOWN + 1, :]
        hat, inv = normalize(value)
        res_out[here, :] = (mid[here, :] + hat * gain(3) + shift(3)).astype(BF)
        upstream = upstream_of(i)
        grad = norm_back(hat, inv, gain(3), upstream).astype(BF)
        gff[own_group, here, :] = grad
        accumulate(ROW_GAIN + 3, upstream * hat)
        accumulate(ROW_SHIFT + 3, upstream)
        accumulate(ROW_DOWN, grad.astype(F32))

    def top():
        locals_[22].wait()
        down.wait()
        for half in range(2):
            loop(chunks // 2, lambda i: top_tile(i + half * (chunks // 2)))
            share_gff.send(half)

    steps.append(top)
    for piece, stage in GATHER_STEPS:
        if piece < 0:
            steps[stage]()
        else:
            gather(piece, stage)


    out_copies = []

    def deliver(src, dst):
        copy = pltpu.make_async_copy(src, dst, local_sems.at[23 + len(out_copies)])
        copy.start()
        out_copies.append((copy, net.sibling(src, dst)))

    def ship(group, lane0, count):
        if group == "d":
            at = pl.ds(lane0, count)
            deliver(st_d.at[:, at], gd_out.at[pl.ds(mul(core, 128), 128), at])
        if group == "u":
            for part in range(2):
                for zy in range(lane0 // 128, (lane0 + count) // 128):
                    deliver(
                        st_u.at[part, :, pl.ds(zy * 128, 128)],
                        gu_out.at[:, lanes_of((zy * 2 + part) * 256 + core * 128, 128)],
                    )
        if group == "o":
            deliver(
                st_o.at[:, pl.ds(lane0, count)], go_out.at[:, lanes_of(core * OWN + lane0, count)]
            )
        if group == "q":
            start = (lane0 // OWN) * WIDTH + lane0 % OWN
            deliver(
                st_q.at[:, pl.ds(lane0, count)], gq_out.at[:, lanes_of(core * OWN + start, count)]
            )

    plan = pieces_of(SCATTER, WIDTHS)
    sums = {"o": gqo, "q": gqo, "v": gv}
    stage_of = {"o": st_o, "q": st_q, "v": gvec_out}

    def store_to(stage, lane0, count):
        def done(row0, size, total):
            stage[row0 : row0 + size, lane0 : lane0 + count] = total

        return done

    def sums_of(group, lane0, count, order, bufs):
        lanes = pl.ds(lane0, count)
        if group == "d":

            def keep(total):
                for part in range(4):
                    here = pl.ds(part * 32, 32)
                    st_d[here, lanes] = total(here)

            return plane_scatter_stages(net, gd, lanes, order, bufs, keep)
        if group == "u":
            got_x = net.sem()

            def cross(total):
                for part in range(2):
                    here = pl.ds(part * 32, 32)
                    theirs = pl.multiple_of((1 - net.x) * 64 + part * 32, 32)
                    st_ux[here, lanes] = total(pl.ds(theirs, 32)).astype(BF)
                net.send(st_ux.at[:, lanes], r_ux.at[:, lanes], got_x, net.peers("x")[0])
                for part in range(2):
                    here = pl.ds(part * 32, 32)
                    mine = pl.multiple_of(net.x * 64 + part * 32, 32)
                    st_u[net.x, here, lanes] = total(pl.ds(mine, 32))

            def crossed():
                await_bytes(r_ux.at[:, lanes], got_x)
                st_u[1 - net.x, :, lanes] = r_ux[:, lanes].astype(F32)

            return [*plane_scatter_stages(net, gu, lanes, order, bufs, cross), crossed]
        base = 3 * OWN if group == "o" else 0
        return scatter_stages(
            net,
            sums[group],
            pl.ds(base + lane0, count),
            order,
            bufs,
            store_to(stage_of[group], lane0, count),
        )

    scatters = [
        sums_of(*piece, bufs) for piece, bufs in zip(plan, piece_bufs, strict=True)
    ]

    def scatter(piece, stage):
        scatters[piece][stage]()
        if stage == len(scatters[piece]) - 1:
            ship(*plan[piece][:3])

    def over_rows(chip_x, left, right, out, at, count, add):
        groups = pl.ds(chip_x * 2, 2)

        def tile(z):
            a, b = left(groups, pl.ds(mul(z, 256), 256)), right(groups, at)
            value = dot_tn(a.reshape(NPOS, 256), b.reshape(NPOS, count)).reshape(2, 128, count)
            if add:
                value = value + out[z, :, :, at].astype(F32)
            out[z, :, :, at] = value.astype(BF)

        loop(NZ, tile)

    def rows_of(ref):
        return lambda groups, at: ref[pl.ds(mul(groups.start, LEN), NPOS), at]

    def groups_of(ref):
        return lambda groups, at: ref[groups, :, at]

    def gdown_piece(chip_x, add, lane0, count):
        at = pl.ds(lane0, count)
        if add:
            share_gff.wait_passed()
        over_rows(chip_x, rows_of(act), groups_of(gff), gd, at, count, add)

    def gpre_tile(group, z):
        at = pl.ds(mul(z, 256), 256)
        rows = pl.ds(mul(group, LEN), LEN)
        weight = wd[z].reshape(256, WIDTH)
        value = dot_nt(gff[group], weight) * dge[rows, at].astype(F32)
        value = value.astype(BF)
        dge[rows, at] = value
        acc_up[:, at] += jnp.sum(value.astype(F32).reshape(32, 8, 256), axis=0)

    def gpre_group(group):
        loop(NZ, functools.partial(gpre_tile, group))

    def gpre_beside():
        share_gff.wait_beside()
        gpre_group(net.x * 2 + 1 - core)

    def gpre_last():
        share_gff.wait_passed()
        gpre_group((1 - net.x) * 2 + 1 - core)

    def gup_piece(chip_x, add, lane0, count):
        at = pl.ds(lane0, count)
        over_rows(chip_x, groups_of(fin), rows_of(dge), gu, at, count, add)

    def grad_ffn_in_product(rows, n):
        return dot_nt(dge[rows, :], wu[n].reshape(256, FF4))

    gfi = Reduce(grad_ffn_in_product)

    def grad_ffn_in_here():
        down.free()
        for n in range(4):
            gfi.multiply_here(n)

    def grad_ffn_in_there():
        for n in range(4):
            gfi.multiply_there(n)

    def grad_ffn_in_cross():
        for n in range(4):
            gfi.cross(n)

    def middle_tile(i):
        here = pl.ds(mul(i, chunk), chunk)
        grad_in = own[here, :] + rcv_x[here, :].astype(F32)
        second = hat2[here, :]
        accumulate(ROW_GAIN + 2, grad_in * second)
        accumulate(ROW_SHIFT + 2, grad_in)
        grad_mid = upstream_of(i) + norm_back(second, inv2[here, 0:1], gain(2), grad_in)
        mid[here, :] = grad_mid
        first = hat1[here, :]
        accumulate(ROW_GAIN + 1, grad_mid * first)
        accumulate(ROW_SHIFT + 1, grad_mid)
        grad = norm_back(first, inv1[here, 0:1], gain(1), grad_mid).astype(BF)
        gbr[core, here, :] = grad
        accumulate(ROW_OUT, grad.astype(F32))

    def grad_middle():
        gfi.wait()
        loop(chunks, middle_tile)
        got["gbr"] = net.sibling(gbr.at[core], gbr.at[core])

    go = gqo.at[:, :, :, :, pl.ds(3 * OWN, OWN)]

    def gout_tile(k, cols, put):
        left = attb[:, pl.ds(mul(k, 256), 256)]
        grad = gbr[:, :, cols].reshape(NPOS, OWN)
        put(k, dot_tn(left, grad).astype(BF).reshape(2, 2, 64, OWN))

    def put_swap(k, value):
        swap[k] = value

    def put_own(k, value):
        gqo[2 * core + k, :, :, :, pl.ds(3 * OWN, OWN)] = value


    def gatt_tile(t):
        k = t // 2
        m = t % 2
        left = wo[0, 2 * core + k].reshape(256, OWN)
        right = wo[1, 2 * core + k].reshape(256, OWN)
        value = dot_nt(gbr[m, :, 0:OWN], left) + dot_nt(gbr[m, :, OWN:WIDTH], right)
        dob[pl.ds(mul(m, 256), 256), pl.ds(mul(k, 256), 256)] = value.astype(BF)

    def grad_out():
        got["gbr"].wait_recv()
        loop(2, lambda k: gout_tile(k, lanes_of((1 - core) * OWN, OWN), put_swap))
        got["swap"] = net.sibling(swap, go.at[pl.ds(2 * core, 2)])
        loop(2, lambda k: gout_tile(k, lanes_of(core * OWN, OWN), put_own))
        loop(4, gatt_tile)

    def attend_back(pair):
        at = pl.ds(mul(pair, 128), 128)
        sums = []
        for head in range(2):
            mine = (lane < 64) if head == 0 else (lane >= 64)
            queries_ = []
            for r in range(NPOS // block):
                rows = pl.ds(r * block, block)
                count = (r + 1) * block
                grad = dob[rows, at]
                grad = jnp.where(mine, grad, jnp.zeros_like(grad))
                delta = jnp.sum(grad.astype(F32) * att[rows, at], axis=1, keepdims=True)
                probs = pb[pair * 2 + head, rows, 0:count].astype(F32)
                grad_probs = dot_nt(grad, vb[0:count, at])
                scores = (probs * (grad_probs - delta)).astype(BF)
                dsb[rows, 0:count] = scores
                queries_.append(dot_nn(scores, kb[0:count, at]))
            keys_, values_ = [], []
            for r in range(NPOS // block):
                rows = pl.ds(r * block, NPOS - r * block)
                cols = pl.ds(r * block, block)
                keys_.append(dot_tn(dsb[rows, cols], qb[rows, at]))
                values_.append(dot_tn(pb[pair * 2 + head, rows, cols], dob[rows, at]))
            sums.append((queries_, keys_, values_))
        total_q = jnp.zeros((8, 128), F32)
        total_v = jnp.zeros((8, 128), F32)
        for r in range(NPOS // block):
            rows = pl.ds(r * block, block)
            merged = [
                (jnp.where(lane < 64, sums[0][i][r], sums[1][i][r]) * power).astype(BF)
                for i, power in enumerate((float(ALPHA), float(ALPHA), 1.0))
            ]
            grad_q = merged[0] * jnp.asarray(scale, BF)
            qb[rows, at] = grad_q
            kb[rows, at] = merged[1]
            vb[rows, at] = merged[2]
            total_q += jnp.sum(grad_q.astype(F32).reshape(block // 8, 8, 128), axis=0)
            total_v += jnp.sum(merged[2].astype(F32).reshape(block // 8, 8, 128), axis=0)
        acc_qv[0, :, at] = total_q
        acc_qv[1, :, at] = total_v

    def gqkv_piece(lane0, count):
        ref = (qb, kb, vb)[lane0 // OWN]

        def tile(z):
            left = xin[:, :, pl.ds(mul(z, 256), 256)].reshape(NPOS, 256)
            value = dot_tn(left, ref[:, lane0 % OWN : lane0 % OWN + count]).astype(BF)
            gqo[z, :, :, :, pl.ds(lane0, count)] = value.reshape(2, 2, 64, count)

        loop(NZ, tile)

    def gai_tile(rows, dst):
        def body(z):
            value = None
            for part, ref in enumerate((qb, kb, vb)):
                weight = wq[z, :, :, :, pl.ds(part * OWN, OWN)].reshape(256, OWN)
                term = dot_nt(ref[rows, :], weight)
                value = term if value is None else value + term
            dst[:, pl.ds(mul(z, 256), 256)] = value

        loop(NZ, body)

    def grad_attn_in():
        gai_tile(other_rows, snd)
        got["gai"] = net.sibling(snd, rcv)
        gai_tile(own_rows, own)

    def bottom_tile(i):
        here = pl.ds(mul(i, chunk), chunk)
        hat, inv = normalize(tok[here, :].astype(F32))
        grad_in = own[here, :] + rcv[here, :]
        accumulate(ROW_GAIN, grad_in * hat)
        accumulate(ROW_SHIFT, grad_in)
        gtok_out[here, :] = mid[here, :] + norm_back(hat, inv, gain(0), grad_in)

    def bottom():
        got["gai"].wait_recv()
        loop(chunks, bottom_tile)
        for row in range(16):
            gvecs[row : row + 1, :] = jnp.sum(acc[row], axis=0, keepdims=True)
        row_id = lax.broadcasted_iota(jnp.int32, (16, 1), 0)
        for z in range(NZ):
            for y in range(2):
                base = gvecs[:, pl.ds((z * 2 + y) * 128, 128)]
                for x in range(2):
                    at = pl.ds((y * 2 + x) * 128, 128)
                    kind = 0 if z < 2 else 1
                    qv_row = jnp.sum(acc_qv[kind, :, at], axis=0, keepdims=True)
                    qv_row = jnp.where(core == z % 2, qv_row, 0.0)
                    up_at = pl.ds((z * 2 + y) * 128, 128)
                    up_row = jnp.sum(acc_up[:, up_at], axis=0, keepdims=True)
                    up_row = jnp.where(net.x == x, up_row, 0.0)
                    value = base + jnp.where(row_id == 0, qv_row, 0.0)
                    gv[z, y, x] = value + jnp.where(row_id == 1 + core, up_row, 0.0)

    steps = [
        lambda: None,
        lambda: gpre_group(own_group),
        gpre_beside,
        lambda: share_gff.pass_on(0),
        lambda: share_gff.pass_on(1),
        *tiles_of(WIDTH, 512, functools.partial(gdown_piece, 1 - net.x, True)),
        lambda: gpre_group(across_group),
        gpre_last,
        *tiles_of(FF4, 512, functools.partial(gup_piece, 1 - net.x, True)),
        grad_ffn_in_there,
        grad_ffn_in_cross,
        grad_middle,
        grad_out,
        lambda: got["swap"].wait_recv(),
    ]
    steps += [functools.partial(loop, 1, lambda i, pair=p: attend_back(i + pair)) for p in range(4)]
    steps += tiles_of(3 * OWN, 512, gqkv_piece)
    steps += [grad_attn_in, bottom]

    def both(piece, width):
        for step in tiles_of(width, 512, functools.partial(piece, net.x, False)):
            step()

    steps += [
        lambda: both(gdown_piece, WIDTH),
        lambda: both(gup_piece, FF4),
        grad_ffn_in_here,
    ]
    for piece, stage in SCATTER_STEPS:
        if piece < 0:
            steps[stage]()
        else:
            scatter(piece, stage)
    got_vec = net.sibling(gvec_out, vother)
    got_vec.wait_send()
    got_vec.wait_recv()
    gvec_out[...] = gvec_out[...] + vother[...]
    for copy, remote in out_copies:
        copy.wait()
        remote.wait_recv()
    net.drain(net.unsent, (*down.beside, *down.across, got_vec))


def scatter_bufs(group, count, order):
    rows, dtype = {"v": (16, F32)}.get(group, (64, BF))
    size = {"z": NZ, "y": 2, "x": 2}
    if group in "du":
        first, second = order
        return [
            pltpu.VMEM((size[first] - 1, size[second], 128, count), BF),
            pltpu.VMEM((size[second] - 1, 128, count), BF),
        ]
    first, second, third = order
    left = [size[dim] for dim in "zyx" if dim != first]
    return [
        pltpu.VMEM((size[first] - 1, *left, rows, count), dtype),
        pltpu.VMEM((size[second] - 1, size[third], rows, count), dtype),
        pltpu.VMEM((size[third] - 1, rows, count), dtype),
    ]


def hand_out_kernel(*refs):
    large, vec = refs[:6], refs[6]
    outs, small = refs[7:13], refs[13:19]
    for src, dst in zip(large, outs, strict=True):
        dst[...] = src[...]
    right = lax.axis_index("dp") % 2 == 1
    values = vec[...]
    half = jnp.where(right, values[:, 64:], values[:, :64])
    small[0][...] = values[0:1]
    small[1][...] = half[ROW_OUT : ROW_OUT + 1]
    small[2][...] = values[1:3]
    small[3][...] = half[ROW_DOWN : ROW_DOWN + 1]
    small[4][...] = half[ROW_GAIN : ROW_GAIN + 4]
    small[5][...] = half[ROW_SHIFT : ROW_SHIFT + 4]

def fused(
    tokens,
    doc_lengths,
    cotangent,
    w_qkv,
    qv_bias,
    w_out,
    out_bias,
    w_up,
    up_bias,
    w_down,
    down_bias,
    norm_gain,
    norm_bias,
):
    vmem = pl.BlockSpec(memory_space=pltpu.VMEM)
    anywhere = pl.BlockSpec(memory_space=pl.ANY)
    scratch = [
        pltpu.VMEM((NZ, 2, 2, 64, 3 * OWN), BF),
        pltpu.VMEM((2, NZ, 2, 2, 64, OWN), BF),
        pltpu.VMEM((NZ, 2, 128, FF4), BF),
        pltpu.VMEM((64, FF4), BF),
        pltpu.VMEM((NZ, 2, 128, WIDTH), BF),
        pltpu.VMEM((NZ, 2, 2, 16, 128), BF),
        pltpu.VMEM((LEN, WIDTH), BF),
        pltpu.VMEM((LEN, WIDTH), BF),
        pltpu.VMEM((16, 128), F32),
        pltpu.VMEM((16, WIDTH), F32),
        pltpu.VMEM((16, OWN), F32),
        pltpu.VMEM((8, FF4), F32),
        pltpu.VMEM((2, LEN, WIDTH), BF),
        pltpu.VMEM((NPOS, OWN), BF),
        pltpu.VMEM((NPOS, OWN), BF),
        pltpu.VMEM((NPOS, OWN), BF),
        pltpu.VMEM((8, NPOS, NPOS), BF),
        pltpu.VMEM((NPOS, NPOS), F32),
        pltpu.VMEM((NPOS, OWN), F32),
        pltpu.VMEM((NPOS, OWN), BF),
        pltpu.VMEM((LEN, OWN), BF),
        pltpu.VMEM((LEN, WIDTH), F32),
        pltpu.VMEM((LEN, WIDTH), F32),
        pltpu.VMEM((LEN, 128), F32),
        pltpu.VMEM((LEN, 128), F32),
        pltpu.VMEM((LEN, WIDTH), F32),
        pltpu.VMEM((4, LEN, WIDTH), BF),
        pltpu.VMEM((4 * LEN, FF4), BF),
        pltpu.VMEM((4 * LEN, FF4), BF),
        pltpu.VMEM((LEN, WIDTH), F32),
        pltpu.VMEM((LEN, WIDTH), F32),
        pltpu.VMEM((LEN, WIDTH), F32),
        pltpu.VMEM((LEN, WIDTH), F32),
        pltpu.VMEM((2, LEN, WIDTH), BF),
        pltpu.VMEM((2, LEN, WIDTH), BF),
        pltpu.VMEM((LEN, WIDTH), BF),
        pltpu.VMEM((LEN, WIDTH), BF),
        pltpu.VMEM((4, LEN, WIDTH), BF),
        pltpu.VMEM((2, LEN, WIDTH), BF),
        pltpu.VMEM((NPOS, OWN), BF),
        pltpu.VMEM((NPOS, NPOS), BF),
        pltpu.VMEM((NZ, 2, 2, 64, 4 * OWN), BF),
        pltpu.VMEM((NZ, 2, 128, FF4), BF),
        pltpu.VMEM((NZ, 2, 128, WIDTH), BF),
        pltpu.VMEM((2, 2, 2, 64, OWN), BF),
        pltpu.VMEM((16, 8, WIDTH), F32),
        pltpu.VMEM((2, 8, OWN), F32),
        pltpu.VMEM((8, FF4), F32),
        pltpu.VMEM((16, WIDTH), F32),
        pltpu.VMEM((NZ, 2, 2, 16, 128), F32),
        pltpu.VMEM((16, 128), F32),
        [
            scatter_bufs(group, count, order)
            for group, _, count, order in pieces_of(SCATTER, WIDTHS)
        ],
        pltpu.VMEM((64, 3 * OWN), F32),
        pltpu.VMEM((64, OWN), F32),
        pltpu.VMEM((2, 64, FF4), F32),
        pltpu.VMEM((64, FF4), BF),
        pltpu.VMEM((64, FF4), BF),
        pltpu.VMEM((128, WIDTH), F32),
        pltpu.SemaphoreType.DMA((800,)),
        pltpu.SemaphoreType.DMA((90,)),
    ]
    outs = pl.pallas_call(
        layer_kernel,
        out_shape=[
            jax.ShapeDtypeStruct((LEN, WIDTH), BF),
            jax.ShapeDtypeStruct((LEN, WIDTH), F32),
            jax.ShapeDtypeStruct((64, 3 * WIDTH), F32),
            jax.ShapeDtypeStruct((64, WIDTH), F32),
            jax.ShapeDtypeStruct((64, 4 * FF4), F32),
            jax.ShapeDtypeStruct((256, WIDTH), F32),
            jax.ShapeDtypeStruct((16, 128), F32),
        ],
        in_specs=[anywhere, pl.BlockSpec(memory_space=pltpu.SMEM), anywhere]
        + [anywhere] * 4
        + [vmem] * 6,
        out_specs=[vmem, vmem] + [anywhere] * 4 + [vmem],
        scratch_shapes=scratch,
        compiler_params=pltpu.CompilerParams(
            collective_id=0, has_side_effects=True, vmem_limit_bytes=63 * MIB
        ),
        name="layer",
    )(
        tokens[0],
        doc_lengths,
        cotangent[0],
        w_qkv,
        w_out,
        w_up,
        w_down,
        qv_bias.reshape(1, 128),
        up_bias.reshape(2, 128),
        out_bias.reshape(1, 64),
        down_bias.reshape(1, 64),
        norm_gain,
        norm_bias,
    )
    *large, vec = outs
    done = pl.pallas_call(
        hand_out_kernel,
        out_shape=[jax.ShapeDtypeStruct(array.shape, array.dtype) for array in large]
        + [
            jax.ShapeDtypeStruct((1, 128), F32),
            jax.ShapeDtypeStruct((1, 64), F32),
            jax.ShapeDtypeStruct((2, 128), F32),
            jax.ShapeDtypeStruct((1, 64), F32),
            jax.ShapeDtypeStruct((4, 64), F32),
            jax.ShapeDtypeStruct((4, 64), F32),
        ],
        in_specs=[vmem] * 7,
        out_specs=[vmem] * 12,
        compiler_params=pltpu.CompilerParams(vmem_limit_bytes=63 * MIB),
        name="hand_out",
    )(*large, vec)
    result, grad_inputs, grad_qkv, grad_out, grad_up, grad_down = done[:6]
    grad_qv, grad_out_shift, grad_up_shift, grad_down_shift, grad_gain, grad_shift = done[6:]
    return (
        result[None],
        grad_inputs[None],
        grad_qkv,
        grad_qv.reshape(128),
        grad_out,
        grad_out_shift.reshape(64),
        grad_up,
        grad_up_shift.reshape(256),
        grad_down,
        grad_down_shift.reshape(64),
        grad_gain,
        grad_shift,
    )


def solution(mesh):
    placed = (
        P("dp", "blk", None),
        P("dp", None),
        P("dp", "blk", None),
        P("dp", None),
        P("dp"),
        P("dp", None),
        P("dp"),
        P("dp", None),
        P("dp"),
        P("dp", None),
        P("dp"),
        P(None, "dp"),
        P(None, "dp"),
    )
    sizes = (mesh.shape["dp"], mesh.shape["blk"])
    return jax.shard_map(
        fused if sizes == (NZ * 4, 2) else shards,
        mesh=mesh,
        in_specs=placed,
        out_specs=(
            P("dp", "blk", None),
            P("dp", "blk", None),
            P("dp", None),
            P("dp"),
            P("dp", None),
            P("dp"),
            P("dp", None),
            P("dp"),
            P("dp", None),
            P("dp"),
            P(None, "dp"),
            P(None, "dp"),
        ),
        check_vma=False,
    )
```

```python
import functools
import math

import jax
import jax.numpy as jnp
from jax import lax
from jax.experimental import pallas as pl
from jax.experimental.pallas import tpu as pltpu
from jax.sharding import PartitionSpec as P

HEADS = 16
ALPHA = 32


EPSILON = 1e-05
FILLER = -1000000000.0


def normalize(values):
    center = values - jnp.mean(values, axis=-1, keepdims=True)
    inverse = lax.rsqrt(jnp.mean(center * center, axis=-1, keepdims=True) + EPSILON)
    return (center * inverse, inverse)


def norm_back(normed, inverse, gain_row, upstream):
    scaled = upstream * gain_row
    return inverse * (
        scaled
        - jnp.mean(scaled, axis=-1, keepdims=True)
        - normed * jnp.mean(scaled * normed, axis=-1, keepdims=True)
    )


def segment_of(position, doc_ends):
    return jnp.sum((position[:, None] >= doc_ends[None, :]).astype(jnp.int32), axis=1)


def gelu_tanh(values):
    return jax.nn.gelu(values, approximate=True)


def shards(
    tokens,
    doc_lengths,
    cotangent,
    w_qkv,
    qv_bias,
    w_out,
    out_bias,
    w_up,
    up_bias,
    w_down,
    down_bias,
    norm_gain,
    norm_bias,
):
    inputs = tokens[0].astype(jnp.float32)
    length = inputs.shape[0]
    model_width = inputs.shape[1]
    block_count = lax.axis_size("blk")
    seq_len = length * block_count
    offset = lax.axis_index("blk") * length
    doc_ends = jnp.cumsum(doc_lengths[0])
    filled = doc_ends[-1]
    query_pos = offset + jnp.arange(length, dtype=jnp.int32)
    query_seg = segment_of(query_pos, doc_ends)
    valid_rows = (query_pos < filled).astype(jnp.float32)
    key_seg = segment_of(jnp.arange(seq_len, dtype=jnp.int32), doc_ends)
    last_query = offset + length - 1

    def block_meets(first_row, piece_rows):
        first_at = jnp.asarray(first_row, jnp.int32)
        first_seg = lax.dynamic_index_in_dim(key_seg, first_at, keepdims=False)
        last_seg = lax.dynamic_index_in_dim(key_seg, first_at + piece_rows - 1, keepdims=False)
        return (first_at <= last_query) & (first_seg <= query_seg[-1]) & (last_seg >= query_seg[0])

    gathered = (
        lax.all_gather(w_qkv, "dp", axis=0, tiled=True),
        lax.all_gather(qv_bias, "dp", axis=0, tiled=True),
        lax.all_gather(w_out, "dp", axis=0, tiled=True),
        lax.all_gather(out_bias, "dp", axis=0, tiled=True),
        lax.all_gather(w_up, "dp", axis=0, tiled=True),
        lax.all_gather(up_bias, "dp", axis=0, tiled=True),
        lax.all_gather(w_down, "dp", axis=0, tiled=True),
        lax.all_gather(down_bias, "dp", axis=0, tiled=True),
        lax.all_gather(norm_gain, "dp", axis=1, tiled=True),
        lax.all_gather(norm_bias, "dp", axis=1, tiled=True),
    )
    (
        qkv_weight,
        qv_shift,
        out_weight,
        out_shift,
        up_weight,
        up_shift,
        down_weight,
        down_shift,
        gain_all,
        shift_all,
    ) = gathered
    gain_rows = gain_all.astype(jnp.float32)
    shift_rows = shift_all.astype(jnp.float32)
    query_scale = 1.0 / (ALPHA * math.sqrt(model_width // HEADS))
    first_hat, first_inv = normalize(inputs)
    attn_in = (first_hat * gain_rows[0] + shift_rows[0]).astype(jnp.bfloat16)
    projected = jnp.dot(attn_in, qkv_weight, preferred_element_type=jnp.float32)
    qv_float = qv_shift.astype(jnp.float32)
    queries = ((projected[:, :model_width] + qv_float[:model_width]) * query_scale).astype(
        jnp.bfloat16
    )
    keys_own = projected[:, model_width : 2 * model_width].astype(jnp.bfloat16)
    values_own = (projected[:, 2 * model_width :] + qv_float[model_width:]).astype(jnp.bfloat16)
    query_heads = queries.reshape(length, HEADS, -1)

    def scores_of(key_piece, first_row):
        piece_rows = key_piece.shape[0]
        piece_pos = first_row + jnp.arange(piece_rows, dtype=jnp.int32)
        piece_seg = lax.dynamic_slice_in_dim(key_seg, jnp.asarray(first_row, jnp.int32), piece_rows)
        allowed_pairs = (query_seg[:, None] == piece_seg[None, :]) & (
            piece_pos[None, :] <= query_pos[:, None]
        )
        raw_scores = jnp.einsum(
            "qhd,khd->hqk",
            query_heads,
            key_piece.reshape(piece_rows, HEADS, -1),
            preferred_element_type=jnp.float32,
        )
        return (jnp.where(allowed_pairs[None], raw_scores, FILLER), allowed_pairs[None])

    head_dim = model_width // HEADS
    start_state = (
        jnp.full((HEADS, length), FILLER, jnp.float32),
        jnp.zeros((HEADS, length), jnp.float32),
        jnp.zeros((HEADS, length, head_dim), jnp.float32),
    )
    accumulate_first_row = jnp.int32(0)
    accumulate_key_piece = lax.all_gather(keys_own, "blk", axis=0, tiled=True)
    accumulate_value_piece = lax.all_gather(values_own, "blk", axis=0, tiled=True)
    piece_rows = accumulate_value_piece.shape[0]

    def update(state):
        row_top, row_total, summed = state
        masked, allowed_pairs = scores_of(accumulate_key_piece, accumulate_first_row)
        new_top = jnp.maximum(row_top, jnp.max(masked, axis=2))
        factor = jnp.exp(ALPHA * (row_top - new_top))
        weights = jnp.where(allowed_pairs, jnp.exp(ALPHA * (masked - new_top[:, :, None])), 0.0)
        summed = summed * factor[:, :, None] + jnp.einsum(
            "hqk,khd->hqd",
            weights,
            accumulate_value_piece.reshape(piece_rows, HEADS, -1),
            preferred_element_type=jnp.float32,
        )
        return (new_top, row_total * factor + jnp.sum(weights, axis=2), summed)

    def unchanged(state):
        return state

    softmax_state = lax.cond(
        block_meets(accumulate_first_row, piece_rows), update, unchanged, start_state
    )
    row_top, row_total, summed = softmax_state
    attended_heads = summed / row_total[:, :, None]
    attended = jnp.transpose(attended_heads, (1, 0, 2)).reshape(length, model_width)
    attn_low = attended.astype(jnp.bfloat16)
    branch = jnp.dot(attn_low, out_weight, preferred_element_type=jnp.float32) + out_shift.astype(
        jnp.float32
    )
    second_hat, second_inv = normalize(branch)
    middle = inputs + second_hat * gain_rows[1] + shift_rows[1]
    third_hat, third_inv = normalize(middle)
    ffn_in = (third_hat * gain_rows[2] + shift_rows[2]).astype(jnp.bfloat16)
    pre_act = jnp.dot(ffn_in, up_weight, preferred_element_type=jnp.float32) + up_shift.astype(
        jnp.float32
    )
    activated, gelu_pullback = jax.vjp(gelu_tanh, pre_act)
    act_low = activated.astype(jnp.bfloat16)
    ffn_out = jnp.dot(act_low, down_weight, preferred_element_type=jnp.float32) + down_shift.astype(
        jnp.float32
    )
    fourth_hat, fourth_inv = normalize(ffn_out)
    result = middle + fourth_hat * gain_rows[3] + shift_rows[3]
    qkv_again, out_again, up_again, down_again, gain_again = (
        lax.all_gather(w_qkv, "dp", axis=0, tiled=True),
        lax.all_gather(w_out, "dp", axis=0, tiled=True),
        lax.all_gather(w_up, "dp", axis=0, tiled=True),
        lax.all_gather(w_down, "dp", axis=0, tiled=True),
        lax.all_gather(norm_gain, "dp", axis=1, tiled=True),
    )
    back_gains = gain_again.astype(jnp.float32)
    upstream = cotangent[0].astype(jnp.float32) * valid_rows[:, None]
    grad_ffn = norm_back(fourth_hat, fourth_inv, back_gains[3], upstream).astype(jnp.bfloat16)
    grad_down = jnp.einsum("tf,td->fd", act_low, grad_ffn, preferred_element_type=jnp.float32)
    grad_act = jnp.einsum("td,fd->tf", grad_ffn, down_again, preferred_element_type=jnp.float32)
    grad_pre = gelu_pullback(grad_act)[0].astype(jnp.bfloat16)
    grad_up = jnp.einsum("td,tf->df", ffn_in, grad_pre, preferred_element_type=jnp.float32)
    grad_ffn_in = jnp.einsum("tf,df->td", grad_pre, up_again, preferred_element_type=jnp.float32)
    grad_middle = upstream + norm_back(third_hat, third_inv, back_gains[2], grad_ffn_in)
    grad_branch = norm_back(second_hat, second_inv, back_gains[1], grad_middle).astype(jnp.bfloat16)
    grad_out = jnp.einsum("td,te->de", attn_low, grad_branch, preferred_element_type=jnp.float32)
    grad_attn = jnp.einsum(
        "te,de->td", grad_branch, out_again, preferred_element_type=jnp.float32
    ).astype(jnp.bfloat16)
    grad_heads = grad_attn.reshape(length, HEADS, -1)
    row_delta = jnp.einsum(
        "qhd,hqd->hq", grad_heads, attended_heads, preferred_element_type=jnp.float32
    )
    keys_all, values_all = (
        lax.all_gather(keys_own, "blk", axis=0, tiled=True),
        lax.all_gather(values_own, "blk", axis=0, tiled=True),
    )
    grad_query = jnp.zeros((length, HEADS, head_dim), jnp.float32)
    key_terms = []
    for block_index in range(block_count):
        first_row = block_index * length
        key_piece = keys_all[first_row : first_row + length]
        value_piece = values_all[first_row : first_row + length]

        def block_grads(operands):
            key_block, value_block = operands
            value_heads = value_block.reshape(length, HEADS, -1)
            masked, allowed_pairs = scores_of(key_block, first_row)
            probabilities = (
                jnp.where(allowed_pairs, jnp.exp(ALPHA * (masked - row_top[:, :, None])), 0.0)
                / row_total[:, :, None]
            )
            grad_probs = jnp.einsum(
                "qhd,khd->hqk", grad_heads, value_heads, preferred_element_type=jnp.float32
            )
            grad_scores = ALPHA * probabilities * (grad_probs - row_delta[:, :, None])
            query_term = jnp.einsum(
                "hqk,khd->qhd",
                grad_scores,
                key_block.reshape(length, HEADS, -1),
                preferred_element_type=jnp.float32,
            )
            grad_key = jnp.einsum(
                "hqk,qhd->khd", grad_scores, query_heads, preferred_element_type=jnp.float32
            )
            grad_value = jnp.einsum(
                "hqk,qhd->khd", probabilities, grad_heads, preferred_element_type=jnp.float32
            )
            return (
                query_term,
                jnp.concatenate(
                    [
                        grad_key.reshape(length, model_width),
                        grad_value.reshape(length, model_width),
                    ],
                    1,
                ),
            )

        def block_zeros(operands):
            return (
                jnp.zeros((length, HEADS, head_dim), jnp.float32),
                jnp.zeros((length, 2 * model_width), jnp.float32),
            )

        query_term, key_term = lax.cond(
            block_meets(first_row, length), block_grads, block_zeros, (key_piece, value_piece)
        )
        grad_query = grad_query + query_term
        key_terms.append(key_term)
    key_grads = lax.psum_scatter(
        jnp.concatenate(key_terms, 0).astype(jnp.bfloat16), "blk", scatter_dimension=0, tiled=True
    ).astype(jnp.float32)
    grad_keys = key_grads[:, :model_width].astype(jnp.bfloat16)
    grad_values = key_grads[:, model_width:].astype(jnp.bfloat16)
    grad_queries = grad_query.reshape(length, model_width).astype(jnp.bfloat16) * jnp.asarray(
        query_scale, jnp.bfloat16
    )
    grad_projected = jnp.concatenate([grad_queries, grad_keys, grad_values], 1)
    grad_qkv = jnp.einsum("td,te->de", attn_in, grad_projected, preferred_element_type=jnp.float32)
    grad_qv = jnp.concatenate(
        [
            jnp.sum(grad_queries.astype(jnp.float32), axis=0),
            jnp.sum(grad_values.astype(jnp.float32), axis=0),
        ]
    )
    grad_attn_in = jnp.einsum(
        "te,de->td", grad_projected, qkv_again, preferred_element_type=jnp.float32
    )
    grad_inputs = grad_middle + norm_back(first_hat, first_inv, back_gains[0], grad_attn_in)
    grad_gains = jnp.stack(
        [
            jnp.sum(grad_attn_in * first_hat, axis=0),
            jnp.sum(grad_middle * second_hat, axis=0),
            jnp.sum(grad_ffn_in * third_hat, axis=0),
            jnp.sum(upstream * fourth_hat, axis=0),
        ]
    )
    grad_shifts = jnp.stack(
        [
            jnp.sum(grad_attn_in, axis=0),
            jnp.sum(grad_middle, axis=0),
            jnp.sum(grad_ffn_in, axis=0),
            jnp.sum(upstream, axis=0),
        ]
    )
    grad_out_shift = jnp.sum(grad_branch.astype(jnp.float32), axis=0)
    grad_up_shift = jnp.sum(grad_pre.astype(jnp.float32), axis=0)
    grad_down_shift = jnp.sum(grad_ffn.astype(jnp.float32), axis=0)
    shares = (
        lax.psum_scatter(grad_qkv, "dp", scatter_dimension=0, tiled=True),
        lax.psum_scatter(grad_qv, "dp", scatter_dimension=0, tiled=True),
        lax.psum_scatter(grad_out, "dp", scatter_dimension=0, tiled=True),
        lax.psum_scatter(grad_out_shift, "dp", scatter_dimension=0, tiled=True),
        lax.psum_scatter(grad_up, "dp", scatter_dimension=0, tiled=True),
        lax.psum_scatter(grad_up_shift, "dp", scatter_dimension=0, tiled=True),
        lax.psum_scatter(grad_down, "dp", scatter_dimension=0, tiled=True),
        lax.psum_scatter(grad_down_shift, "dp", scatter_dimension=0, tiled=True),
        lax.psum_scatter(grad_gains, "dp", scatter_dimension=1, tiled=True),
        lax.psum_scatter(grad_shifts, "dp", scatter_dimension=1, tiled=True),
    )
    totals = (
        lax.psum(shares[0].astype(jnp.bfloat16), "blk").astype(jnp.float32),
        lax.psum(shares[1].astype(jnp.bfloat16), "blk").astype(jnp.float32),
        lax.psum(shares[2].astype(jnp.bfloat16), "blk").astype(jnp.float32),
        lax.psum(shares[3].astype(jnp.bfloat16), "blk").astype(jnp.float32),
        lax.psum(shares[4].astype(jnp.bfloat16), "blk").astype(jnp.float32),
        lax.psum(shares[5].astype(jnp.bfloat16), "blk").astype(jnp.float32),
        lax.psum(shares[6].astype(jnp.bfloat16), "blk").astype(jnp.float32),
        lax.psum(shares[7].astype(jnp.bfloat16), "blk").astype(jnp.float32),
        lax.psum(shares[8].astype(jnp.bfloat16), "blk").astype(jnp.float32),
        lax.psum(shares[9].astype(jnp.bfloat16), "blk").astype(jnp.float32),
    )
    return (result.astype(jnp.bfloat16)[None], grad_inputs[None]) + tuple(totals)


NZ = 4
NPOS = 512
LEN = 256
WIDTH = 1024
OWN = 512
FF4 = 1024
BF = jnp.bfloat16
F32 = jnp.float32
MESH = pl.DeviceIdType.MESH
MIB = 1 << 20
ROW_OUT, ROW_DOWN, ROW_GAIN, ROW_SHIFT = 3, 4, 5, 9
GATHER = (
    ("v", 0, "zyx"), ("q", 0, "zxy"), ("q", 1, "zyx"), ("q", 2, "zxy"),
    ("q", 3, "zyx"), ("o", 0, "zyx"), ("u", 0, "zy"), ("u", 1, "zy"),
    ("d", 0, "zy"), ("u", 2, "yz"), ("d", 1, "zy"), ("d", 2, "zy"),
    ("u", 3, "zy"), ("d", 3, "zy"),
)
GATHER_STEPS = (
    (0, 0), (1, 0), (0, 1), (2, 0), (0, 2), (1, 1), (3, 0), (0, 3),
    (-1, 0), (-1, 1), (2, 1), (4, 0), (1, 2), (3, 1), (5, 0), (7, 0),
    (4, 1), (6, 0), (2, 2), (7, 1), (8, 0), (6, 1), (5, 1), (9, 0),
    (3, 2), (1, 3), (9, 1), (12, 0), (4, 2), (2, 3), (12, 1), (9, 2),
    (7, 2), (8, 1), (10, 0), (11, 0), (3, 3), (5, 2), (6, 2), (4, 3),
    (-1, 2), (-1, 3), (-1, 4), (5, 3), (-1, 5), (-1, 7), (-1, 6), (6, 3),
    (7, 3), (8, 2), (12, 2), (-1, 8), (10, 1), (13, 0), (11, 1), (-1, 9),
    (12, 3), (9, 3), (-1, 10), (-1, 11), (-1, 12), (13, 1), (-1, 13), (-1, 14),
    (-1, 15), (10, 2), (-1, 16), (11, 2), (-1, 17), (-1, 18), (-1, 19), (13, 2),
    (-1, 20), (-1, 21), (-1, 22), (-1, 23),
)
SCATTER = (
    ("q", 0, "xyz"), ("d", 0, "zy"), ("o", 0, "xyz"), ("d", 1, "yz"),
    ("u", 0, "yz"), ("d", 2, "zy"), ("u", 1, "yz"), ("o", 1, "xyz"),
    ("q", 1, "yxz"), ("q", 2, "yxz"), ("u", 2, "yz"), ("q", 3, "xyz"),
    ("d", 3, "yz"), ("q", 4, "xyz"), ("q", 5, "xyz"), ("u", 3, "yz"),
    ("v", 0, "xyz"),
)
SCATTER_STEPS = (
    (-1, 0), (-1, 1), (-1, 2), (-1, 25), (-1, 26), (-1, 27), (-1, 3), (-1, 4),
    (-1, 7), (-1, 8), (-1, 11), (-1, 5), (1, 0), (3, 0), (-1, 12), (-1, 6),
    (5, 0), (-1, 9), (4, 0), (-1, 10), (3, 1), (6, 0), (-1, 13), (4, 1),
    (12, 0), (-1, 14), (6, 1), (10, 0), (15, 0), (-1, 15), (2, 0), (7, 0),
    (-1, 16), (-1, 17), (-1, 18), (1, 1), (12, 1), (-1, 19), (3, 2), (-1, 20),
    (0, 0), (-1, 21), (9, 0), (11, 0), (-1, 22), (1, 2), (2, 1), (7, 1),
    (10, 1), (14, 0), (15, 1), (-1, 23), (4, 2), (5, 1), (8, 0), (-1, 24),
    (6, 2), (2, 2), (4, 3), (0, 1), (7, 2), (9, 1), (5, 2), (6, 3),
    (11, 1), (12, 2), (13, 0), (14, 1), (9, 2), (0, 2), (8, 1), (16, 0),
    (10, 2), (2, 3), (11, 2), (7, 3), (13, 1), (14, 2), (15, 2), (16, 1),
    (10, 3), (8, 2), (9, 3), (15, 3), (0, 3), (13, 2), (16, 2), (11, 3),
    (14, 3), (16, 3), (8, 3), (13, 3),
)
WIDTHS = {"v": 128, "q": 3 * OWN, "o": OWN, "u": FF4, "d": WIDTH}


def dot_nn(a, b):
    return lax.dot_general(a, b, (((1,), (0,)), ((), ())), preferred_element_type=F32)


def dot_nt(a, b):
    return lax.dot_general(a, b, (((1,), (1,)), ((), ())), preferred_element_type=F32)


def dot_tn(a, b):
    return lax.dot_general(a, b, (((0,), (0,)), ((), ())), preferred_element_type=F32)


def loop(count, body):
    lax.fori_loop(0, count, lambda index, carry: (body(index), carry)[1], 0)


def mul(index, size):
    return pl.multiple_of(index * size, size)


class Net:
    def __init__(self, sems):
        self.chip = lax.axis_index("dp")
        self.core = lax.axis_index("blk")
        self.z = self.chip // 4
        self.y = (self.chip // 2) % 2
        self.x = self.chip % 2
        self.sems = sems
        self.used = 0
        self.unsent = []

    def sem(self):
        self.used += 1
        return self.sems.at[self.used - 1]

    def chip_at(self, z, y, x):
        return z * 4 + y * 2 + x

    def peers(self, dim):
        if dim == "x":
            return [(1, self.z, self.y, 1 - self.x, self.core)]
        if dim == "y":
            return [(1, self.z, 1 - self.y, self.x, self.core)]
        if dim == "c":
            return [(1, self.z, self.y, self.x, 1 - self.core)]
        return [(k, (self.z + k) % NZ, self.y, self.x, self.core) for k in range(1, NZ)]

    def send(self, src, dst, recv, peer):
        _, z, y, x, core = peer
        copy = pltpu.make_async_remote_copy(
            src_ref=src,
            dst_ref=dst,
            send_sem=self.sem(),
            recv_sem=recv,
            device_id=(self.chip_at(z, y, x), core),
            device_id_type=MESH,
        )
        copy.start()
        self.unsent.append(copy)
        return copy

    @staticmethod
    def drain(sends, waited):
        for copy in sends:
            if not any(copy is other for other in waited):
                copy.wait_send()

    def sibling(self, src, dst):
        return self.send(src, dst, self.sem(), self.peers("c")[0])

    def greet(self):
        barrier = pltpu.get_barrier_semaphore()
        count = 0
        for dim in "xyzc":
            for _, z, y, x, core in self.peers(dim):
                pl.semaphore_signal(
                    barrier, inc=1, device_id=(self.chip_at(z, y, x), core), device_id_type=MESH
                )
                count += 1
        return lambda: pl.semaphore_wait(barrier, count)


def await_bytes(view, sem):
    pltpu.make_async_copy(view, view, sem).wait()


def view_of(net, ref, lanes, **given):
    where = {"z": net.z, "y": net.y, "x": net.x}
    where.update(given)
    return ref.at[where["z"], where["y"], where["x"], :, lanes]


ALL = slice(None)


def gather_stages(net, ref, lanes, order):
    first, second, third = order
    others = {"z": pl.ds(0, NZ - 1), "y": 1 - net.y, "x": 1 - net.x}
    got_first, got_second, got_near, got_far = net.sem(), net.sem(), net.sem(), net.sem()

    def pass_on(dim, sem, **held):
        blocks = view_of(net, ref, lanes, **held)
        for peer in net.peers(dim):
            net.send(blocks, blocks, sem, peer)

    def start():
        pass_on(first, got_first)

    def after_first():
        await_bytes(view_of(net, ref, lanes, **{first: others[first]}), got_first)
        pass_on(second, got_second, **{first: ALL})
        pass_on(third, got_near, **{first: ALL})

    def after_second():
        held = {first: ALL, second: others[second]}
        await_bytes(view_of(net, ref, lanes, **held), got_second)
        if second == "z":
            for peer in net.peers("z"):
                pass_on(third, got_far, **{first: ALL, "z": peer[1]})
        else:
            pass_on(third, got_far, **held)

    def finish():
        held = {first: ALL, third: others[third]}
        await_bytes(view_of(net, ref, lanes, **held), got_near)
        held[second] = others[second]
        await_bytes(view_of(net, ref, lanes, **held), got_far)

    return start, after_first, after_second, finish


def scatter_stages(net, ref, lanes, order, bufs, done):
    first, second, third = order
    wide, half, line = bufs
    got_wide, got_half, got_line = net.sem(), net.sem(), net.sem()
    dtype = wide.dtype
    rows, cols = wide.shape[-2:]
    step = min(rows, max(16, 32768 // cols))
    size = {"z": NZ, "y": 2, "x": 2}
    place = {"z": 0, "y": 1, "x": 2}
    mine = {"z": net.z, "y": net.y, "x": net.x}

    def coordinate(dim, peer):
        return peer[1 + place[dim]]

    def block_add(target, sources):
        for part in range(rows // step):
            here = pl.ds(part * step, step)
            total = ref[(*target, here, lanes)].astype(F32)
            for buf, at in sources:
                total = total + buf[(*at, here)].astype(F32)
            ref[(*target, here, lanes)] = total.astype(dtype)

    def target_of(**given):
        where = dict(mine)
        where.update(given)
        return (where["z"], where["y"], where["x"])

    def start():
        for peer in net.peers(first):
            there = {"z": ALL, "y": ALL, "x": ALL, first: coordinate(first, peer)}
            net.send(view_of(net, ref, lanes, **there), wide.at[peer[0] - 1], got_wide, peer)

    def after_first():
        await_bytes(wide, got_wide)
        left = [dim for dim in "zyx" if dim != first]

        def add(second_at, third_at):
            at = {second: second_at, third: third_at}
            place_in = (0, at[left[0]], at[left[1]])
            block_add(target_of(**at), [(wide, place_in)])

        for peer in net.peers(second):
            gone = coordinate(second, peer)
            loop(size[third], lambda other: add(gone, other))
            blocks = view_of(net, ref, lanes, **{second: gone, third: ALL})
            net.send(blocks, half.at[peer[0] - 1], got_half, peer)
        loop(size[third], lambda other: add(mine[second], other))

    def after_second():
        await_bytes(half, got_half)
        for peer in net.peers(third):
            gone = coordinate(third, peer)
            block_add(
                target_of(**{third: gone}), [(half, (k, gone)) for k in range(size[second] - 1)]
            )
            blocks = view_of(net, ref, lanes, **{third: gone})
            net.send(blocks, line.at[peer[0] - 1], got_line, peer)

    def finish():
        await_bytes(line, got_line)
        for part in range(rows // step):
            here = pl.ds(part * step, step)
            total = ref[(*target_of(), here, lanes)].astype(F32)
            for k in range(size[second] - 1):
                total = total + half[k, mine[third], here].astype(F32)
            for k in range(size[third] - 1):
                total = total + line[k, here].astype(F32)
            done(part * step, step, total)

    return start, after_first, after_second, finish


def plane_gather_stages(net, ref, lanes, order):
    first, second = order
    others = {"z": pl.ds(0, NZ - 1), "y": 1 - net.y}
    got_first, got_second = net.sem(), net.sem()

    def place(**given):
        where = {"z": net.z, "y": net.y}
        where.update(given)
        return ref.at[where["z"], where["y"], :, lanes]

    def pass_on(dim, sem, **held):
        for peer in net.peers(dim):
            net.send(place(**held), place(**held), sem, peer)

    def start():
        pass_on(first, got_first)

    def after_first():
        await_bytes(place(**{first: others[first]}), got_first)
        pass_on(second, got_second, **{first: ALL})

    def finish():
        await_bytes(place(**{first: ALL, second: others[second]}), got_second)

    return [start, after_first, finish]


def plane_scatter_stages(net, ref, lanes, order, bufs, emit):
    first, second = order
    wide, line = bufs[:2]
    got_wide, got_line = net.sem(), net.sem()
    rows, cols = wide.shape[-2:]
    step = min(rows, max(16, 32768 // cols))
    size = {"z": NZ, "y": 2}
    place = {"z": 1, "y": 2}
    mine = {"z": net.z, "y": net.y}

    def at(**given):
        where = dict(mine)
        where.update(given)
        return (where["z"], where["y"])

    def start():
        for peer in net.peers(first):
            there = at(**{first: peer[place[first]], second: ALL})
            net.send(ref.at[(*there, ALL, lanes)], wide.at[peer[0] - 1], got_wide, peer)

    def total(where, slot, here):
        value = ref[(*where, here, lanes)].astype(F32)
        for k in range(size[first] - 1):
            value = value + wide[k, slot, here].astype(F32)
        return value

    def after_first():
        await_bytes(wide, got_wide)
        for peer in net.peers(second):
            gone = peer[place[second]]
            there = at(**{second: gone})

            def add(part):
                here = pl.ds(mul(part, step), step)
                ref[(*there, here, lanes)] = total(there, gone, here).astype(BF)

            loop(rows // step, add)
            net.send(ref.at[(*there, ALL, lanes)], line.at[peer[0] - 1], got_line, peer)

    def final(here):
        value = total(at(), mine[second], here)
        for k in range(size[second] - 1):
            value = value + line[k, here].astype(F32)
        return value

    def finish():
        await_bytes(line, got_line)
        emit(final)

    return [start, after_first, finish]


def pieces_of(plan, widths):
    counts = {}
    for group, _, _ in plan:
        counts[group] = counts.get(group, 0) + 1
    return [
        (group, index * (widths[group] // counts[group]), widths[group] // counts[group], order)
        for group, index, order in plan
    ]


def layer_kernel(
    tok_in,
    doc,
    cot_in,
    wq_in,
    wo_in,
    wu_in,
    wd_in,
    qv_in,
    up_in,
    out_in,
    down_in,
    gain_in,
    shift_in,
    res_out,
    gtok_out,
    gq_out,
    go_out,
    gu_out,
    gd_out,
    gvec_out,
    wq,
    wo,
    wu,
    wux,
    wd,
    vbuf,
    tok,
    cot,
    pack,
    vecs,
    vq,
    vu,
    xin,
    qb,
    kb,
    vb,
    pb,
    bias,
    att,
    attb,
    attx,
    hat1,
    hat2,
    inv1,
    inv2,
    mid,
    fin,
    act,
    dge,
    rcv,
    own,
    snd,
    own_x,
    snd_s,
    rcv_s,
    snd_x,
    rcv_x,
    gff,
    gbr,
    dob,
    dsb,
    gqo,
    gu,
    gd,
    swap,
    acc,
    acc_qv,
    acc_up,
    gvecs,
    gv,
    vother,
    piece_bufs,
    res,
    gtok,
    st_q,
    st_o,
    st_u,
    st_ux,
    r_ux,
    st_d,
    sems,
    local_sems,
):
    net = Net(sems)
    core = net.core
    greeted = net.greet()

    locals_ = []

    def fetch(src, dst):
        copy = pltpu.make_async_copy(src, dst, local_sems.at[len(locals_)])
        copy.start()
        locals_.append(copy)

    def lanes_of(start, size):
        return pl.ds(pl.multiple_of(start, 128), size)

    for part in range(3):
        fetch(
            wq_in.at[:, lanes_of(part * WIDTH + core * OWN, OWN)],
            wq.at[net.z, net.y, net.x, :, pl.ds(part * OWN, OWN)],
        )
    fetch(wo_in.at[:, lanes_of(core * OWN, OWN)], wo.at[core, net.z, net.y, net.x])
    for zy in range(8):
        fetch(
            wu_in.at[:, lanes_of((zy * 2 + 1 - net.x) * 256 + core * 128, 128)],
            wux.at[:, pl.ds(zy * 128, 128)],
        )
    own_half = pl.ds(mul(net.x, 64), 64)
    for zy in range(8):
        fetch(
            wu_in.at[:, lanes_of((zy * 2 + net.x) * 256 + core * 128, 128)],
            wu.at[net.z, net.y, own_half, pl.ds(zy * 128, 128)],
        )
    fetch(wd_in.at[pl.ds(mul(core, 128), 128), :], wd.at[net.z, net.y])
    fetch(tok_in, tok)
    fetch(cot_in, cot)
    pack[...] = jnp.zeros_like(pack)
    pack[0:1, :] = qv_in[...].astype(F32)
    pack[1:3, :] = up_in[...].astype(F32)
    for row, ref in (
        (ROW_OUT, out_in),
        (ROW_DOWN, down_in),
        (ROW_GAIN, gain_in),
        (ROW_SHIFT, shift_in),
    ):
        value = ref[...].astype(F32)
        rows = slice(row, row + value.shape[0])
        pack[rows, 0:64] = jnp.where(net.x == 0, value, 0.0)
        pack[rows, 64:128] = jnp.where(net.x == 1, value, 0.0)
    vbuf[net.z, net.y, net.x] = pack[...].astype(BF)
    wo_own = wo.at[core]
    plan = pieces_of(GATHER, WIDTHS)
    sources = {"v": vbuf, "q": wq, "o": wo_own}

    def stages_of(group, lanes, order):
        if group == "d":
            return plane_gather_stages(net, wd, lanes, order)
        if group == "u":
            passing = plane_gather_stages(net, wu, lanes, order)
            got_x = net.sem()

            def cross():
                net.send(
                    wux.at[:, lanes],
                    wu.at[net.z, net.y, own_half, lanes],
                    got_x,
                    net.peers("x")[0],
                )

            def crossed():
                await_bytes(wux.at[:, lanes], got_x)
                passing[0]()

            return [cross, crossed, *passing[1:]]
        return gather_stages(net, sources[group], lanes, order)

    gathers = [
        stages_of(group, pl.ds(lane0, count), order) for group, lane0, count, order in plan
    ]
    greeted()
    ready = {("q", 0): 3, ("o", 0): 4, ("u", 0): 12, ("u", 1): 20, ("d", 0): 21}
    state = {"landed": 0}
    got_wo = []

    def gather(piece, stage):
        while state["landed"] < ready.get((plan[piece][0], stage), 0):
            locals_[state["landed"]].wait()
            state["landed"] += 1
        gathers[piece][stage]()
        group, lane0, count, _ = plan[piece]
        if group == "o" and stage == 3:
            half = wo_own.at[:, :, :, :, pl.ds(lane0, count)]
            got_wo.append(net.sibling(half, half))

    def spread_vectors():
        for z in range(NZ):
            for y in range(2):
                both = vbuf[z, y, 0].astype(F32) + vbuf[z, y, 1].astype(F32)
                vecs[:, pl.ds((z * 2 + y) * 128, 128)] = both
        for y in range(2):
            for x in range(2):
                at = pl.ds((y * 2 + x) * 128, 128)
                vq[0:8, at] = vbuf[core, y, x].astype(F32)[0:8]
                vq[8:16, at] = vbuf[core + 2, y, x].astype(F32)[0:8]
        for z in range(NZ):
            for y in range(2):
                block = vbuf[z, y, net.x].astype(F32)
                vu[0:1, pl.ds((z * 2 + y) * 128, 128)] = jnp.where(
                    core == 0, block[1:2], block[2:3]
                )
        acc[...] = jnp.zeros_like(acc)
        acc_up[...] = jnp.zeros_like(acc_up)

    def gain(n):
        return vecs[ROW_GAIN + n : ROW_GAIN + n + 1, :]

    def shift(n):
        return vecs[ROW_SHIFT + n : ROW_SHIFT + n + 1, :]

    def accumulate(row, value):
        parts = value.reshape(value.shape[0] // 8, 8, value.shape[1])
        acc[row] += jnp.sum(parts, axis=0)

    got = {}

    chunk = 32
    chunks = LEN // chunk

    def ln0(i):
        here = pl.ds(mul(i, chunk), chunk)
        hat, _ = normalize(tok[here, :].astype(F32))
        xin[core, here, :] = (hat * gain(0) + shift(0)).astype(BF)

    def attention_input():
        locals_[21].wait()
        loop(chunks, ln0)
        got["x"] = net.sibling(xin.at[core], xin.at[core])

    ends = []
    end = jnp.int32(0)
    for j in range(8):
        end = end + doc[0, j]
        ends.append(end)

    def segment(position):
        total = jnp.zeros(position.shape, jnp.int32)
        for value in ends:
            total = total + (position >= value).astype(jnp.int32)
        return total

    scale = 1.0 / (ALPHA * 8.0)

    def project(t):
        n = t // 2
        m = t % 2
        tile = pl.ds(mul(n, 256), 256)
        rows = pl.ds(mul(m, 256), 256)

        def part(index, dst, bias, factor):
            weight = wq[:, :, :, :, pl.ds(pl.multiple_of(index * OWN + n * 256, 256), 256)]
            value = dot_nn(xin[m], weight.reshape(WIDTH, 256))
            if bias is not None:
                value = value + vq[bias : bias + 1, tile]
            if factor is not None:
                value = value * factor
            dst[rows, tile] = value.astype(BF)

        part(0, qb, 0, scale)
        part(1, kb, None, None)
        part(2, vb, 8, None)

    def projections():
        got["x"].wait_recv()
        loop(4, project)

    lane = lax.broadcasted_iota(jnp.int32, (1, 128), 1)
    block = 128

    def masks():
        for r in range(NPOS // block):
            count = (r + 1) * block
            q_pos = r * block + lax.broadcasted_iota(jnp.int32, (block, 1), 0)
            k_pos = lax.broadcasted_iota(jnp.int32, (1, count), 1)
            allowed = (segment(q_pos) == segment(k_pos)) & (k_pos <= q_pos)
            bias[r * block : (r + 1) * block, 0:count] = jnp.where(allowed, 0.0, FILLER)

    def attend(half, pair):
        at = pl.ds(mul(pair, 128), 128)
        for r in (half, half + 2):
            rows = pl.ds(r * block, block)
            count = (r + 1) * block
            q = qb[rows, at]
            k = kb[0:count, at]
            v = vb[0:count, at]
            outs = []
            for head in range(2):
                mine = (lane < 64) if head == 0 else (lane >= 64)
                scores = dot_nt(jnp.where(mine, q, jnp.zeros_like(q)), k) + bias[rows, 0:count]
                top = jnp.max(scores, axis=1, keepdims=True)
                weights = jnp.exp2((scores - top) * (ALPHA * math.log2(math.e)))
                summed = dot_nn(weights.astype(BF), jnp.where(mine, v, jnp.ones_like(v)))
                turned = pltpu.roll(summed, 64, 1)
                inverse = 1.0 / jnp.where(mine, turned, summed)
                wide = jnp.concatenate([inverse] * (r + 1), axis=1)
                pb[pair * 2 + head, rows, 0:count] = (weights * wide).astype(BF)
                outs.append(summed * inverse)
            out = jnp.where(lane < 64, outs[0], outs[1])
            att[rows, at] = out
            attb[rows, at] = out.astype(BF)

    other_rows = pl.ds(mul(1 - core, LEN), LEN)
    own_rows = pl.ds(mul(core, LEN), LEN)
    got_att = []

    def half_rows(of_core, half):
        return pl.ds(pl.multiple_of(of_core * LEN + half * block, block), block)

    def attend_some(half, pair0):
        loop(2, lambda i: attend(half, i + pair0))
        if pair0 == 2:
            sent = attb.at[half_rows(1 - core, half), :]
            got_att.append(net.sibling(sent, attx.at[pl.ds(half * block, block), :]))

    own_group = net.x * 2 + core
    across_group = (1 - net.x) * 2 + core

    def branch_tile(half, n):
        lanes = pl.ds(mul(n % 2, 256), 256)
        mine = wo[n // 2, pl.ds(2 * core, 2), :, :, :, lanes].reshape(OWN, 256)
        theirs = wo[n // 2, pl.ds(2 * (1 - core), 2), :, :, :, lanes].reshape(OWN, 256)
        at = pl.ds(mul(n, 256), 256)
        here = pl.ds(half * block, block)
        value = dot_nn(attb[half_rows(core, half), :], mine)
        own[here, at] = value + dot_nn(attx[here, :], theirs)

    def ln12(i):
        here = pl.ds(mul(i, chunk), chunk)
        first, first_inv = normalize(own[here, :] + vecs[ROW_OUT : ROW_OUT + 1, :])
        hat1[here, :] = first
        inv1[here, :] = jnp.broadcast_to(first_inv, (chunk, 128))
        middle = tok[here, :].astype(F32) + first * gain(1) + shift(1)
        mid[here, :] = middle
        second, second_inv = normalize(middle)
        hat2[here, :] = second
        inv2[here, :] = jnp.broadcast_to(second_inv, (chunk, 128))
        fin[own_group, here, :] = (second * gain(2) + shift(2)).astype(BF)

    class Share:
        def __init__(self, ref):
            self.ref = ref
            self.beside, self.across, self.passed = [], [], []

        def send(self, half):
            rows = pl.ds(half * 128, 128)
            view = self.ref.at[own_group, rows]
            self.beside.append(net.sibling(view, view))
            self.across.append(net.send(view, view, net.sem(), net.peers("x")[0]))

        def pass_on(self, half):
            self.across[half].wait_recv()
            view = self.ref.at[across_group, pl.ds(half * 128, 128)]
            self.passed.append(net.sibling(view, view))

        def wait_beside(self):
            for copy in self.beside:
                copy.wait_recv()

        def wait_passed(self):
            for copy in self.passed:
                copy.wait_recv()
            self.passed = []

    class Reduce:
        def __init__(self, product):
            self.product = product
            self.beside, self.across = [], []

        def group_rows(self, group):
            return pl.ds(mul(group, LEN), LEN)

        def multiply_here(self, n):
            at = pl.ds(n * 256, 256)
            value = self.product(self.group_rows(net.x * 2 + 1 - core), n)
            snd_s[net.x, :, at] = value.astype(BF)
            own[:, at] = self.product(self.group_rows(own_group), n)

        def multiply_there(self, n):
            at = pl.ds(n * 256, 256)
            value = self.product(self.group_rows((1 - net.x) * 2 + 1 - core), n)
            snd_s[1 - net.x, :, at] = value.astype(BF)
            self.beside.append(net.sibling(snd_s.at[:, :, at], rcv_s.at[:, :, at]))
            own_x[:, at] = self.product(self.group_rows(across_group), n)

        def multiply(self, n):
            self.multiply_here(n)
            self.multiply_there(n)

        def cross(self, n):
            at = pl.ds(n * 256, 256)
            self.beside[n].wait_recv()

            def add(i):
                here = pl.ds(mul(i, 64), 64)
                over = own_x[here, at] + rcv_s[1 - net.x, here, at].astype(F32)
                snd_x[here, at] = over.astype(BF)
                own[here, at] += rcv_s[net.x, here, at].astype(F32)

            loop(4, add)
            self.across.append(
                net.send(snd_x.at[:, at], rcv_x.at[:, at], net.sem(), net.peers("x")[0])
            )

        def wait(self):
            for copy in self.across:
                copy.wait_recv()

        def free(self):
            for copy in self.beside + self.across:
                copy.wait_send()

    share_fin, share_gff = Share(fin), Share(gff)
    row_copies = []

    def copy_out(src, dst):
        row_copies.append(pltpu.make_async_copy(src, dst, local_sems.at[23 + len(row_copies)]))
        row_copies[-1].start()

    def branch_half(half):
        got_att[half].wait_recv()
        if half == 0:
            loop(2, lambda i: branch_tile(half, core * 2 + i))
            for part in got_wo:
                part.wait_recv()
            loop(2, lambda i: branch_tile(half, (1 - core) * 2 + i))
        else:
            loop(4, functools.partial(branch_tile, half))
        loop(chunks // 2, lambda i: ln12(i + half * (chunks // 2)))
        share_fin.send(half)

    root = math.sqrt(2.0 / math.pi)

    def up_tile(n, group):
        at = pl.ds(mul(n, 256), 256)
        rows = pl.ds(mul(group, LEN), LEN)
        u = dot_nn(fin[group], wu[:, :, :, at].reshape(WIDTH, 256)) + vu[0:1, at]
        square = u * u
        inner = jnp.tanh(root * (u + 0.044715 * (square * u)))
        half = 0.5 * (1.0 + inner)
        act[rows, at] = (u * half).astype(BF)
        slope = 0.5 * u * (1.0 - inner * inner) * (root * (1.0 + (3 * 0.044715) * square))
        dge[rows, at] = (half + slope).astype(BF)

    def up_group(group):
        loop(4, lambda n: up_tile(n, group))

    def up_beside():
        share_fin.wait_beside()
        up_group(net.x * 2 + 1 - core)

    def up_last():
        share_fin.wait_passed()
        up_group((1 - net.x) * 2 + 1 - core)

    def down_product(rows, n):
        return dot_nn(act[rows, :], wd[:, :, :, pl.ds(n * 256, 256)].reshape(FF4, 256))

    down = Reduce(down_product)

    def tiles_of(width, count, body):
        return [functools.partial(body, lane0, count) for lane0 in range(0, width, count)]

    def attention_input_and_masks():
        attention_input()
        masks()

    steps = [
        spread_vectors,
        attention_input_and_masks,
        projections,
        lambda: attend_some(0, 0),
        lambda: attend_some(0, 2),
        lambda: attend_some(1, 0),
        lambda: attend_some(1, 2),
        lambda: branch_half(0),
        lambda: branch_half(1),
        lambda: share_fin.pass_on(0),
        lambda: share_fin.pass_on(1),
    ]
    steps += [
        lambda: up_group(own_group),
        up_beside,
        lambda: up_group(across_group),
        up_last,
        functools.partial(down.multiply, 0),
        functools.partial(down.multiply, 1),
        functools.partial(down.cross, 0),
        functools.partial(down.multiply, 2),
        functools.partial(down.cross, 1),
        functools.partial(down.multiply, 3),
        functools.partial(down.cross, 2),
        functools.partial(down.cross, 3),
    ]
    filled = ends[-1]

    def upstream_of(i):
        here = pl.ds(mul(i, chunk), chunk)
        position = core * LEN + i * chunk + lax.broadcasted_iota(jnp.int32, (chunk, 1), 0)
        return cot[here, :].astype(F32) * (position < filled).astype(F32)

    def top_tile(i):
        here = pl.ds(mul(i, chunk), chunk)
        value = own[here, :] + rcv_x[here, :].astype(F32) + vecs[ROW_DOWN : ROW_DOWN + 1, :]
        hat, inv = normalize(value)
        res[here, :] = (mid[here, :] + hat * gain(3) + shift(3)).astype(BF)
        upstream = upstream_of(i)
        grad = norm_back(hat, inv, gain(3), upstream).astype(BF)
        gff[own_group, here, :] = grad
        accumulate(ROW_GAIN + 3, upstream * hat)
        accumulate(ROW_SHIFT + 3, upstream)
        accumulate(ROW_DOWN, grad.astype(F32))

    def top():
        locals_[22].wait()
        down.wait()
        for half in range(2):
            loop(chunks // 2, lambda i: top_tile(i + half * (chunks // 2)))
            share_gff.send(half)
        copy_out(res, res_out)

    steps.append(top)
    for piece, stage in GATHER_STEPS:
        if piece < 0:
            steps[stage]()
        else:
            gather(piece, stage)


    out_copies = []

    def deliver(src, dst):
        copy = pltpu.make_async_copy(src, dst, local_sems.at[25 + len(out_copies)])
        copy.start()
        out_copies.append((copy, net.sibling(src, dst)))

    def ship(group, lane0, count):
        if group == "d":
            at = pl.ds(lane0, count)
            deliver(st_d.at[:, at], gd_out.at[pl.ds(mul(core, 128), 128), at])
        if group == "u":
            for part in range(2):
                for zy in range(lane0 // 128, (lane0 + count) // 128):
                    deliver(
                        st_u.at[part, :, pl.ds(zy * 128, 128)],
                        gu_out.at[:, lanes_of((zy * 2 + part) * 256 + core * 128, 128)],
                    )
        if group == "o":
            deliver(
                st_o.at[:, pl.ds(lane0, count)], go_out.at[:, lanes_of(core * OWN + lane0, count)]
            )
        if group == "q":
            start = (lane0 // OWN) * WIDTH + lane0 % OWN
            deliver(
                st_q.at[:, pl.ds(lane0, count)], gq_out.at[:, lanes_of(core * OWN + start, count)]
            )

    plan = pieces_of(SCATTER, WIDTHS)
    sums = {"o": gqo, "q": gqo, "v": gv}
    stage_of = {"o": st_o, "q": st_q, "v": gvec_out}

    def store_to(stage, lane0, count):
        def done(row0, size, total):
            stage[row0 : row0 + size, lane0 : lane0 + count] = total

        return done

    def sums_of(group, lane0, count, order, bufs):
        lanes = pl.ds(lane0, count)
        if group == "d":

            def keep(total):
                for part in range(4):
                    here = pl.ds(part * 32, 32)
                    st_d[here, lanes] = total(here)

            return plane_scatter_stages(net, gd, lanes, order, bufs, keep)
        if group == "u":
            got_x = net.sem()

            def cross(total):
                for part in range(2):
                    here = pl.ds(part * 32, 32)
                    theirs = pl.multiple_of((1 - net.x) * 64 + part * 32, 32)
                    st_ux[here, lanes] = total(pl.ds(theirs, 32)).astype(BF)
                net.send(st_ux.at[:, lanes], r_ux.at[:, lanes], got_x, net.peers("x")[0])
                for part in range(2):
                    here = pl.ds(part * 32, 32)
                    mine = pl.multiple_of(net.x * 64 + part * 32, 32)
                    st_u[net.x, here, lanes] = total(pl.ds(mine, 32))

            def crossed():
                await_bytes(r_ux.at[:, lanes], got_x)
                st_u[1 - net.x, :, lanes] = r_ux[:, lanes].astype(F32)

            return [*plane_scatter_stages(net, gu, lanes, order, bufs, cross), crossed]
        base = 3 * OWN if group == "o" else 0
        return scatter_stages(
            net,
            sums[group],
            pl.ds(base + lane0, count),
            order,
            bufs,
            store_to(stage_of[group], lane0, count),
        )

    scatters = [
        sums_of(*piece, bufs) for piece, bufs in zip(plan, piece_bufs, strict=True)
    ]

    def scatter(piece, stage):
        scatters[piece][stage]()
        if stage == len(scatters[piece]) - 1:
            ship(*plan[piece][:3])

    def over_rows(chip_x, left, right, out, at, count, add):
        groups = pl.ds(chip_x * 2, 2)

        def tile(z):
            a, b = left(groups, pl.ds(mul(z, 256), 256)), right(groups, at)
            value = dot_tn(a.reshape(NPOS, 256), b.reshape(NPOS, count)).reshape(2, 128, count)
            if add:
                value = value + out[z, :, :, at].astype(F32)
            out[z, :, :, at] = value.astype(BF)

        loop(NZ, tile)

    def rows_of(ref):
        return lambda groups, at: ref[pl.ds(mul(groups.start, LEN), NPOS), at]

    def groups_of(ref):
        return lambda groups, at: ref[groups, :, at]

    def gdown_piece(chip_x, add, lane0, count):
        at = pl.ds(lane0, count)
        if add:
            share_gff.wait_passed()
        over_rows(chip_x, rows_of(act), groups_of(gff), gd, at, count, add)

    def gpre_tile(group, z):
        at = pl.ds(mul(z, 256), 256)
        rows = pl.ds(mul(group, LEN), LEN)
        weight = wd[z].reshape(256, WIDTH)
        value = dot_nt(gff[group], weight) * dge[rows, at].astype(F32)
        value = value.astype(BF)
        dge[rows, at] = value
        acc_up[:, at] += jnp.sum(value.astype(F32).reshape(32, 8, 256), axis=0)

    def gpre_group(group):
        loop(NZ, functools.partial(gpre_tile, group))

    def gpre_beside():
        share_gff.wait_beside()
        gpre_group(net.x * 2 + 1 - core)

    def gpre_last():
        share_gff.wait_passed()
        gpre_group((1 - net.x) * 2 + 1 - core)

    def gup_piece(chip_x, add, lane0, count):
        at = pl.ds(lane0, count)
        over_rows(chip_x, groups_of(fin), rows_of(dge), gu, at, count, add)

    def grad_ffn_in_product(rows, n):
        return dot_nt(dge[rows, :], wu[n].reshape(256, FF4))

    gfi = Reduce(grad_ffn_in_product)

    def grad_ffn_in_here():
        down.free()
        for n in range(4):
            gfi.multiply_here(n)

    def grad_ffn_in_there():
        for n in range(4):
            gfi.multiply_there(n)

    def grad_ffn_in_cross():
        for n in range(4):
            gfi.cross(n)

    def middle_tile(i):
        here = pl.ds(mul(i, chunk), chunk)
        grad_in = own[here, :] + rcv_x[here, :].astype(F32)
        second = hat2[here, :]
        accumulate(ROW_GAIN + 2, grad_in * second)
        accumulate(ROW_SHIFT + 2, grad_in)
        grad_mid = upstream_of(i) + norm_back(second, inv2[here, 0:1], gain(2), grad_in)
        mid[here, :] = grad_mid
        first = hat1[here, :]
        accumulate(ROW_GAIN + 1, grad_mid * first)
        accumulate(ROW_SHIFT + 1, grad_mid)
        grad = norm_back(first, inv1[here, 0:1], gain(1), grad_mid).astype(BF)
        gbr[core, here, :] = grad
        accumulate(ROW_OUT, grad.astype(F32))

    def grad_middle():
        gfi.wait()
        loop(chunks, middle_tile)
        got["gbr"] = net.sibling(gbr.at[core], gbr.at[core])

    go = gqo.at[:, :, :, :, pl.ds(3 * OWN, OWN)]

    def gout_tile(k, cols, put):
        left = attb[:, pl.ds(mul(k, 256), 256)]
        grad = gbr[:, :, cols].reshape(NPOS, OWN)
        put(k, dot_tn(left, grad).astype(BF).reshape(2, 2, 64, OWN))

    def put_swap(k, value):
        swap[k] = value

    def put_own(k, value):
        gqo[2 * core + k, :, :, :, pl.ds(3 * OWN, OWN)] = value


    def gatt_tile(t):
        k = t // 2
        m = t % 2
        left = wo[0, 2 * core + k].reshape(256, OWN)
        right = wo[1, 2 * core + k].reshape(256, OWN)
        value = dot_nt(gbr[m, :, 0:OWN], left) + dot_nt(gbr[m, :, OWN:WIDTH], right)
        dob[pl.ds(mul(m, 256), 256), pl.ds(mul(k, 256), 256)] = value.astype(BF)

    def grad_out():
        got["gbr"].wait_recv()
        loop(2, lambda k: gout_tile(k, lanes_of((1 - core) * OWN, OWN), put_swap))
        got["swap"] = net.sibling(swap, go.at[pl.ds(2 * core, 2)])
        loop(2, lambda k: gout_tile(k, lanes_of(core * OWN, OWN), put_own))
        loop(4, gatt_tile)

    def attend_back(pair):
        at = pl.ds(mul(pair, 128), 128)
        sums = []
        for head in range(2):
            mine = (lane < 64) if head == 0 else (lane >= 64)
            queries_ = []
            for r in range(NPOS // block):
                rows = pl.ds(r * block, block)
                count = (r + 1) * block
                grad = dob[rows, at]
                grad = jnp.where(mine, grad, jnp.zeros_like(grad))
                delta = jnp.sum(grad.astype(F32) * att[rows, at], axis=1, keepdims=True)
                probs = pb[pair * 2 + head, rows, 0:count].astype(F32)
                grad_probs = dot_nt(grad, vb[0:count, at])
                scores = (probs * (grad_probs - delta)).astype(BF)
                dsb[rows, 0:count] = scores
                queries_.append(dot_nn(scores, kb[0:count, at]))
            keys_, values_ = [], []
            for r in range(NPOS // block):
                rows = pl.ds(r * block, NPOS - r * block)
                cols = pl.ds(r * block, block)
                keys_.append(dot_tn(dsb[rows, cols], qb[rows, at]))
                values_.append(dot_tn(pb[pair * 2 + head, rows, cols], dob[rows, at]))
            sums.append((queries_, keys_, values_))
        total_q = jnp.zeros((8, 128), F32)
        total_v = jnp.zeros((8, 128), F32)
        for r in range(NPOS // block):
            rows = pl.ds(r * block, block)
            merged = [
                (jnp.where(lane < 64, sums[0][i][r], sums[1][i][r]) * power).astype(BF)
                for i, power in enumerate((float(ALPHA), float(ALPHA), 1.0))
            ]
            grad_q = merged[0] * jnp.asarray(scale, BF)
            qb[rows, at] = grad_q
            kb[rows, at] = merged[1]
            vb[rows, at] = merged[2]
            total_q += jnp.sum(grad_q.astype(F32).reshape(block // 8, 8, 128), axis=0)
            total_v += jnp.sum(merged[2].astype(F32).reshape(block // 8, 8, 128), axis=0)
        acc_qv[0, :, at] = total_q
        acc_qv[1, :, at] = total_v

    def gqkv_piece(lane0, count):
        ref = (qb, kb, vb)[lane0 // OWN]

        def tile(z):
            left = xin[:, :, pl.ds(mul(z, 256), 256)].reshape(NPOS, 256)
            value = dot_tn(left, ref[:, lane0 % OWN : lane0 % OWN + count]).astype(BF)
            gqo[z, :, :, :, pl.ds(lane0, count)] = value.reshape(2, 2, 64, count)

        loop(NZ, tile)

    def gai_tile(rows, dst):
        def body(z):
            value = None
            for part, ref in enumerate((qb, kb, vb)):
                weight = wq[z, :, :, :, pl.ds(part * OWN, OWN)].reshape(256, OWN)
                term = dot_nt(ref[rows, :], weight)
                value = term if value is None else value + term
            dst[:, pl.ds(mul(z, 256), 256)] = value

        loop(NZ, body)

    def grad_attn_in():
        gai_tile(other_rows, snd)
        got["gai"] = net.sibling(snd, rcv)
        gai_tile(own_rows, own)

    def bottom_tile(i):
        here = pl.ds(mul(i, chunk), chunk)
        hat, inv = normalize(tok[here, :].astype(F32))
        grad_in = own[here, :] + rcv[here, :]
        accumulate(ROW_GAIN, grad_in * hat)
        accumulate(ROW_SHIFT, grad_in)
        gtok[here, :] = mid[here, :] + norm_back(hat, inv, gain(0), grad_in)

    def bottom():
        got["gai"].wait_recv()
        loop(chunks, bottom_tile)
        copy_out(gtok, gtok_out)
        for row in range(16):
            gvecs[row : row + 1, :] = jnp.sum(acc[row], axis=0, keepdims=True)
        row_id = lax.broadcasted_iota(jnp.int32, (16, 1), 0)
        for z in range(NZ):
            for y in range(2):
                base = gvecs[:, pl.ds((z * 2 + y) * 128, 128)]
                for x in range(2):
                    at = pl.ds((y * 2 + x) * 128, 128)
                    kind = 0 if z < 2 else 1
                    qv_row = jnp.sum(acc_qv[kind, :, at], axis=0, keepdims=True)
                    qv_row = jnp.where(core == z % 2, qv_row, 0.0)
                    up_at = pl.ds((z * 2 + y) * 128, 128)
                    up_row = jnp.sum(acc_up[:, up_at], axis=0, keepdims=True)
                    up_row = jnp.where(net.x == x, up_row, 0.0)
                    value = base + jnp.where(row_id == 0, qv_row, 0.0)
                    gv[z, y, x] = value + jnp.where(row_id == 1 + core, up_row, 0.0)

    steps = [
        lambda: None,
        lambda: gpre_group(own_group),
        gpre_beside,
        lambda: share_gff.pass_on(0),
        lambda: share_gff.pass_on(1),
        *tiles_of(WIDTH, 512, functools.partial(gdown_piece, 1 - net.x, True)),
        lambda: gpre_group(across_group),
        gpre_last,
        *tiles_of(FF4, 512, functools.partial(gup_piece, 1 - net.x, True)),
        grad_ffn_in_there,
        grad_ffn_in_cross,
        grad_middle,
        grad_out,
        lambda: got["swap"].wait_recv(),
    ]
    steps += [functools.partial(loop, 1, lambda i, pair=p: attend_back(i + pair)) for p in range(4)]
    steps += tiles_of(3 * OWN, 512, gqkv_piece)
    steps += [grad_attn_in, bottom]

    def both(piece, width):
        for step in tiles_of(width, 512, functools.partial(piece, net.x, False)):
            step()

    steps += [
        lambda: both(gdown_piece, WIDTH),
        lambda: both(gup_piece, FF4),
        grad_ffn_in_here,
    ]
    for piece, stage in SCATTER_STEPS:
        if piece < 0:
            steps[stage]()
        else:
            scatter(piece, stage)
    got_vec = net.sibling(gvec_out, vother)
    got_vec.wait_send()
    got_vec.wait_recv()
    gvec_out[...] = gvec_out[...] + vother[...]
    for copy in row_copies:
        copy.wait()
    for copy, remote in out_copies:
        copy.wait()
        remote.wait_recv()
    net.drain(net.unsent, (*down.beside, *down.across, got_vec))


def scatter_bufs(group, count, order):
    rows, dtype = {"v": (16, F32)}.get(group, (64, BF))
    size = {"z": NZ, "y": 2, "x": 2}
    if group in "du":
        first, second = order
        return [
            pltpu.VMEM((size[first] - 1, size[second], 128, count), BF),
            pltpu.VMEM((size[second] - 1, 128, count), BF),
        ]
    first, second, third = order
    left = [size[dim] for dim in "zyx" if dim != first]
    return [
        pltpu.VMEM((size[first] - 1, *left, rows, count), dtype),
        pltpu.VMEM((size[second] - 1, size[third], rows, count), dtype),
        pltpu.VMEM((size[third] - 1, rows, count), dtype),
    ]


def hand_out_kernel(*refs):
    large, vec = refs[:6], refs[6]
    outs, small = refs[7:13], refs[13:19]
    for src, dst in zip(large, outs, strict=True):
        dst[...] = src[...]
    right = lax.axis_index("dp") % 2 == 1
    values = vec[...]
    half = jnp.where(right, values[:, 64:], values[:, :64])
    small[0][...] = values[0:1]
    small[1][...] = half[ROW_OUT : ROW_OUT + 1]
    small[2][...] = values[1:3]
    small[3][...] = half[ROW_DOWN : ROW_DOWN + 1]
    small[4][...] = half[ROW_GAIN : ROW_GAIN + 4]
    small[5][...] = half[ROW_SHIFT : ROW_SHIFT + 4]

def fused(
    tokens,
    doc_lengths,
    cotangent,
    w_qkv,
    qv_bias,
    w_out,
    out_bias,
    w_up,
    up_bias,
    w_down,
    down_bias,
    norm_gain,
    norm_bias,
):
    vmem = pl.BlockSpec(memory_space=pltpu.VMEM)
    anywhere = pl.BlockSpec(memory_space=pl.ANY)
    scratch = [
        pltpu.VMEM((NZ, 2, 2, 64, 3 * OWN), BF),
        pltpu.VMEM((2, NZ, 2, 2, 64, OWN), BF),
        pltpu.VMEM((NZ, 2, 128, FF4), BF),
        pltpu.VMEM((64, FF4), BF),
        pltpu.VMEM((NZ, 2, 128, WIDTH), BF),
        pltpu.VMEM((NZ, 2, 2, 16, 128), BF),
        pltpu.VMEM((LEN, WIDTH), BF),
        pltpu.VMEM((LEN, WIDTH), BF),
        pltpu.VMEM((16, 128), F32),
        pltpu.VMEM((16, WIDTH), F32),
        pltpu.VMEM((16, OWN), F32),
        pltpu.VMEM((8, FF4), F32),
        pltpu.VMEM((2, LEN, WIDTH), BF),
        pltpu.VMEM((NPOS, OWN), BF),
        pltpu.VMEM((NPOS, OWN), BF),
        pltpu.VMEM((NPOS, OWN), BF),
        pltpu.VMEM((8, NPOS, NPOS), BF),
        pltpu.VMEM((NPOS, NPOS), F32),
        pltpu.VMEM((NPOS, OWN), F32),
        pltpu.VMEM((NPOS, OWN), BF),
        pltpu.VMEM((LEN, OWN), BF),
        pltpu.VMEM((LEN, WIDTH), F32),
        pltpu.VMEM((LEN, WIDTH), F32),
        pltpu.VMEM((LEN, 128), F32),
        pltpu.VMEM((LEN, 128), F32),
        pltpu.VMEM((LEN, WIDTH), F32),
        pltpu.VMEM((4, LEN, WIDTH), BF),
        pltpu.VMEM((4 * LEN, FF4), BF),
        pltpu.VMEM((4 * LEN, FF4), BF),
        pltpu.VMEM((LEN, WIDTH), F32),
        pltpu.VMEM((LEN, WIDTH), F32),
        pltpu.VMEM((LEN, WIDTH), F32),
        pltpu.VMEM((LEN, WIDTH), F32),
        pltpu.VMEM((2, LEN, WIDTH), BF),
        pltpu.VMEM((2, LEN, WIDTH), BF),
        pltpu.VMEM((LEN, WIDTH), BF),
        pltpu.VMEM((LEN, WIDTH), BF),
        pltpu.VMEM((4, LEN, WIDTH), BF),
        pltpu.VMEM((2, LEN, WIDTH), BF),
        pltpu.VMEM((NPOS, OWN), BF),
        pltpu.VMEM((NPOS, NPOS), BF),
        pltpu.VMEM((NZ, 2, 2, 64, 4 * OWN), BF),
        pltpu.VMEM((NZ, 2, 128, FF4), BF),
        pltpu.VMEM((NZ, 2, 128, WIDTH), BF),
        pltpu.VMEM((2, 2, 2, 64, OWN), BF),
        pltpu.VMEM((16, 8, WIDTH), F32),
        pltpu.VMEM((2, 8, OWN), F32),
        pltpu.VMEM((8, FF4), F32),
        pltpu.VMEM((16, WIDTH), F32),
        pltpu.VMEM((NZ, 2, 2, 16, 128), F32),
        pltpu.VMEM((16, 128), F32),
        [
            scatter_bufs(group, count, order)
            for group, _, count, order in pieces_of(SCATTER, WIDTHS)
        ],
        pltpu.VMEM((LEN, WIDTH), BF),
        pltpu.VMEM((LEN, WIDTH), F32),
        pltpu.VMEM((64, 3 * OWN), F32),
        pltpu.VMEM((64, OWN), F32),
        pltpu.VMEM((2, 64, FF4), F32),
        pltpu.VMEM((64, FF4), BF),
        pltpu.VMEM((64, FF4), BF),
        pltpu.VMEM((128, WIDTH), F32),
        pltpu.SemaphoreType.DMA((800,)),
        pltpu.SemaphoreType.DMA((90,)),
    ]
    outs = pl.pallas_call(
        layer_kernel,
        out_shape=[
            jax.ShapeDtypeStruct((LEN, WIDTH), BF),
            jax.ShapeDtypeStruct((LEN, WIDTH), F32),
            jax.ShapeDtypeStruct((64, 3 * WIDTH), F32),
            jax.ShapeDtypeStruct((64, WIDTH), F32),
            jax.ShapeDtypeStruct((64, 4 * FF4), F32),
            jax.ShapeDtypeStruct((256, WIDTH), F32),
            jax.ShapeDtypeStruct((16, 128), F32),
        ],
        in_specs=[anywhere, pl.BlockSpec(memory_space=pltpu.SMEM), anywhere]
        + [anywhere] * 4
        + [vmem] * 6,
        out_specs=[anywhere] * 6 + [vmem],
        scratch_shapes=scratch,
        compiler_params=pltpu.CompilerParams(
            collective_id=0, has_side_effects=True, vmem_limit_bytes=63 * MIB
        ),
        name="layer",
    )(
        tokens[0],
        doc_lengths,
        cotangent[0],
        w_qkv,
        w_out,
        w_up,
        w_down,
        qv_bias.reshape(1, 128),
        up_bias.reshape(2, 128),
        out_bias.reshape(1, 64),
        down_bias.reshape(1, 64),
        norm_gain,
        norm_bias,
    )
    *large, vec = outs
    done = pl.pallas_call(
        hand_out_kernel,
        out_shape=[jax.ShapeDtypeStruct(array.shape, array.dtype) for array in large]
        + [
            jax.ShapeDtypeStruct((1, 128), F32),
            jax.ShapeDtypeStruct((1, 64), F32),
            jax.ShapeDtypeStruct((2, 128), F32),
            jax.ShapeDtypeStruct((1, 64), F32),
            jax.ShapeDtypeStruct((4, 64), F32),
            jax.ShapeDtypeStruct((4, 64), F32),
        ],
        in_specs=[vmem] * 7,
        out_specs=[vmem] * 12,
        compiler_params=pltpu.CompilerParams(vmem_limit_bytes=63 * MIB),
        name="hand_out",
    )(*large, vec)
    result, grad_inputs, grad_qkv, grad_out, grad_up, grad_down = done[:6]
    grad_qv, grad_out_shift, grad_up_shift, grad_down_shift, grad_gain, grad_shift = done[6:]
    return (
        result[None],
        grad_inputs[None],
        grad_qkv,
        grad_qv.reshape(128),
        grad_out,
        grad_out_shift.reshape(64),
        grad_up,
        grad_up_shift.reshape(256),
        grad_down,
        grad_down_shift.reshape(64),
        grad_gain,
        grad_shift,
    )


def solution(mesh):
    placed = (
        P("dp", "blk", None),
        P("dp", None),
        P("dp", "blk", None),
        P("dp", None),
        P("dp"),
        P("dp", None),
        P("dp"),
        P("dp", None),
        P("dp"),
        P("dp", None),
        P("dp"),
        P(None, "dp"),
        P(None, "dp"),
    )
    sizes = (mesh.shape["dp"], mesh.shape["blk"])
    return jax.shard_map(
        fused if sizes == (NZ * 4, 2) else shards,
        mesh=mesh,
        in_specs=placed,
        out_specs=(
            P("dp", "blk", None),
            P("dp", "blk", None),
            P("dp", None),
            P("dp"),
            P("dp", None),
            P("dp"),
            P("dp", None),
            P("dp"),
            P("dp", None),
            P("dp"),
            P(None, "dp"),
            P(None, "dp"),
        ),
        check_vma=False,
    )
```

```python
import functools
import math

import jax
import jax.numpy as jnp
from jax import lax
from jax.experimental import pallas as pl
from jax.experimental.pallas import tpu as pltpu
from jax.sharding import PartitionSpec as P

HEADS = 16
ALPHA = 32


EPSILON = 1e-05
FILLER = -1000000000.0


def normalize(values):
    center = values - jnp.mean(values, axis=-1, keepdims=True)
    inverse = lax.rsqrt(jnp.mean(center * center, axis=-1, keepdims=True) + EPSILON)
    return (center * inverse, inverse)


def norm_back(normed, inverse, gain_row, upstream):
    scaled = upstream * gain_row
    return inverse * (
        scaled
        - jnp.mean(scaled, axis=-1, keepdims=True)
        - normed * jnp.mean(scaled * normed, axis=-1, keepdims=True)
    )


def segment_of(position, doc_ends):
    return jnp.sum((position[:, None] >= doc_ends[None, :]).astype(jnp.int32), axis=1)


def gelu_tanh(values):
    return jax.nn.gelu(values, approximate=True)


def shards(
    tokens,
    doc_lengths,
    cotangent,
    w_qkv,
    qv_bias,
    w_out,
    out_bias,
    w_up,
    up_bias,
    w_down,
    down_bias,
    norm_gain,
    norm_bias,
):
    inputs = tokens[0].astype(jnp.float32)
    length = inputs.shape[0]
    model_width = inputs.shape[1]
    block_count = lax.axis_size("blk")
    seq_len = length * block_count
    offset = lax.axis_index("blk") * length
    doc_ends = jnp.cumsum(doc_lengths[0])
    filled = doc_ends[-1]
    query_pos = offset + jnp.arange(length, dtype=jnp.int32)
    query_seg = segment_of(query_pos, doc_ends)
    valid_rows = (query_pos < filled).astype(jnp.float32)
    key_seg = segment_of(jnp.arange(seq_len, dtype=jnp.int32), doc_ends)
    last_query = offset + length - 1

    def block_meets(first_row, piece_rows):
        first_at = jnp.asarray(first_row, jnp.int32)
        first_seg = lax.dynamic_index_in_dim(key_seg, first_at, keepdims=False)
        last_seg = lax.dynamic_index_in_dim(key_seg, first_at + piece_rows - 1, keepdims=False)
        return (first_at <= last_query) & (first_seg <= query_seg[-1]) & (last_seg >= query_seg[0])

    gathered = (
        lax.all_gather(w_qkv, "dp", axis=0, tiled=True),
        lax.all_gather(qv_bias, "dp", axis=0, tiled=True),
        lax.all_gather(w_out, "dp", axis=0, tiled=True),
        lax.all_gather(out_bias, "dp", axis=0, tiled=True),
        lax.all_gather(w_up, "dp", axis=0, tiled=True),
        lax.all_gather(up_bias, "dp", axis=0, tiled=True),
        lax.all_gather(w_down, "dp", axis=0, tiled=True),
        lax.all_gather(down_bias, "dp", axis=0, tiled=True),
        lax.all_gather(norm_gain, "dp", axis=1, tiled=True),
        lax.all_gather(norm_bias, "dp", axis=1, tiled=True),
    )
    (
        qkv_weight,
        qv_shift,
        out_weight,
        out_shift,
        up_weight,
        up_shift,
        down_weight,
        down_shift,
        gain_all,
        shift_all,
    ) = gathered
    gain_rows = gain_all.astype(jnp.float32)
    shift_rows = shift_all.astype(jnp.float32)
    query_scale = 1.0 / (ALPHA * math.sqrt(model_width // HEADS))
    first_hat, first_inv = normalize(inputs)
    attn_in = (first_hat * gain_rows[0] + shift_rows[0]).astype(jnp.bfloat16)
    projected = jnp.dot(attn_in, qkv_weight, preferred_element_type=jnp.float32)
    qv_float = qv_shift.astype(jnp.float32)
    queries = ((projected[:, :model_width] + qv_float[:model_width]) * query_scale).astype(
        jnp.bfloat16
    )
    keys_own = projected[:, model_width : 2 * model_width].astype(jnp.bfloat16)
    values_own = (projected[:, 2 * model_width :] + qv_float[model_width:]).astype(jnp.bfloat16)
    query_heads = queries.reshape(length, HEADS, -1)

    def scores_of(key_piece, first_row):
        piece_rows = key_piece.shape[0]
        piece_pos = first_row + jnp.arange(piece_rows, dtype=jnp.int32)
        piece_seg = lax.dynamic_slice_in_dim(key_seg, jnp.asarray(first_row, jnp.int32), piece_rows)
        allowed_pairs = (query_seg[:, None] == piece_seg[None, :]) & (
            piece_pos[None, :] <= query_pos[:, None]
        )
        raw_scores = jnp.einsum(
            "qhd,khd->hqk",
            query_heads,
            key_piece.reshape(piece_rows, HEADS, -1),
            preferred_element_type=jnp.float32,
        )
        return (jnp.where(allowed_pairs[None], raw_scores, FILLER), allowed_pairs[None])

    head_dim = model_width // HEADS
    start_state = (
        jnp.full((HEADS, length), FILLER, jnp.float32),
        jnp.zeros((HEADS, length), jnp.float32),
        jnp.zeros((HEADS, length, head_dim), jnp.float32),
    )
    accumulate_first_row = jnp.int32(0)
    accumulate_key_piece = lax.all_gather(keys_own, "blk", axis=0, tiled=True)
    accumulate_value_piece = lax.all_gather(values_own, "blk", axis=0, tiled=True)
    piece_rows = accumulate_value_piece.shape[0]

    def update(state):
        row_top, row_total, summed = state
        masked, allowed_pairs = scores_of(accumulate_key_piece, accumulate_first_row)
        new_top = jnp.maximum(row_top, jnp.max(masked, axis=2))
        factor = jnp.exp(ALPHA * (row_top - new_top))
        weights = jnp.where(allowed_pairs, jnp.exp(ALPHA * (masked - new_top[:, :, None])), 0.0)
        summed = summed * factor[:, :, None] + jnp.einsum(
            "hqk,khd->hqd",
            weights,
            accumulate_value_piece.reshape(piece_rows, HEADS, -1),
            preferred_element_type=jnp.float32,
        )
        return (new_top, row_total * factor + jnp.sum(weights, axis=2), summed)

    def unchanged(state):
        return state

    softmax_state = lax.cond(
        block_meets(accumulate_first_row, piece_rows), update, unchanged, start_state
    )
    row_top, row_total, summed = softmax_state
    attended_heads = summed / row_total[:, :, None]
    attended = jnp.transpose(attended_heads, (1, 0, 2)).reshape(length, model_width)
    attn_low = attended.astype(jnp.bfloat16)
    branch = jnp.dot(attn_low, out_weight, preferred_element_type=jnp.float32) + out_shift.astype(
        jnp.float32
    )
    second_hat, second_inv = normalize(branch)
    middle = inputs + second_hat * gain_rows[1] + shift_rows[1]
    third_hat, third_inv = normalize(middle)
    ffn_in = (third_hat * gain_rows[2] + shift_rows[2]).astype(jnp.bfloat16)
    pre_act = jnp.dot(ffn_in, up_weight, preferred_element_type=jnp.float32) + up_shift.astype(
        jnp.float32
    )
    activated, gelu_pullback = jax.vjp(gelu_tanh, pre_act)
    act_low = activated.astype(jnp.bfloat16)
    ffn_out = jnp.dot(act_low, down_weight, preferred_element_type=jnp.float32) + down_shift.astype(
        jnp.float32
    )
    fourth_hat, fourth_inv = normalize(ffn_out)
    result = middle + fourth_hat * gain_rows[3] + shift_rows[3]
    qkv_again, out_again, up_again, down_again, gain_again = (
        lax.all_gather(w_qkv, "dp", axis=0, tiled=True),
        lax.all_gather(w_out, "dp", axis=0, tiled=True),
        lax.all_gather(w_up, "dp", axis=0, tiled=True),
        lax.all_gather(w_down, "dp", axis=0, tiled=True),
        lax.all_gather(norm_gain, "dp", axis=1, tiled=True),
    )
    back_gains = gain_again.astype(jnp.float32)
    upstream = cotangent[0].astype(jnp.float32) * valid_rows[:, None]
    grad_ffn = norm_back(fourth_hat, fourth_inv, back_gains[3], upstream).astype(jnp.bfloat16)
    grad_down = jnp.einsum("tf,td->fd", act_low, grad_ffn, preferred_element_type=jnp.float32)
    grad_act = jnp.einsum("td,fd->tf", grad_ffn, down_again, preferred_element_type=jnp.float32)
    grad_pre = gelu_pullback(grad_act)[0].astype(jnp.bfloat16)
    grad_up = jnp.einsum("td,tf->df", ffn_in, grad_pre, preferred_element_type=jnp.float32)
    grad_ffn_in = jnp.einsum("tf,df->td", grad_pre, up_again, preferred_element_type=jnp.float32)
    grad_middle = upstream + norm_back(third_hat, third_inv, back_gains[2], grad_ffn_in)
    grad_branch = norm_back(second_hat, second_inv, back_gains[1], grad_middle).astype(jnp.bfloat16)
    grad_out = jnp.einsum("td,te->de", attn_low, grad_branch, preferred_element_type=jnp.float32)
    grad_attn = jnp.einsum(
        "te,de->td", grad_branch, out_again, preferred_element_type=jnp.float32
    ).astype(jnp.bfloat16)
    grad_heads = grad_attn.reshape(length, HEADS, -1)
    row_delta = jnp.einsum(
        "qhd,hqd->hq", grad_heads, attended_heads, preferred_element_type=jnp.float32
    )
    keys_all, values_all = (
        lax.all_gather(keys_own, "blk", axis=0, tiled=True),
        lax.all_gather(values_own, "blk", axis=0, tiled=True),
    )
    grad_query = jnp.zeros((length, HEADS, head_dim), jnp.float32)
    key_terms = []
    for block_index in range(block_count):
        first_row = block_index * length
        key_piece = keys_all[first_row : first_row + length]
        value_piece = values_all[first_row : first_row + length]

        def block_grads(operands):
            key_block, value_block = operands
            value_heads = value_block.reshape(length, HEADS, -1)
            masked, allowed_pairs = scores_of(key_block, first_row)
            probabilities = (
                jnp.where(allowed_pairs, jnp.exp(ALPHA * (masked - row_top[:, :, None])), 0.0)
                / row_total[:, :, None]
            )
            grad_probs = jnp.einsum(
                "qhd,khd->hqk", grad_heads, value_heads, preferred_element_type=jnp.float32
            )
            grad_scores = ALPHA * probabilities * (grad_probs - row_delta[:, :, None])
            query_term = jnp.einsum(
                "hqk,khd->qhd",
                grad_scores,
                key_block.reshape(length, HEADS, -1),
                preferred_element_type=jnp.float32,
            )
            grad_key = jnp.einsum(
                "hqk,qhd->khd", grad_scores, query_heads, preferred_element_type=jnp.float32
            )
            grad_value = jnp.einsum(
                "hqk,qhd->khd", probabilities, grad_heads, preferred_element_type=jnp.float32
            )
            return (
                query_term,
                jnp.concatenate(
                    [
                        grad_key.reshape(length, model_width),
                        grad_value.reshape(length, model_width),
                    ],
                    1,
                ),
            )

        def block_zeros(operands):
            return (
                jnp.zeros((length, HEADS, head_dim), jnp.float32),
                jnp.zeros((length, 2 * model_width), jnp.float32),
            )

        query_term, key_term = lax.cond(
            block_meets(first_row, length), block_grads, block_zeros, (key_piece, value_piece)
        )
        grad_query = grad_query + query_term
        key_terms.append(key_term)
    key_grads = lax.psum_scatter(
        jnp.concatenate(key_terms, 0).astype(jnp.bfloat16), "blk", scatter_dimension=0, tiled=True
    ).astype(jnp.float32)
    grad_keys = key_grads[:, :model_width].astype(jnp.bfloat16)
    grad_values = key_grads[:, model_width:].astype(jnp.bfloat16)
    grad_queries = grad_query.reshape(length, model_width).astype(jnp.bfloat16) * jnp.asarray(
        query_scale, jnp.bfloat16
    )
    grad_projected = jnp.concatenate([grad_queries, grad_keys, grad_values], 1)
    grad_qkv = jnp.einsum("td,te->de", attn_in, grad_projected, preferred_element_type=jnp.float32)
    grad_qv = jnp.concatenate(
        [
            jnp.sum(grad_queries.astype(jnp.float32), axis=0),
            jnp.sum(grad_values.astype(jnp.float32), axis=0),
        ]
    )
    grad_attn_in = jnp.einsum(
        "te,de->td", grad_projected, qkv_again, preferred_element_type=jnp.float32
    )
    grad_inputs = grad_middle + norm_back(first_hat, first_inv, back_gains[0], grad_attn_in)
    grad_gains = jnp.stack(
        [
            jnp.sum(grad_attn_in * first_hat, axis=0),
            jnp.sum(grad_middle * second_hat, axis=0),
            jnp.sum(grad_ffn_in * third_hat, axis=0),
            jnp.sum(upstream * fourth_hat, axis=0),
        ]
    )
    grad_shifts = jnp.stack(
        [
            jnp.sum(grad_attn_in, axis=0),
            jnp.sum(grad_middle, axis=0),
            jnp.sum(grad_ffn_in, axis=0),
            jnp.sum(upstream, axis=0),
        ]
    )
    grad_out_shift = jnp.sum(grad_branch.astype(jnp.float32), axis=0)
    grad_up_shift = jnp.sum(grad_pre.astype(jnp.float32), axis=0)
    grad_down_shift = jnp.sum(grad_ffn.astype(jnp.float32), axis=0)
    shares = (
        lax.psum_scatter(grad_qkv, "dp", scatter_dimension=0, tiled=True),
        lax.psum_scatter(grad_qv, "dp", scatter_dimension=0, tiled=True),
        lax.psum_scatter(grad_out, "dp", scatter_dimension=0, tiled=True),
        lax.psum_scatter(grad_out_shift, "dp", scatter_dimension=0, tiled=True),
        lax.psum_scatter(grad_up, "dp", scatter_dimension=0, tiled=True),
        lax.psum_scatter(grad_up_shift, "dp", scatter_dimension=0, tiled=True),
        lax.psum_scatter(grad_down, "dp", scatter_dimension=0, tiled=True),
        lax.psum_scatter(grad_down_shift, "dp", scatter_dimension=0, tiled=True),
        lax.psum_scatter(grad_gains, "dp", scatter_dimension=1, tiled=True),
        lax.psum_scatter(grad_shifts, "dp", scatter_dimension=1, tiled=True),
    )
    totals = (
        lax.psum(shares[0].astype(jnp.bfloat16), "blk").astype(jnp.float32),
        lax.psum(shares[1].astype(jnp.bfloat16), "blk").astype(jnp.float32),
        lax.psum(shares[2].astype(jnp.bfloat16), "blk").astype(jnp.float32),
        lax.psum(shares[3].astype(jnp.bfloat16), "blk").astype(jnp.float32),
        lax.psum(shares[4].astype(jnp.bfloat16), "blk").astype(jnp.float32),
        lax.psum(shares[5].astype(jnp.bfloat16), "blk").astype(jnp.float32),
        lax.psum(shares[6].astype(jnp.bfloat16), "blk").astype(jnp.float32),
        lax.psum(shares[7].astype(jnp.bfloat16), "blk").astype(jnp.float32),
        lax.psum(shares[8].astype(jnp.bfloat16), "blk").astype(jnp.float32),
        lax.psum(shares[9].astype(jnp.bfloat16), "blk").astype(jnp.float32),
    )
    return (result.astype(jnp.bfloat16)[None], grad_inputs[None]) + tuple(totals)


NZ = 4
NPOS = 512
LEN = 256
WIDTH = 1024
OWN = 512
FF4 = 1024
BF = jnp.bfloat16
F32 = jnp.float32
MESH = pl.DeviceIdType.MESH
MIB = 1 << 20
ROW_OUT, ROW_DOWN, ROW_GAIN, ROW_SHIFT = 3, 4, 5, 9
GATHER = (
    ("v", 0, "zyx"), ("q", 0, "zxy"), ("q", 1, "zyx"), ("q", 2, "zxy"),
    ("q", 3, "zyx"), ("o", 0, "zyx"), ("u", 0, "zy"), ("u", 1, "zy"),
    ("d", 0, "zy"), ("u", 2, "yz"), ("d", 1, "zy"), ("d", 2, "zy"),
    ("u", 3, "zy"), ("d", 3, "zy"),
)
GATHER_STEPS = (
    (0, 0), (1, 0), (0, 1), (2, 0), (0, 2), (1, 1), (3, 0), (0, 3),
    (-1, 0), (-1, 1), (2, 1), (4, 0), (1, 2), (3, 1), (5, 0), (7, 0),
    (4, 1), (6, 0), (2, 2), (7, 1), (8, 0), (6, 1), (5, 1), (9, 0),
    (3, 2), (1, 3), (9, 1), (12, 0), (4, 2), (2, 3), (12, 1), (9, 2),
    (7, 2), (8, 1), (10, 0), (11, 0), (3, 3), (5, 2), (6, 2), (4, 3),
    (-1, 2), (-1, 3), (-1, 4), (5, 3), (-1, 5), (-1, 7), (-1, 6), (6, 3),
    (7, 3), (8, 2), (12, 2), (-1, 8), (10, 1), (13, 0), (11, 1), (-1, 9),
    (12, 3), (9, 3), (-1, 10), (-1, 11), (-1, 12), (13, 1), (-1, 13), (-1, 14),
    (-1, 15), (10, 2), (-1, 16), (11, 2), (-1, 17), (-1, 18), (-1, 19), (13, 2),
    (-1, 20), (-1, 21), (-1, 22), (-1, 23),
)
SCATTER = (
    ("q", 0, "xyz"), ("d", 0, "zy"), ("o", 0, "xyz"), ("d", 1, "yz"),
    ("u", 0, "yz"), ("d", 2, "zy"), ("u", 1, "yz"), ("o", 1, "xyz"),
    ("q", 1, "yxz"), ("q", 2, "yxz"), ("u", 2, "yz"), ("q", 3, "xyz"),
    ("d", 3, "yz"), ("q", 4, "xyz"), ("q", 5, "xyz"), ("u", 3, "yz"),
    ("v", 0, "xyz"),
)
SCATTER_STEPS = (
    (-1, 0), (-1, 1), (-1, 2), (-1, 25), (-1, 26), (-1, 27), (-1, 3), (-1, 4),
    (-1, 7), (-1, 8), (-1, 11), (-1, 5), (1, 0), (3, 0), (-1, 12), (-1, 6),
    (5, 0), (-1, 9), (4, 0), (-1, 10), (3, 1), (6, 0), (-1, 13), (4, 1),
    (12, 0), (-1, 14), (6, 1), (10, 0), (15, 0), (-1, 15), (2, 0), (7, 0),
    (-1, 16), (-1, 17), (-1, 18), (1, 1), (12, 1), (-1, 19), (3, 2), (-1, 20),
    (0, 0), (-1, 21), (9, 0), (11, 0), (-1, 22), (1, 2), (2, 1), (7, 1),
    (10, 1), (14, 0), (15, 1), (-1, 23), (4, 2), (5, 1), (8, 0), (-1, 24),
    (6, 2), (2, 2), (4, 3), (0, 1), (7, 2), (9, 1), (5, 2), (6, 3),
    (11, 1), (12, 2), (13, 0), (14, 1), (9, 2), (0, 2), (8, 1), (16, 0),
    (10, 2), (2, 3), (11, 2), (7, 3), (13, 1), (14, 2), (15, 2), (16, 1),
    (10, 3), (8, 2), (9, 3), (15, 3), (0, 3), (13, 2), (16, 2), (11, 3),
    (14, 3), (16, 3), (8, 3), (13, 3),
)
WIDTHS = {"v": 128, "q": 3 * OWN, "o": OWN, "u": FF4, "d": WIDTH}


def dot_nn(a, b):
    return lax.dot_general(a, b, (((1,), (0,)), ((), ())), preferred_element_type=F32)


def dot_nt(a, b):
    return lax.dot_general(a, b, (((1,), (1,)), ((), ())), preferred_element_type=F32)


def dot_tn(a, b):
    return lax.dot_general(a, b, (((0,), (0,)), ((), ())), preferred_element_type=F32)


def loop(count, body):
    lax.fori_loop(0, count, lambda index, carry: (body(index), carry)[1], 0)


def mul(index, size):
    return pl.multiple_of(index * size, size)


class Net:
    def __init__(self, sems):
        self.chip = lax.axis_index("dp")
        self.core = lax.axis_index("blk")
        self.z = self.chip // 4
        self.y = (self.chip // 2) % 2
        self.x = self.chip % 2
        self.sems = sems
        self.used = 0
        self.unsent = []

    def sem(self):
        self.used += 1
        return self.sems.at[self.used - 1]

    def chip_at(self, z, y, x):
        return z * 4 + y * 2 + x

    def peers(self, dim):
        if dim == "x":
            return [(1, self.z, self.y, 1 - self.x, self.core)]
        if dim == "y":
            return [(1, self.z, 1 - self.y, self.x, self.core)]
        if dim == "c":
            return [(1, self.z, self.y, self.x, 1 - self.core)]
        return [(k, (self.z + k) % NZ, self.y, self.x, self.core) for k in range(1, NZ)]

    def send(self, src, dst, recv, peer):
        _, z, y, x, core = peer
        copy = pltpu.make_async_remote_copy(
            src_ref=src,
            dst_ref=dst,
            send_sem=self.sem(),
            recv_sem=recv,
            device_id=(self.chip_at(z, y, x), core),
            device_id_type=MESH,
        )
        copy.start()
        self.unsent.append(copy)
        return copy

    @staticmethod
    def drain(sends, waited):
        for copy in sends:
            if not any(copy is other for other in waited):
                copy.wait_send()

    def sibling(self, src, dst):
        return self.send(src, dst, self.sem(), self.peers("c")[0])

    def greet(self):
        barrier = pltpu.get_barrier_semaphore()
        count = 0
        for dim in "xyzc":
            for _, z, y, x, core in self.peers(dim):
                pl.semaphore_signal(
                    barrier, inc=1, device_id=(self.chip_at(z, y, x), core), device_id_type=MESH
                )
                count += 1
        return lambda: pl.semaphore_wait(barrier, count)


def await_bytes(view, sem):
    pltpu.make_async_copy(view, view, sem).wait()


def view_of(net, ref, lanes, **given):
    where = {"z": net.z, "y": net.y, "x": net.x}
    where.update(given)
    return ref.at[where["z"], where["y"], where["x"], :, lanes]


ALL = slice(None)


def gather_stages(net, ref, lanes, order):
    first, second, third = order
    others = {"z": pl.ds(0, NZ - 1), "y": 1 - net.y, "x": 1 - net.x}
    got_first, got_second, got_near, got_far = net.sem(), net.sem(), net.sem(), net.sem()

    def pass_on(dim, sem, **held):
        blocks = view_of(net, ref, lanes, **held)
        for peer in net.peers(dim):
            net.send(blocks, blocks, sem, peer)

    def start():
        pass_on(first, got_first)

    def after_first():
        await_bytes(view_of(net, ref, lanes, **{first: others[first]}), got_first)
        pass_on(second, got_second, **{first: ALL})
        pass_on(third, got_near, **{first: ALL})

    def after_second():
        held = {first: ALL, second: others[second]}
        await_bytes(view_of(net, ref, lanes, **held), got_second)
        if second == "z":
            for peer in net.peers("z"):
                pass_on(third, got_far, **{first: ALL, "z": peer[1]})
        else:
            pass_on(third, got_far, **held)

    def finish():
        held = {first: ALL, third: others[third]}
        await_bytes(view_of(net, ref, lanes, **held), got_near)
        held[second] = others[second]
        await_bytes(view_of(net, ref, lanes, **held), got_far)

    return start, after_first, after_second, finish


def scatter_stages(net, ref, lanes, order, bufs, done):
    first, second, third = order
    wide, half, line = bufs
    got_wide, got_half, got_line = net.sem(), net.sem(), net.sem()
    dtype = wide.dtype
    rows, cols = wide.shape[-2:]
    step = min(rows, max(16, 32768 // cols))
    size = {"z": NZ, "y": 2, "x": 2}
    place = {"z": 0, "y": 1, "x": 2}
    mine = {"z": net.z, "y": net.y, "x": net.x}

    def coordinate(dim, peer):
        return peer[1 + place[dim]]

    def block_add(target, sources):
        for part in range(rows // step):
            here = pl.ds(part * step, step)
            total = ref[(*target, here, lanes)].astype(F32)
            for buf, at in sources:
                total = total + buf[(*at, here)].astype(F32)
            ref[(*target, here, lanes)] = total.astype(dtype)

    def target_of(**given):
        where = dict(mine)
        where.update(given)
        return (where["z"], where["y"], where["x"])

    def start():
        for peer in net.peers(first):
            there = {"z": ALL, "y": ALL, "x": ALL, first: coordinate(first, peer)}
            net.send(view_of(net, ref, lanes, **there), wide.at[peer[0] - 1], got_wide, peer)

    def after_first():
        await_bytes(wide, got_wide)
        left = [dim for dim in "zyx" if dim != first]

        def add(second_at, third_at):
            at = {second: second_at, third: third_at}
            place_in = (0, at[left[0]], at[left[1]])
            block_add(target_of(**at), [(wide, place_in)])

        for peer in net.peers(second):
            gone = coordinate(second, peer)
            loop(size[third], lambda other: add(gone, other))
            blocks = view_of(net, ref, lanes, **{second: gone, third: ALL})
            net.send(blocks, half.at[peer[0] - 1], got_half, peer)
        loop(size[third], lambda other: add(mine[second], other))

    def after_second():
        await_bytes(half, got_half)
        for peer in net.peers(third):
            gone = coordinate(third, peer)
            block_add(
                target_of(**{third: gone}), [(half, (k, gone)) for k in range(size[second] - 1)]
            )
            blocks = view_of(net, ref, lanes, **{third: gone})
            net.send(blocks, line.at[peer[0] - 1], got_line, peer)

    def finish():
        await_bytes(line, got_line)
        for part in range(rows // step):
            here = pl.ds(part * step, step)
            total = ref[(*target_of(), here, lanes)].astype(F32)
            for k in range(size[second] - 1):
                total = total + half[k, mine[third], here].astype(F32)
            for k in range(size[third] - 1):
                total = total + line[k, here].astype(F32)
            done(part * step, step, total)

    return start, after_first, after_second, finish


def plane_gather_stages(net, ref, lanes, order):
    first, second = order
    others = {"z": pl.ds(0, NZ - 1), "y": 1 - net.y}
    got_first, got_second = net.sem(), net.sem()

    def place(**given):
        where = {"z": net.z, "y": net.y}
        where.update(given)
        return ref.at[where["z"], where["y"], :, lanes]

    def pass_on(dim, sem, **held):
        for peer in net.peers(dim):
            net.send(place(**held), place(**held), sem, peer)

    def start():
        pass_on(first, got_first)

    def after_first():
        await_bytes(place(**{first: others[first]}), got_first)
        pass_on(second, got_second, **{first: ALL})

    def finish():
        await_bytes(place(**{first: ALL, second: others[second]}), got_second)

    return [start, after_first, finish]


def plane_scatter_stages(net, ref, lanes, order, bufs, emit):
    first, second = order
    wide, line = bufs[:2]
    got_wide, got_line = net.sem(), net.sem()
    rows, cols = wide.shape[-2:]
    step = min(rows, max(16, 32768 // cols))
    size = {"z": NZ, "y": 2}
    place = {"z": 1, "y": 2}
    mine = {"z": net.z, "y": net.y}

    def at(**given):
        where = dict(mine)
        where.update(given)
        return (where["z"], where["y"])

    def start():
        for peer in net.peers(first):
            there = at(**{first: peer[place[first]], second: ALL})
            net.send(ref.at[(*there, ALL, lanes)], wide.at[peer[0] - 1], got_wide, peer)

    def total(where, slot, here):
        value = ref[(*where, here, lanes)].astype(F32)
        for k in range(size[first] - 1):
            value = value + wide[k, slot, here].astype(F32)
        return value

    def after_first():
        await_bytes(wide, got_wide)
        for peer in net.peers(second):
            gone = peer[place[second]]
            there = at(**{second: gone})

            def add(part):
                here = pl.ds(mul(part, step), step)
                ref[(*there, here, lanes)] = total(there, gone, here).astype(BF)

            loop(rows // step, add)
            net.send(ref.at[(*there, ALL, lanes)], line.at[peer[0] - 1], got_line, peer)

    def final(here):
        value = total(at(), mine[second], here)
        for k in range(size[second] - 1):
            value = value + line[k, here].astype(F32)
        return value

    def finish():
        await_bytes(line, got_line)
        emit(final)

    return [start, after_first, finish]


def pieces_of(plan, widths):
    counts = {}
    for group, _, _ in plan:
        counts[group] = counts.get(group, 0) + 1
    return [
        (group, index * (widths[group] // counts[group]), widths[group] // counts[group], order)
        for group, index, order in plan
    ]


def layer_kernel(
    tok_in,
    doc,
    cot_in,
    wq_in,
    wo_in,
    wu_in,
    wd_in,
    qv_in,
    up_in,
    out_in,
    down_in,
    gain_in,
    shift_in,
    res_out,
    gtok_out,
    gq_out,
    go_out,
    gu_out,
    gd_out,
    gvec_out,
    wq,
    wo,
    wu,
    wux,
    wd,
    vbuf,
    tok,
    cot,
    pack,
    vecs,
    vq,
    vu,
    xin,
    qb,
    kb,
    vb,
    pb,
    bias,
    att,
    attb,
    attx,
    hat1,
    hat2,
    inv1,
    inv2,
    mid,
    fin,
    act,
    dge,
    rcv,
    own,
    snd,
    own_x,
    snd_s,
    rcv_s,
    snd_x,
    rcv_x,
    gff,
    gbr,
    dob,
    dsb,
    gqo,
    gu,
    gd,
    swap,
    acc,
    acc_qv,
    acc_up,
    gvecs,
    gv,
    vother,
    piece_bufs,
    res,
    gtok,
    st_q,
    st_o,
    st_u,
    st_ux,
    r_ux,
    st_d,
    sems,
    local_sems,
):
    net = Net(sems)
    core = net.core
    greeted = net.greet()

    locals_ = []

    def fetch(src, dst):
        copy = pltpu.make_async_copy(src, dst, local_sems.at[len(locals_)])
        copy.start()
        locals_.append(copy)

    def lanes_of(start, size):
        return pl.ds(pl.multiple_of(start, 128), size)

    for part in range(3):
        fetch(
            wq_in.at[:, lanes_of(part * WIDTH + core * OWN, OWN)],
            wq.at[net.z, net.y, net.x, :, pl.ds(part * OWN, OWN)],
        )
    fetch(wo_in.at[:, lanes_of(core * OWN, OWN)], wo.at[core, net.z, net.y, net.x])
    for zy in range(8):
        fetch(
            wu_in.at[:, lanes_of((zy * 2 + 1 - net.x) * 256 + core * 128, 128)],
            wux.at[:, pl.ds(zy * 128, 128)],
        )
    own_half = pl.ds(mul(net.x, 64), 64)
    for zy in range(8):
        fetch(
            wu_in.at[:, lanes_of((zy * 2 + net.x) * 256 + core * 128, 128)],
            wu.at[net.z, net.y, own_half, pl.ds(zy * 128, 128)],
        )
    fetch(wd_in.at[pl.ds(mul(core, 128), 128), :], wd.at[net.z, net.y])
    fetch(tok_in, tok)
    fetch(cot_in, cot)
    pack[...] = jnp.zeros_like(pack)
    pack[0:1, :] = qv_in[...].astype(F32)
    pack[1:3, :] = up_in[...].astype(F32)
    for row, ref in (
        (ROW_OUT, out_in),
        (ROW_DOWN, down_in),
        (ROW_GAIN, gain_in),
        (ROW_SHIFT, shift_in),
    ):
        value = ref[...].astype(F32)
        rows = slice(row, row + value.shape[0])
        pack[rows, 0:64] = jnp.where(net.x == 0, value, 0.0)
        pack[rows, 64:128] = jnp.where(net.x == 1, value, 0.0)
    vbuf[net.z, net.y, net.x] = pack[...].astype(BF)
    wo_own = wo.at[core]
    plan = pieces_of(GATHER, WIDTHS)
    sources = {"v": vbuf, "q": wq, "o": wo_own}

    def stages_of(group, lanes, order):
        if group == "d":
            return plane_gather_stages(net, wd, lanes, order)
        if group == "u":
            passing = plane_gather_stages(net, wu, lanes, order)
            got_x = net.sem()

            def cross():
                net.send(
                    wux.at[:, lanes],
                    wu.at[net.z, net.y, own_half, lanes],
                    got_x,
                    net.peers("x")[0],
                )

            def crossed():
                await_bytes(wux.at[:, lanes], got_x)
                passing[0]()

            return [cross, crossed, *passing[1:]]
        return gather_stages(net, sources[group], lanes, order)

    gathers = [
        stages_of(group, pl.ds(lane0, count), order) for group, lane0, count, order in plan
    ]
    greeted()
    ready = {("q", 0): 3, ("o", 0): 4, ("u", 0): 12, ("u", 1): 20, ("d", 0): 21}
    state = {"landed": 0}
    got_wo = []

    def gather(piece, stage):
        while state["landed"] < ready.get((plan[piece][0], stage), 0):
            locals_[state["landed"]].wait()
            state["landed"] += 1
        gathers[piece][stage]()
        group, lane0, count, _ = plan[piece]
        if group == "o" and stage == 3:
            half = wo_own.at[:, :, :, :, pl.ds(lane0, count)]
            got_wo.append(net.sibling(half, half))

    def spread_vectors():
        for z in range(NZ):
            for y in range(2):
                both = vbuf[z, y, 0].astype(F32) + vbuf[z, y, 1].astype(F32)
                vecs[:, pl.ds((z * 2 + y) * 128, 128)] = both
        for y in range(2):
            for x in range(2):
                at = pl.ds((y * 2 + x) * 128, 128)
                vq[0:8, at] = vbuf[core, y, x].astype(F32)[0:8]
                vq[8:16, at] = vbuf[core + 2, y, x].astype(F32)[0:8]
        for z in range(NZ):
            for y in range(2):
                block = vbuf[z, y, net.x].astype(F32)
                vu[0:1, pl.ds((z * 2 + y) * 128, 128)] = jnp.where(
                    core == 0, block[1:2], block[2:3]
                )
        acc[...] = jnp.zeros_like(acc)
        acc_up[...] = jnp.zeros_like(acc_up)

    def gain(n):
        return vecs[ROW_GAIN + n : ROW_GAIN + n + 1, :]

    def shift(n):
        return vecs[ROW_SHIFT + n : ROW_SHIFT + n + 1, :]

    def accumulate(row, value):
        parts = value.reshape(value.shape[0] // 8, 8, value.shape[1])
        acc[row] += jnp.sum(parts, axis=0)

    got = {}

    chunk = 32
    chunks = LEN // chunk

    def ln0(i):
        here = pl.ds(mul(i, chunk), chunk)
        hat, _ = normalize(tok[here, :].astype(F32))
        xin[core, here, :] = (hat * gain(0) + shift(0)).astype(BF)

    def attention_input():
        locals_[21].wait()
        loop(chunks, ln0)
        got["x"] = net.sibling(xin.at[core], xin.at[core])

    ends = []
    end = jnp.int32(0)
    for j in range(8):
        end = end + doc[0, j]
        ends.append(end)

    def segment(position):
        total = jnp.zeros(position.shape, jnp.int32)
        for value in ends:
            total = total + (position >= value).astype(jnp.int32)
        return total

    scale = 1.0 / (ALPHA * 8.0)

    def project(t):
        n = t // 2
        m = t % 2
        tile = pl.ds(mul(n, 256), 256)
        rows = pl.ds(mul(m, 256), 256)

        def part(index, dst, bias, factor):
            weight = wq[:, :, :, :, pl.ds(pl.multiple_of(index * OWN + n * 256, 256), 256)]
            value = dot_nn(xin[m], weight.reshape(WIDTH, 256))
            if bias is not None:
                value = value + vq[bias : bias + 1, tile]
            if factor is not None:
                value = value * factor
            dst[rows, tile] = value.astype(BF)

        part(0, qb, 0, scale)
        part(1, kb, None, None)
        part(2, vb, 8, None)

    def projections():
        got["x"].wait_recv()
        loop(4, project)

    lane = lax.broadcasted_iota(jnp.int32, (1, 128), 1)
    block = 128

    def masks():
        for r in range(NPOS // block):
            count = (r + 1) * block
            q_pos = r * block + lax.broadcasted_iota(jnp.int32, (block, 1), 0)
            k_pos = lax.broadcasted_iota(jnp.int32, (1, count), 1)
            allowed = (segment(q_pos) == segment(k_pos)) & (k_pos <= q_pos)
            bias[r * block : (r + 1) * block, 0:count] = jnp.where(allowed, 0.0, FILLER)

    def attend(half, pair):
        at = pl.ds(mul(pair, 128), 128)
        for r in (half, half + 2):
            rows = pl.ds(r * block, block)
            count = (r + 1) * block
            q = qb[rows, at]
            k = kb[0:count, at]
            v = vb[0:count, at]
            outs = []
            for head in range(2):
                mine = (lane < 64) if head == 0 else (lane >= 64)
                scores = dot_nt(jnp.where(mine, q, jnp.zeros_like(q)), k) + bias[rows, 0:count]
                top = jnp.max(scores, axis=1, keepdims=True)
                weights = jnp.exp2((scores - top) * (ALPHA * math.log2(math.e)))
                summed = dot_nn(weights.astype(BF), jnp.where(mine, v, jnp.ones_like(v)))
                turned = pltpu.roll(summed, 64, 1)
                inverse = 1.0 / jnp.where(mine, turned, summed)
                wide = jnp.concatenate([inverse] * (r + 1), axis=1)
                pb[pair * 2 + head, rows, 0:count] = (weights * wide).astype(BF)
                outs.append(summed * inverse)
            out = jnp.where(lane < 64, outs[0], outs[1])
            att[rows, at] = out
            attb[rows, at] = out.astype(BF)

    other_rows = pl.ds(mul(1 - core, LEN), LEN)
    own_rows = pl.ds(mul(core, LEN), LEN)
    got_att = []

    def half_rows(of_core, half):
        return pl.ds(pl.multiple_of(of_core * LEN + half * block, block), block)

    def attend_some(half, pair0):
        loop(2, lambda i: attend(half, i + pair0))
        if pair0 == 2:
            sent = attb.at[half_rows(1 - core, half), :]
            got_att.append(net.sibling(sent, attx.at[pl.ds(half * block, block), :]))

    own_group = net.x * 2 + core
    across_group = (1 - net.x) * 2 + core

    def branch_tile(half, n):
        lanes = pl.ds(mul(n % 2, 256), 256)
        mine = wo[n // 2, pl.ds(2 * core, 2), :, :, :, lanes].reshape(OWN, 256)
        theirs = wo[n // 2, pl.ds(2 * (1 - core), 2), :, :, :, lanes].reshape(OWN, 256)
        at = pl.ds(mul(n, 256), 256)
        here = pl.ds(half * block, block)
        value = dot_nn(attb[half_rows(core, half), :], mine)
        own[here, at] = value + dot_nn(attx[here, :], theirs)

    def ln12(i):
        here = pl.ds(mul(i, chunk), chunk)
        first, first_inv = normalize(own[here, :] + vecs[ROW_OUT : ROW_OUT + 1, :])
        hat1[here, :] = first
        inv1[here, :] = jnp.broadcast_to(first_inv, (chunk, 128))
        middle = tok[here, :].astype(F32) + first * gain(1) + shift(1)
        mid[here, :] = middle
        second, second_inv = normalize(middle)
        hat2[here, :] = second
        inv2[here, :] = jnp.broadcast_to(second_inv, (chunk, 128))
        fin[own_group, here, :] = (second * gain(2) + shift(2)).astype(BF)

    class Share:
        def __init__(self, ref):
            self.ref = ref
            self.beside, self.across, self.passed = [], [], []

        def send(self, half):
            rows = pl.ds(half * 128, 128)
            view = self.ref.at[own_group, rows]
            self.across.append(net.send(view, view, net.sem(), net.peers("x")[0]))
            self.beside.append(net.sibling(view, view))

        def pass_on(self, half):
            self.across[half].wait_recv()
            view = self.ref.at[across_group, pl.ds(half * 128, 128)]
            self.passed.append(net.sibling(view, view))

        def wait_beside(self):
            for copy in self.beside:
                copy.wait_recv()

        def wait_passed(self):
            for copy in self.passed:
                copy.wait_recv()
            self.passed = []

    class Reduce:
        def __init__(self, product):
            self.product = product
            self.beside, self.across = [], []

        def group_rows(self, group):
            return pl.ds(mul(group, LEN), LEN)

        def multiply_here(self, n):
            at = pl.ds(n * 256, 256)
            value = self.product(self.group_rows(net.x * 2 + 1 - core), n)
            snd_s[net.x, :, at] = value.astype(BF)
            own[:, at] = self.product(self.group_rows(own_group), n)

        def multiply_there(self, n):
            at = pl.ds(n * 256, 256)
            value = self.product(self.group_rows((1 - net.x) * 2 + 1 - core), n)
            snd_s[1 - net.x, :, at] = value.astype(BF)
            self.beside.append(net.sibling(snd_s.at[:, :, at], rcv_s.at[:, :, at]))
            own_x[:, at] = self.product(self.group_rows(across_group), n)

        def multiply(self, n):
            at = pl.ds(n * 256, 256)
            for xg in range(2):
                value = self.product(self.group_rows(xg * 2 + 1 - core), n)
                snd_s[xg, :, at] = value.astype(BF)
            self.beside.append(net.sibling(snd_s.at[:, :, at], rcv_s.at[:, :, at]))
            own_x[:, at] = self.product(self.group_rows(across_group), n)
            own[:, at] = self.product(self.group_rows(own_group), n)

        def cross(self, n):
            at = pl.ds(n * 256, 256)
            self.beside[n].wait_recv()

            def add(i):
                here = pl.ds(mul(i, 64), 64)
                over = own_x[here, at] + rcv_s[1 - net.x, here, at].astype(F32)
                snd_x[here, at] = over.astype(BF)

            def keep(i):
                here = pl.ds(mul(i, 64), 64)
                own[here, at] += rcv_s[net.x, here, at].astype(F32)

            loop(4, add)
            self.across.append(
                net.send(snd_x.at[:, at], rcv_x.at[:, at], net.sem(), net.peers("x")[0])
            )
            loop(4, keep)

        def wait(self):
            for copy in self.across:
                copy.wait_recv()

        def free(self):
            for copy in self.beside + self.across:
                copy.wait_send()

    share_fin, share_gff = Share(fin), Share(gff)
    row_copies = []

    def copy_out(src, dst):
        row_copies.append(pltpu.make_async_copy(src, dst, local_sems.at[23 + len(row_copies)]))
        row_copies[-1].start()

    def branch_half(half):
        got_att[half].wait_recv()
        if half == 0:
            loop(2, lambda i: branch_tile(half, core * 2 + i))
            for part in got_wo:
                part.wait_recv()
            loop(2, lambda i: branch_tile(half, (1 - core) * 2 + i))
        else:
            loop(4, functools.partial(branch_tile, half))
        loop(chunks // 2, lambda i: ln12(i + half * (chunks // 2)))
        share_fin.send(half)

    root = math.sqrt(2.0 / math.pi)

    def up_tile(n, group):
        at = pl.ds(mul(n, 256), 256)
        rows = pl.ds(mul(group, LEN), LEN)
        u = dot_nn(fin[group], wu[:, :, :, at].reshape(WIDTH, 256)) + vu[0:1, at]
        square = u * u
        inner = jnp.tanh(root * (u + 0.044715 * (square * u)))
        half = 0.5 * (1.0 + inner)
        act[rows, at] = (u * half).astype(BF)
        slope = 0.5 * u * (1.0 - inner * inner) * (root * (1.0 + (3 * 0.044715) * square))
        dge[rows, at] = (half + slope).astype(BF)

    def up_group(group):
        loop(4, lambda n: up_tile(n, group))

    def up_beside():
        share_fin.wait_beside()
        up_group(net.x * 2 + 1 - core)

    def up_last():
        share_fin.wait_passed()
        up_group((1 - net.x) * 2 + 1 - core)

    def down_product(rows, n):
        return dot_nn(act[rows, :], wd[:, :, :, pl.ds(n * 256, 256)].reshape(FF4, 256))

    down = Reduce(down_product)

    def tiles_of(width, count, body):
        return [functools.partial(body, lane0, count) for lane0 in range(0, width, count)]

    def attention_input_and_masks():
        attention_input()
        masks()

    steps = [
        spread_vectors,
        attention_input_and_masks,
        projections,
        lambda: attend_some(0, 0),
        lambda: attend_some(0, 2),
        lambda: attend_some(1, 0),
        lambda: attend_some(1, 2),
        lambda: branch_half(0),
        lambda: branch_half(1),
        lambda: share_fin.pass_on(0),
        lambda: share_fin.pass_on(1),
    ]
    steps += [
        lambda: up_group(own_group),
        up_beside,
        lambda: up_group(across_group),
        up_last,
        functools.partial(down.multiply, 0),
        functools.partial(down.multiply, 1),
        functools.partial(down.cross, 0),
        functools.partial(down.multiply, 2),
        functools.partial(down.cross, 1),
        functools.partial(down.multiply, 3),
        functools.partial(down.cross, 2),
        functools.partial(down.cross, 3),
    ]
    filled = ends[-1]

    def upstream_of(i):
        here = pl.ds(mul(i, chunk), chunk)
        position = core * LEN + i * chunk + lax.broadcasted_iota(jnp.int32, (chunk, 1), 0)
        return cot[here, :].astype(F32) * (position < filled).astype(F32)

    def top_tile(i):
        here = pl.ds(mul(i, chunk), chunk)
        value = own[here, :] + rcv_x[here, :].astype(F32) + vecs[ROW_DOWN : ROW_DOWN + 1, :]
        hat, inv = normalize(value)
        res[here, :] = (mid[here, :] + hat * gain(3) + shift(3)).astype(BF)
        upstream = upstream_of(i)
        grad = norm_back(hat, inv, gain(3), upstream).astype(BF)
        gff[own_group, here, :] = grad
        accumulate(ROW_GAIN + 3, upstream * hat)
        accumulate(ROW_SHIFT + 3, upstream)
        accumulate(ROW_DOWN, grad.astype(F32))

    def top():
        locals_[22].wait()
        down.wait()
        for half in range(2):
            loop(chunks // 2, lambda i: top_tile(i + half * (chunks // 2)))
            share_gff.send(half)
        copy_out(res, res_out)

    steps.append(top)
    for piece, stage in GATHER_STEPS:
        if piece < 0:
            steps[stage]()
        else:
            gather(piece, stage)


    out_copies = []

    def deliver(src, dst):
        copy = pltpu.make_async_copy(src, dst, local_sems.at[25 + len(out_copies)])
        copy.start()
        out_copies.append((copy, net.sibling(src, dst)))

    def ship(group, lane0, count):
        if group == "d":
            at = pl.ds(lane0, count)
            deliver(st_d.at[:, at], gd_out.at[pl.ds(mul(core, 128), 128), at])
        if group == "u":
            for part in range(2):
                for zy in range(lane0 // 128, (lane0 + count) // 128):
                    deliver(
                        st_u.at[part, :, pl.ds(zy * 128, 128)],
                        gu_out.at[:, lanes_of((zy * 2 + part) * 256 + core * 128, 128)],
                    )
        if group == "o":
            deliver(
                st_o.at[:, pl.ds(lane0, count)], go_out.at[:, lanes_of(core * OWN + lane0, count)]
            )
        if group == "q":
            start = (lane0 // OWN) * WIDTH + lane0 % OWN
            deliver(
                st_q.at[:, pl.ds(lane0, count)], gq_out.at[:, lanes_of(core * OWN + start, count)]
            )

    plan = pieces_of(SCATTER, WIDTHS)
    sums = {"o": gqo, "q": gqo, "v": gv}
    stage_of = {"o": st_o, "q": st_q, "v": gvec_out}

    def store_to(stage, lane0, count):
        def done(row0, size, total):
            stage[row0 : row0 + size, lane0 : lane0 + count] = total

        return done

    def sums_of(group, lane0, count, order, bufs):
        lanes = pl.ds(lane0, count)
        if group == "d":

            def keep(total):
                for part in range(4):
                    here = pl.ds(part * 32, 32)
                    st_d[here, lanes] = total(here)

            return plane_scatter_stages(net, gd, lanes, order, bufs, keep)
        if group == "u":
            got_x = net.sem()

            def cross(total):
                for part in range(2):
                    here = pl.ds(part * 32, 32)
                    theirs = pl.multiple_of((1 - net.x) * 64 + part * 32, 32)
                    st_ux[here, lanes] = total(pl.ds(theirs, 32)).astype(BF)
                net.send(st_ux.at[:, lanes], r_ux.at[:, lanes], got_x, net.peers("x")[0])
                for part in range(2):
                    here = pl.ds(part * 32, 32)
                    mine = pl.multiple_of(net.x * 64 + part * 32, 32)
                    st_u[net.x, here, lanes] = total(pl.ds(mine, 32))

            def crossed():
                await_bytes(r_ux.at[:, lanes], got_x)
                st_u[1 - net.x, :, lanes] = r_ux[:, lanes].astype(F32)

            return [*plane_scatter_stages(net, gu, lanes, order, bufs, cross), crossed]
        base = 3 * OWN if group == "o" else 0
        return scatter_stages(
            net,
            sums[group],
            pl.ds(base + lane0, count),
            order,
            bufs,
            store_to(stage_of[group], lane0, count),
        )

    scatters = [
        sums_of(*piece, bufs) for piece, bufs in zip(plan, piece_bufs, strict=True)
    ]

    def scatter(piece, stage):
        scatters[piece][stage]()
        if stage == len(scatters[piece]) - 1:
            ship(*plan[piece][:3])

    def over_rows(chip_x, left, right, out, at, count, add):
        groups = pl.ds(chip_x * 2, 2)

        def tile(z):
            a, b = left(groups, pl.ds(mul(z, 256), 256)), right(groups, at)
            value = dot_tn(a.reshape(NPOS, 256), b.reshape(NPOS, count)).reshape(2, 128, count)
            if add:
                value = value + out[z, :, :, at].astype(F32)
            out[z, :, :, at] = value.astype(BF)

        loop(NZ, tile)

    def rows_of(ref):
        return lambda groups, at: ref[pl.ds(mul(groups.start, LEN), NPOS), at]

    def groups_of(ref):
        return lambda groups, at: ref[groups, :, at]

    def gdown_piece(chip_x, add, lane0, count):
        at = pl.ds(lane0, count)
        if add:
            share_gff.wait_passed()
        over_rows(chip_x, rows_of(act), groups_of(gff), gd, at, count, add)

    def gpre_tile(group, z):
        at = pl.ds(mul(z, 256), 256)
        rows = pl.ds(mul(group, LEN), LEN)
        weight = wd[z].reshape(256, WIDTH)
        value = dot_nt(gff[group], weight) * dge[rows, at].astype(F32)
        value = value.astype(BF)
        dge[rows, at] = value
        acc_up[:, at] += jnp.sum(value.astype(F32).reshape(32, 8, 256), axis=0)

    def gpre_group(group):
        loop(NZ, functools.partial(gpre_tile, group))

    def gpre_beside():
        share_gff.wait_beside()
        gpre_group(net.x * 2 + 1 - core)

    def gpre_last():
        share_gff.wait_passed()
        gpre_group((1 - net.x) * 2 + 1 - core)

    def gup_piece(chip_x, add, lane0, count):
        at = pl.ds(lane0, count)
        over_rows(chip_x, groups_of(fin), rows_of(dge), gu, at, count, add)

    def grad_ffn_in_product(rows, n):
        return dot_nt(dge[rows, :], wu[n].reshape(256, FF4))

    gfi = Reduce(grad_ffn_in_product)

    def grad_ffn_in_here():
        down.free()
        for n in range(4):
            gfi.multiply_here(n)

    def grad_ffn_in_there():
        for n in range(4):
            gfi.multiply_there(n)

    def grad_ffn_in_cross():
        for n in range(4):
            gfi.cross(n)

    def middle_tile(i):
        here = pl.ds(mul(i, chunk), chunk)
        grad_in = own[here, :] + rcv_x[here, :].astype(F32)
        second = hat2[here, :]
        accumulate(ROW_GAIN + 2, grad_in * second)
        accumulate(ROW_SHIFT + 2, grad_in)
        grad_mid = upstream_of(i) + norm_back(second, inv2[here, 0:1], gain(2), grad_in)
        mid[here, :] = grad_mid
        first = hat1[here, :]
        accumulate(ROW_GAIN + 1, grad_mid * first)
        accumulate(ROW_SHIFT + 1, grad_mid)
        grad = norm_back(first, inv1[here, 0:1], gain(1), grad_mid).astype(BF)
        gbr[core, here, :] = grad
        accumulate(ROW_OUT, grad.astype(F32))

    def grad_middle():
        gfi.wait()
        loop(chunks, middle_tile)
        got["gbr"] = net.sibling(gbr.at[core], gbr.at[core])

    go = gqo.at[:, :, :, :, pl.ds(3 * OWN, OWN)]

    def gout_tile(k, cols, put):
        left = attb[:, pl.ds(mul(k, 256), 256)]
        grad = gbr[:, :, cols].reshape(NPOS, OWN)
        put(k, dot_tn(left, grad).astype(BF).reshape(2, 2, 64, OWN))

    def put_swap(k, value):
        swap[k] = value

    def put_own(k, value):
        gqo[2 * core + k, :, :, :, pl.ds(3 * OWN, OWN)] = value


    def gatt_tile(t):
        k = t // 2
        m = t % 2
        left = wo[0, 2 * core + k].reshape(256, OWN)
        right = wo[1, 2 * core + k].reshape(256, OWN)
        value = dot_nt(gbr[m, :, 0:OWN], left) + dot_nt(gbr[m, :, OWN:WIDTH], right)
        dob[pl.ds(mul(m, 256), 256), pl.ds(mul(k, 256), 256)] = value.astype(BF)

    def grad_out():
        got["gbr"].wait_recv()
        loop(2, lambda k: gout_tile(k, lanes_of((1 - core) * OWN, OWN), put_swap))
        got["swap"] = net.sibling(swap, go.at[pl.ds(2 * core, 2)])
        loop(2, lambda k: gout_tile(k, lanes_of(core * OWN, OWN), put_own))
        loop(4, gatt_tile)

    def attend_back(pair):
        at = pl.ds(mul(pair, 128), 128)
        sums = []
        for head in range(2):
            mine = (lane < 64) if head == 0 else (lane >= 64)
            queries_ = []
            for r in range(NPOS // block):
                rows = pl.ds(r * block, block)
                count = (r + 1) * block
                grad = dob[rows, at]
                grad = jnp.where(mine, grad, jnp.zeros_like(grad))
                delta = jnp.sum(grad.astype(F32) * att[rows, at], axis=1, keepdims=True)
                probs = pb[pair * 2 + head, rows, 0:count].astype(F32)
                grad_probs = dot_nt(grad, vb[0:count, at])
                scores = (probs * (grad_probs - delta)).astype(BF)
                dsb[rows, 0:count] = scores
                queries_.append(dot_nn(scores, kb[0:count, at]))
            keys_, values_ = [], []
            for r in range(NPOS // block):
                rows = pl.ds(r * block, NPOS - r * block)
                cols = pl.ds(r * block, block)
                keys_.append(dot_tn(dsb[rows, cols], qb[rows, at]))
                values_.append(dot_tn(pb[pair * 2 + head, rows, cols], dob[rows, at]))
            sums.append((queries_, keys_, values_))
        total_q = jnp.zeros((8, 128), F32)
        total_v = jnp.zeros((8, 128), F32)
        for r in range(NPOS // block):
            rows = pl.ds(r * block, block)
            merged = [
                (jnp.where(lane < 64, sums[0][i][r], sums[1][i][r]) * power).astype(BF)
                for i, power in enumerate((float(ALPHA), float(ALPHA), 1.0))
            ]
            grad_q = merged[0] * jnp.asarray(scale, BF)
            qb[rows, at] = grad_q
            kb[rows, at] = merged[1]
            vb[rows, at] = merged[2]
            total_q += jnp.sum(grad_q.astype(F32).reshape(block // 8, 8, 128), axis=0)
            total_v += jnp.sum(merged[2].astype(F32).reshape(block // 8, 8, 128), axis=0)
        acc_qv[0, :, at] = total_q
        acc_qv[1, :, at] = total_v

    def gqkv_piece(lane0, count):
        ref = (qb, kb, vb)[lane0 // OWN]

        def tile(z):
            left = xin[:, :, pl.ds(mul(z, 256), 256)].reshape(NPOS, 256)
            value = dot_tn(left, ref[:, lane0 % OWN : lane0 % OWN + count]).astype(BF)
            gqo[z, :, :, :, pl.ds(lane0, count)] = value.reshape(2, 2, 64, count)

        loop(NZ, tile)

    def gai_tile(rows, dst):
        def body(z):
            value = None
            for part, ref in enumerate((qb, kb, vb)):
                weight = wq[z, :, :, :, pl.ds(part * OWN, OWN)].reshape(256, OWN)
                term = dot_nt(ref[rows, :], weight)
                value = term if value is None else value + term
            dst[:, pl.ds(mul(z, 256), 256)] = value

        loop(NZ, body)

    def grad_attn_in():
        gai_tile(other_rows, snd)
        got["gai"] = net.sibling(snd, rcv)
        gai_tile(own_rows, own)

    def bottom_tile(i):
        here = pl.ds(mul(i, chunk), chunk)
        hat, inv = normalize(tok[here, :].astype(F32))
        grad_in = own[here, :] + rcv[here, :]
        accumulate(ROW_GAIN, grad_in * hat)
        accumulate(ROW_SHIFT, grad_in)
        gtok[here, :] = mid[here, :] + norm_back(hat, inv, gain(0), grad_in)

    def bottom():
        got["gai"].wait_recv()
        loop(chunks, bottom_tile)
        copy_out(gtok, gtok_out)
        for row in range(16):
            gvecs[row : row + 1, :] = jnp.sum(acc[row], axis=0, keepdims=True)
        row_id = lax.broadcasted_iota(jnp.int32, (16, 1), 0)
        for z in range(NZ):
            for y in range(2):
                base = gvecs[:, pl.ds((z * 2 + y) * 128, 128)]
                for x in range(2):
                    at = pl.ds((y * 2 + x) * 128, 128)
                    kind = 0 if z < 2 else 1
                    qv_row = jnp.sum(acc_qv[kind, :, at], axis=0, keepdims=True)
                    qv_row = jnp.where(core == z % 2, qv_row, 0.0)
                    up_at = pl.ds((z * 2 + y) * 128, 128)
                    up_row = jnp.sum(acc_up[:, up_at], axis=0, keepdims=True)
                    up_row = jnp.where(net.x == x, up_row, 0.0)
                    value = base + jnp.where(row_id == 0, qv_row, 0.0)
                    gv[z, y, x] = value + jnp.where(row_id == 1 + core, up_row, 0.0)

    steps = [
        lambda: None,
        lambda: gpre_group(own_group),
        gpre_beside,
        lambda: share_gff.pass_on(0),
        lambda: share_gff.pass_on(1),
        *tiles_of(WIDTH, 512, functools.partial(gdown_piece, 1 - net.x, True)),
        lambda: gpre_group(across_group),
        gpre_last,
        *tiles_of(FF4, 512, functools.partial(gup_piece, 1 - net.x, True)),
        grad_ffn_in_there,
        grad_ffn_in_cross,
        grad_middle,
        grad_out,
        lambda: got["swap"].wait_recv(),
    ]
    steps += [functools.partial(loop, 1, lambda i, pair=p: attend_back(i + pair)) for p in range(4)]
    steps += tiles_of(3 * OWN, 512, gqkv_piece)
    steps += [grad_attn_in, bottom]

    def both(piece, width):
        for step in tiles_of(width, 512, functools.partial(piece, net.x, False)):
            step()

    steps += [
        lambda: both(gdown_piece, WIDTH),
        lambda: both(gup_piece, FF4),
        grad_ffn_in_here,
    ]
    for piece, stage in SCATTER_STEPS:
        if piece < 0:
            steps[stage]()
        else:
            scatter(piece, stage)
    got_vec = net.sibling(gvec_out, vother)
    got_vec.wait_send()
    got_vec.wait_recv()
    gvec_out[...] = gvec_out[...] + vother[...]
    for copy in row_copies:
        copy.wait()
    for copy, remote in out_copies:
        copy.wait()
        remote.wait_recv()
    net.drain(net.unsent, (*down.beside, *down.across, got_vec))


def scatter_bufs(group, count, order):
    rows, dtype = {"v": (16, F32)}.get(group, (64, BF))
    size = {"z": NZ, "y": 2, "x": 2}
    if group in "du":
        first, second = order
        return [
            pltpu.VMEM((size[first] - 1, size[second], 128, count), BF),
            pltpu.VMEM((size[second] - 1, 128, count), BF),
        ]
    first, second, third = order
    left = [size[dim] for dim in "zyx" if dim != first]
    return [
        pltpu.VMEM((size[first] - 1, *left, rows, count), dtype),
        pltpu.VMEM((size[second] - 1, size[third], rows, count), dtype),
        pltpu.VMEM((size[third] - 1, rows, count), dtype),
    ]


def hand_out_kernel(*refs):
    large, vec = refs[:6], refs[6]
    outs, small = refs[7:13], refs[13:19]
    for src, dst in zip(large, outs, strict=True):
        dst[...] = src[...]
    right = lax.axis_index("dp") % 2 == 1
    values = vec[...]
    half = jnp.where(right, values[:, 64:], values[:, :64])
    small[0][...] = values[0:1]
    small[1][...] = half[ROW_OUT : ROW_OUT + 1]
    small[2][...] = values[1:3]
    small[3][...] = half[ROW_DOWN : ROW_DOWN + 1]
    small[4][...] = half[ROW_GAIN : ROW_GAIN + 4]
    small[5][...] = half[ROW_SHIFT : ROW_SHIFT + 4]

def fused(
    tokens,
    doc_lengths,
    cotangent,
    w_qkv,
    qv_bias,
    w_out,
    out_bias,
    w_up,
    up_bias,
    w_down,
    down_bias,
    norm_gain,
    norm_bias,
):
    vmem = pl.BlockSpec(memory_space=pltpu.VMEM)
    anywhere = pl.BlockSpec(memory_space=pl.ANY)
    scratch = [
        pltpu.VMEM((NZ, 2, 2, 64, 3 * OWN), BF),
        pltpu.VMEM((2, NZ, 2, 2, 64, OWN), BF),
        pltpu.VMEM((NZ, 2, 128, FF4), BF),
        pltpu.VMEM((64, FF4), BF),
        pltpu.VMEM((NZ, 2, 128, WIDTH), BF),
        pltpu.VMEM((NZ, 2, 2, 16, 128), BF),
        pltpu.VMEM((LEN, WIDTH), BF),
        pltpu.VMEM((LEN, WIDTH), BF),
        pltpu.VMEM((16, 128), F32),
        pltpu.VMEM((16, WIDTH), F32),
        pltpu.VMEM((16, OWN), F32),
        pltpu.VMEM((8, FF4), F32),
        pltpu.VMEM((2, LEN, WIDTH), BF),
        pltpu.VMEM((NPOS, OWN), BF),
        pltpu.VMEM((NPOS, OWN), BF),
        pltpu.VMEM((NPOS, OWN), BF),
        pltpu.VMEM((8, NPOS, NPOS), BF),
        pltpu.VMEM((NPOS, NPOS), F32),
        pltpu.VMEM((NPOS, OWN), F32),
        pltpu.VMEM((NPOS, OWN), BF),
        pltpu.VMEM((LEN, OWN), BF),
        pltpu.VMEM((LEN, WIDTH), F32),
        pltpu.VMEM((LEN, WIDTH), F32),
        pltpu.VMEM((LEN, 128), F32),
        pltpu.VMEM((LEN, 128), F32),
        pltpu.VMEM((LEN, WIDTH), F32),
        pltpu.VMEM((4, LEN, WIDTH), BF),
        pltpu.VMEM((4 * LEN, FF4), BF),
        pltpu.VMEM((4 * LEN, FF4), BF),
        pltpu.VMEM((LEN, WIDTH), F32),
        pltpu.VMEM((LEN, WIDTH), F32),
        pltpu.VMEM((LEN, WIDTH), F32),
        pltpu.VMEM((LEN, WIDTH), F32),
        pltpu.VMEM((2, LEN, WIDTH), BF),
        pltpu.VMEM((2, LEN, WIDTH), BF),
        pltpu.VMEM((LEN, WIDTH), BF),
        pltpu.VMEM((LEN, WIDTH), BF),
        pltpu.VMEM((4, LEN, WIDTH), BF),
        pltpu.VMEM((2, LEN, WIDTH), BF),
        pltpu.VMEM((NPOS, OWN), BF),
        pltpu.VMEM((NPOS, NPOS), BF),
        pltpu.VMEM((NZ, 2, 2, 64, 4 * OWN), BF),
        pltpu.VMEM((NZ, 2, 128, FF4), BF),
        pltpu.VMEM((NZ, 2, 128, WIDTH), BF),
        pltpu.VMEM((2, 2, 2, 64, OWN), BF),
        pltpu.VMEM((16, 8, WIDTH), F32),
        pltpu.VMEM((2, 8, OWN), F32),
        pltpu.VMEM((8, FF4), F32),
        pltpu.VMEM((16, WIDTH), F32),
        pltpu.VMEM((NZ, 2, 2, 16, 128), F32),
        pltpu.VMEM((16, 128), F32),
        [
            scatter_bufs(group, count, order)
            for group, _, count, order in pieces_of(SCATTER, WIDTHS)
        ],
        pltpu.VMEM((LEN, WIDTH), BF),
        pltpu.VMEM((LEN, WIDTH), F32),
        pltpu.VMEM((64, 3 * OWN), F32),
        pltpu.VMEM((64, OWN), F32),
        pltpu.VMEM((2, 64, FF4), F32),
        pltpu.VMEM((64, FF4), BF),
        pltpu.VMEM((64, FF4), BF),
        pltpu.VMEM((128, WIDTH), F32),
        pltpu.SemaphoreType.DMA((800,)),
        pltpu.SemaphoreType.DMA((90,)),
    ]
    outs = pl.pallas_call(
        layer_kernel,
        out_shape=[
            jax.ShapeDtypeStruct((LEN, WIDTH), BF),
            jax.ShapeDtypeStruct((LEN, WIDTH), F32),
            jax.ShapeDtypeStruct((64, 3 * WIDTH), F32),
            jax.ShapeDtypeStruct((64, WIDTH), F32),
            jax.ShapeDtypeStruct((64, 4 * FF4), F32),
            jax.ShapeDtypeStruct((256, WIDTH), F32),
            jax.ShapeDtypeStruct((16, 128), F32),
        ],
        in_specs=[anywhere, pl.BlockSpec(memory_space=pltpu.SMEM), anywhere]
        + [anywhere] * 4
        + [vmem] * 6,
        out_specs=[anywhere] * 6 + [vmem],
        scratch_shapes=scratch,
        compiler_params=pltpu.CompilerParams(
            collective_id=0, has_side_effects=True, vmem_limit_bytes=63 * MIB
        ),
        name="layer",
    )(
        tokens[0],
        doc_lengths,
        cotangent[0],
        w_qkv,
        w_out,
        w_up,
        w_down,
        qv_bias.reshape(1, 128),
        up_bias.reshape(2, 128),
        out_bias.reshape(1, 64),
        down_bias.reshape(1, 64),
        norm_gain,
        norm_bias,
    )
    *large, vec = outs
    done = pl.pallas_call(
        hand_out_kernel,
        out_shape=[jax.ShapeDtypeStruct(array.shape, array.dtype) for array in large]
        + [
            jax.ShapeDtypeStruct((1, 128), F32),
            jax.ShapeDtypeStruct((1, 64), F32),
            jax.ShapeDtypeStruct((2, 128), F32),
            jax.ShapeDtypeStruct((1, 64), F32),
            jax.ShapeDtypeStruct((4, 64), F32),
            jax.ShapeDtypeStruct((4, 64), F32),
        ],
        in_specs=[vmem] * 7,
        out_specs=[vmem] * 12,
        compiler_params=pltpu.CompilerParams(vmem_limit_bytes=63 * MIB),
        name="hand_out",
    )(*large, vec)
    result, grad_inputs, grad_qkv, grad_out, grad_up, grad_down = done[:6]
    grad_qv, grad_out_shift, grad_up_shift, grad_down_shift, grad_gain, grad_shift = done[6:]
    return (
        result[None],
        grad_inputs[None],
        grad_qkv,
        grad_qv.reshape(128),
        grad_out,
        grad_out_shift.reshape(64),
        grad_up,
        grad_up_shift.reshape(256),
        grad_down,
        grad_down_shift.reshape(64),
        grad_gain,
        grad_shift,
    )


def solution(mesh):
    placed = (
        P("dp", "blk", None),
        P("dp", None),
        P("dp", "blk", None),
        P("dp", None),
        P("dp"),
        P("dp", None),
        P("dp"),
        P("dp", None),
        P("dp"),
        P("dp", None),
        P("dp"),
        P(None, "dp"),
        P(None, "dp"),
    )
    sizes = (mesh.shape["dp"], mesh.shape["blk"])
    return jax.shard_map(
        fused if sizes == (NZ * 4, 2) else shards,
        mesh=mesh,
        in_specs=placed,
        out_specs=(
            P("dp", "blk", None),
            P("dp", "blk", None),
            P("dp", None),
            P("dp"),
            P("dp", None),
            P("dp"),
            P("dp", None),
            P("dp"),
            P("dp", None),
            P("dp"),
            P(None, "dp"),
            P(None, "dp"),
        ),
        check_vma=False,
    )
```
